32 devices in a mesh: grp: 2 (over x), blade: 8 (over z, y), dof: 2 (over core).
Axes of the slice: x: 2, y: 2, z: 4, core: 2. Of those that a mesh axis runs over, the one named last changes fastest.
Arguments:
- panel: bfloat16 [8192, 512], P(('grp', 'blade', 'dof')), parts along dimension 0, may hold values from -0.25 to 0.25
- stiffness: bfloat16 [96, 64, 128, 128], P(('grp', 'blade'), 'dof'), parts along dimension 0, may hold values from -0.5 to 0.5
- block_rows: int32 [96, 64], P(('grp', 'blade'), 'dof'), parts along dimension 0, may hold values from 0 to 31
- block_cols: int32 [96, 64], P(('grp', 'blade'), 'dof'), parts along dimension 0, may hold values from 0 to 31
Outputs:
- spectral: float32 [2, 96, 512, 512], P(None, ('grp', 'blade'), 'dof'), parts along dimension 1
The draws below stay inside these ranges and needn't reach their ends.
There are 2 independent parts, one for each index of `grp`. The reference program is written for one: setup_inputs(seed, part) draws one part's arguments, and reference() takes and returns one part's arrays. A program takes and returns all parts, laid end to end along the dimension named above; each array names one. Nothing has to cross between parts.
Inputs may be any that keep to these rules, and one draw needn't show every extreme that they name: `block_rows`: row block index of each stiffness block; indices of one blade may repeat. `block_cols`: column block index of each stiffness block; indices of one blade may repeat.
All inputs are finite; a program needn't handle non-finite values.
Results may differ from the reference program's by a relative error of at most 0.0029.
Values may be sent and summed in bfloat16 or wider, within the bound.
A program may use at most 128 MiB of HBM per device.

```python
import math
import jax
import jax.numpy as jnp
from jax import lax

M = 512
BS = 128
NDOF = 4096
BLADES = 48
NBLK = 64


def place_ends(array, rng, low, high):
    index_at = [jax.random.randint(jax.random.fold_in(rng, axis), (), 0, length) for axis, length in enumerate(array.shape)]
    longest = array.shape.index(max(array.shape))
    neighbour = index_at[:longest] + [(index_at[longest] + 1) % array.shape[longest]] + index_at[longest + 1:]
    return array.at[tuple(index_at)].set(low).at[tuple(neighbour)].set(high)


def level_of(stream_key, shape, pieces, low, largest):
    loudness, own = 1.0, jax.random.fold_in(stream_key, 6)
    for position, shards_of in pieces:
        draws = jnp.exp(jax.random.uniform(jax.random.fold_in(own, position), (shards_of,), jnp.float32, low / len(pieces), largest / len(pieces)))
        loudness = loudness * jnp.repeat(draws, shape[position] // shards_of).reshape([-1 if axis == position else 1 for axis in range(len(shape))])
    return loudness


def scatter_about(own_key, extent, spread, reach, shards=(), held_as=jnp.bfloat16):
    factor_of = level_of(own_key, extent, shards, -0.22, 0.18) if shards else 1.0
    values = jax.random.normal(own_key, extent, jnp.float32) * spread * factor_of
    return jnp.minimum(jnp.maximum(values, -reach), reach).astype(held_as)


def setup_inputs(seed: int = 0, part: int = 0) -> dict:
    key_list = jax.random.split(jax.random.key(seed), 5)
    own_keys = jax.random.split(jax.random.fold_in(key_list[4], part), 5)
    panel = scatter_about(own_keys[0], (NDOF, M), ((NBLK * BS * BLADES) ** -0.25), 0.25, ((0, 16),))
    stiffness = scatter_about(own_keys[1], (BLADES, NBLK, BS, BS), BS ** -0.5, 0.5, ((0, 8), (1, 2)))
    block_rows = place_ends(jax.random.randint(own_keys[2], (BLADES, NBLK), 0, NDOF // BS), jax.random.fold_in(own_keys[2], 1), 0, (NDOF // BS) - 1).astype(jnp.int32)
    block_cols = place_ends(jax.random.randint(own_keys[3], (BLADES, NBLK), 0, NDOF // BS), jax.random.fold_in(own_keys[3], 1), 0, (NDOF // BS) - 1).astype(jnp.int32)
    return dict(panel=panel, stiffness=stiffness, block_rows=block_rows, block_cols=block_cols)


def reference(panel, stiffness, block_rows, block_cols):
    blocks = panel.astype(jnp.float32).reshape(NDOF // BS, BS, M)

    def one_blade(items):
        mats, rows, cols = items
        chosen = blocks[cols]
        image = jnp.einsum("nij,njm->nim", mats.astype(jnp.float32), chosen, precision=lax.Precision.HIGHEST)
        image = image.astype(jnp.bfloat16).astype(jnp.float32)
        left = blocks[rows].reshape(-1, M)
        return jnp.dot(left.T, image.reshape(-1, M), precision=lax.Precision.HIGHEST)

    projected = lax.map(one_blade, (stiffness, block_rows, block_cols))
    index = jnp.arange(BLADES, dtype=jnp.int32)
    angle = ((index[:, None] * index[None, :]) % BLADES).astype(jnp.float32) * (2.0 * math.pi / BLADES)
    real_part = jnp.einsum("hb,brc->hrc", jnp.cos(angle), projected, precision=lax.Precision.HIGHEST)
    imag_part = -jnp.einsum("hb,brc->hrc", jnp.sin(angle), projected, precision=lax.Precision.HIGHEST)
    return jnp.stack([real_part, imag_part])
```

```python
import math

import jax
import jax.numpy as jnp
from jax import lax
from jax.sharding import PartitionSpec as P


def body(panel, stiffness, block_rows, block_cols):
    block_size = stiffness.shape[-1]
    modes = panel.shape[-1]
    whole = lax.all_gather(panel, ("blade", "dof"), axis=0, tiled=True)
    blocks = whole.reshape(-1, block_size, modes)

    def one_blade(items):
        mats, rows, cols = items
        chosen = jnp.take(blocks, cols, axis=0)
        image = jnp.einsum("nij,njm->nim", mats, chosen, preferred_element_type=jnp.float32)
        image = image.astype(jnp.bfloat16)
        left = jnp.take(blocks, rows, axis=0).reshape(-1, modes)
        return lax.dot_general(
            left,
            image.reshape(-1, modes),
            (((0,), (0,)), ((), ())),
            preferred_element_type=jnp.float32,
        )

    partial_proj = lax.map(one_blade, (stiffness, block_rows, block_cols))
    half = lax.psum_scatter(partial_proj, "dof", scatter_dimension=1, tiled=True)
    half = half.astype(jnp.bfloat16)
    blade_count = stiffness.shape[0] * lax.axis_size("blade")
    index = jnp.arange(blade_count, dtype=jnp.int32)
    angle = (index[:, None] * index[None, :] % blade_count).astype(jnp.float32) * (
        2.0 * math.pi / blade_count
    )
    table = jnp.stack([jnp.cos(angle), -jnp.sin(angle)])
    stacked = lax.all_to_all(half, "blade", split_axis=1, concat_axis=0, tiled=True)
    joined = jnp.einsum(
        "phb,brc->phrc", table, stacked.astype(jnp.float32), precision=lax.Precision.HIGHEST
    ).astype(jnp.bfloat16)
    full_spec = lax.all_to_all(joined, "blade", split_axis=1, concat_axis=2, tiled=True)
    return full_spec.astype(jnp.float32)


def solution(mesh):
    placed = (
        P(("grp", "blade", "dof"), None),
        P(("grp", "blade"), "dof", None, None),
        P(("grp", "blade"), "dof"),
        P(("grp", "blade"), "dof"),
    )
    return jax.shard_map(
        body,
        mesh=mesh,
        in_specs=placed,
        out_specs=P(None, ("grp", "blade"), "dof", None),
        check_vma=False,
    )
```

```python
import math

import jax
import jax.numpy as jnp
import numpy as np
from jax import lax
from jax.experimental import pallas as pl
from jax.experimental.pallas import tpu as pltpu
from jax.sharding import PartitionSpec as P

MESH = pl.DeviceIdType.MESH
LAYERS = 4
PAIR = 2
BLOCK_GROUP = 8
CHUNK = 32
SUB = 16


def dft_tables(per_chip):
    per_layer = PAIR * per_chip
    count = LAYERS * per_layer
    index = np.arange(count)
    angle = (index[:, None] * index[None, :] % count) * (2.0 * math.pi / count)
    full = np.stack([np.cos(angle), -np.sin(angle)])

    def rows_for(layer):
        part = full[:, layer * per_layer : (layer + 1) * per_layer]
        part = part.reshape(2, PAIR, per_chip, count).transpose(1, 0, 2, 3)
        return part.reshape(2 * per_layer, count)

    def split(weights):
        wide = np.kron(weights, np.eye(SUB)).astype(np.float32)
        high = wide.astype(jnp.bfloat16)
        low = (wide - high.astype(np.float32)).astype(jnp.bfloat16)
        return np.stack([high, low])

    middle, ends = [], []
    for layer, near in ((1, 0), (2, 3)):
        partial = rows_for(near).copy()
        partial[:, near * per_layer : (near + 1) * per_layer] = 0.0
        middle.append(split(np.concatenate([rows_for(layer), partial])))
        own = rows_for(near)[:, near * per_layer : (near + 1) * per_layer]
        ends.append(split(own))
    return np.stack(middle), np.stack(ends)


def kernel(
    panel_ref, stiff_hbm, rows_ref, cols_ref, wmid_hbm, wend_hbm, out_hbm,
    pan, pan_t, stiff, acc, core_in, raw, y_out, wmid, wend,
    comb_out, comb_in, harm_out, harm_in, out_v,
    load_sem, up_send, up_recv, dn_send, dn_recv, ys_send, ys_recv, co_send, co_recv,
    sum_send, sum_recv, sw_send, sw_recv, z_send, z_recv, h_send, h_recv, out_sem,
):
    blade = lax.axis_index("blade")
    d = lax.axis_index("dof")
    z = blade // PAIR
    y = blade % PAIR
    other_y = z * PAIR + (1 - y)
    per_chip, n_blocks = stiff.shape[0], stiff.shape[1]
    per_layer = per_chip * PAIR
    rows_half = core_in.shape[1]
    n_chunks = raw.shape[0]
    half_cols = raw.shape[3]
    per_shard = panel_ref.shape[0]

    def to(src, dst, send, recv, **device):
        return pltpu.make_async_remote_copy(
            src_ref=src, dst_ref=dst, send_sem=send, recv_sem=recv,
            device_id=device, device_id_type=MESH,
        )

    core = dict(dof=1 - d)
    across = dict(blade=other_y)
    up = dict(blade=jnp.minimum(blade + PAIR, LAYERS * PAIR - 1))
    down = dict(blade=jnp.maximum(blade - PAIR, 0))
    has_up = z < LAYERS - 1
    has_dn = z > 0
    is_mid = jnp.logical_and(has_up, has_dn)
    is_end = jnp.logical_not(is_mid)
    which = z // 2

    load = pltpu.make_async_copy(stiff_hbm, stiff, load_sem.at[0])
    load.start()
    load_mid = pltpu.make_async_copy(wmid_hbm.at[which], wmid, load_sem.at[1])
    load_mid.start()
    load_end = pltpu.make_async_copy(wend_hbm.at[which], wend, load_sem.at[2])
    load_end.start()

    barrier = pltpu.get_barrier_semaphore()
    pl.semaphore_signal(barrier, inc=1, device_id=core, device_id_type=MESH)
    pl.semaphore_signal(barrier, inc=1, device_id=across, device_id_type=MESH)

    @pl.when(has_up)
    def _():
        pl.semaphore_signal(barrier, inc=1, device_id=up, device_id_type=MESH)

    @pl.when(has_dn)
    def _():
        pl.semaphore_signal(barrier, inc=1, device_id=down, device_id_type=MESH)

    pl.semaphore_wait(barrier, 2 + has_up.astype(jnp.int32) + has_dn.astype(jnp.int32))

    def shard(zz, yy, dd):
        start = ((zz * PAIR + yy) * 2 + dd) * per_shard
        return pan.at[pl.ds(start, per_shard)]

    def flip(zz, yy, dd):
        start = ((zz * PAIR + yy) * 2 + dd) * per_shard
        for i in range(per_shard):
            pan_t[start + i] = pan[start + i].T

    def up_copy(step):
        s = shard(jnp.maximum(z - step, 0), y, d)
        return to(s, s, up_send.at[step], up_recv.at[step], **up)

    def dn_copy(step):
        s = shard(jnp.minimum(z + step, LAYERS - 1), y, d)
        return to(s, s, dn_send.at[step], dn_recv.at[step], **down)

    def up_arrival(step):
        s = shard(jnp.maximum(z - step, 0), y, d)
        return to(s, s, up_send.at[step - 1], up_recv.at[step - 1], **up)

    def dn_arrival(step):
        s = shard(jnp.minimum(z + step, LAYERS - 1), y, d)
        return to(s, s, dn_send.at[step - 1], dn_recv.at[step - 1], **down)

    def y_copy(zz):
        s = shard(zz, y, d)
        return to(s, s, ys_send.at[zz], ys_recv.at[zz], **across)

    def y_arrival(zz):
        s = shard(zz, 1 - y, d)
        return to(s, s, ys_send.at[zz], ys_recv.at[zz], **across)

    def core_copy(zz, yy):
        s = shard(zz, yy, d)
        return to(s, s, co_send.at[zz * PAIR + yy], co_recv.at[zz * PAIR + yy], **core)

    def core_arrival(zz, yy):
        s = shard(zz, yy, 1 - d)
        return to(s, s, co_send.at[zz * PAIR + yy], co_recv.at[zz * PAIR + yy], **core)

    mine = ((z * PAIR + y) * 2 + d) * per_shard
    pan[pl.ds(mine, per_shard)] = panel_ref[...]

    @pl.when(has_up)
    def _():
        up_copy(0).start()

    @pl.when(has_dn)
    def _():
        dn_copy(0).start()

    y_copy(z).start()
    core_copy(z, y).start()
    flip(z, y, d)

    def take_y(zz):
        y_arrival(zz).wait_recv()
        core_copy(zz, 1 - y).start()
        flip(zz, 1 - y, d)

    for step in range(1, LAYERS):

        @pl.when(z >= step)
        def _(step=step):
            up_arrival(step).wait_recv()
            if step < LAYERS - 1:

                @pl.when(has_up)
                def _():
                    up_copy(step).start()

            y_copy(z - step).start()
            core_copy(z - step, y).start()

        @pl.when(z + step < LAYERS)
        def _(step=step):
            dn_arrival(step).wait_recv()
            if step < LAYERS - 1:

                @pl.when(has_dn)
                def _():
                    dn_copy(step).start()

            y_copy(z + step).start()
            core_copy(z + step, y).start()

        @pl.when(z >= step)
        def _(step=step):
            flip(z - step, y, d)

        @pl.when(z + step < LAYERS)
        def _(step=step):
            flip(z + step, y, d)

        if step == 1:
            take_y(z)
        else:

            @pl.when(z >= step - 1)
            def _(step=step):
                take_y(z - (step - 1))

            @pl.when(z + step - 1 < LAYERS)
            def _(step=step):
                take_y(z + (step - 1))

    last = LAYERS - 1

    @pl.when(z >= last)
    def _():
        take_y(z - last)

    @pl.when(z + last < LAYERS)
    def _():
        take_y(z + last)

    def take_core(i, carry):
        core_arrival(i // PAIR, i % PAIR).wait_recv()
        flip(i // PAIR, i % PAIR, 1 - d)
        return carry

    lax.fori_loop(0, LAYERS * PAIR, take_core, 0)
    load.wait()

    def sum_copy(b):
        src = acc.at[b, pl.ds(pl.multiple_of((1 - d) * rows_half, rows_half), rows_half)]
        return to(src, core_in.at[b], sum_send.at[b], sum_recv.at[b], **core)

    def slot(yy, b):
        return z * per_layer + yy * per_chip + b

    def swap_copy(b):
        return to(y_out.at[b], raw.at[:, slot(y, b)], sw_send.at[b], sw_recv.at[b], **across)

    def swap_arrival(b):
        return to(y_out.at[b], raw.at[:, slot(1 - y, b)], sw_send.at[b], sw_recv.at[b], **across)

    own_rows = pl.ds(pl.multiple_of(d * rows_half, rows_half), rows_half)

    def summed(b, yy):
        cols = pl.ds(pl.multiple_of(yy * half_cols, half_cols), half_cols)
        total = acc[b, own_rows, cols] + core_in[b, :, cols]
        return total.astype(jnp.bfloat16).reshape(n_chunks, CHUNK, half_cols)

    def finish(b):
        sum_copy(b).wait_recv()
        y_out[b] = summed(b, 1 - y)
        swap_copy(b).start()
        raw[:, slot(y, b)] = summed(b, y)

    def one_blade(b, carry):
        acc[b] = jnp.zeros(acc.shape[1:], jnp.float32)

        def group(q, carry):
            left, image = [], []
            for i in range(BLOCK_GROUP):
                n = q * BLOCK_GROUP + i
                product = jnp.dot(
                    stiff[b, n], pan[cols_ref[b, n]], preferred_element_type=jnp.float32
                )
                image.append(product.astype(jnp.bfloat16))
                left.append(pan_t[rows_ref[b, n]])
            acc[b] += jnp.dot(
                jnp.concatenate(left, axis=1),
                jnp.concatenate(image, axis=0),
                preferred_element_type=jnp.float32,
            )
            return carry

        lax.fori_loop(0, n_blocks // BLOCK_GROUP, group, 0)
        sum_copy(b).start()

        @pl.when(b > 0)
        def _():
            finish(b - 1)

        return carry

    lax.fori_loop(0, per_chip, one_blade, 0)
    finish(per_chip - 1)
    load_mid.wait()
    load_end.wait()

    def take_swap(b, carry):
        swap_arrival(b).wait_recv()
        return carry

    lax.fori_loop(0, per_chip, take_swap, 0)

    n_harm = 2 * per_chip
    near = jnp.where(z < 2, 0, LAYERS - 1)
    far = LAYERS - 1 - z
    near_dev = dict(blade=near * PAIR + y)
    far_dev = dict(blade=far * PAIR + y)
    mid_dev = dict(blade=jnp.where(z < 2, 1, LAYERS - 2) * PAIR + y)

    def planes(p, zz):
        return raw.at[p, pl.ds(zz * per_layer, per_layer)]

    def end_copy(p):
        s = planes(p, near)
        return to(s, s, z_send.at[0, p], z_recv.at[0, p], **mid_dev)

    def own_copy(p):
        s = planes(p, z)
        return to(s, s, z_send.at[1, p], z_recv.at[1, p], **far_dev)

    def own_arrival(p):
        s = planes(p, far)
        return to(s, s, z_send.at[1, p], z_recv.at[1, p], **far_dev)

    def pass_copy(p):
        s = planes(p, near)
        return to(s, s, z_send.at[2, p], z_recv.at[2, p], **far_dev)

    def pass_arrival(p):
        s = planes(p, LAYERS - 1 - near)
        return to(s, s, z_send.at[2, p], z_recv.at[2, p], **far_dev)

    def comb_copy(p):
        return to(comb_out.at[p], comb_in.at[p], z_send.at[3, p], z_recv.at[3, p], **near_dev)

    def harm_copy(p):
        return to(harm_out.at[p], harm_in.at[p], h_send.at[p], h_recv.at[p], **across)

    def out_copy(p):
        rows = pl.ds(pl.multiple_of(p * CHUNK, CHUNK), CHUNK)
        return pltpu.make_async_copy(out_v.at[:, rows], out_hbm.at[:, rows], out_sem.at[p])

    def transform(weights, x):
        return jnp.dot(weights[0], x, preferred_element_type=jnp.float32) + jnp.dot(
            weights[1], x, preferred_element_type=jnp.float32
        )

    def store_final(p, sub, final):
        rows = pl.ds(pl.multiple_of(p * CHUNK + sub * SUB, SUB), SUB)
        cols = pl.ds(pl.multiple_of(y * half_cols, half_cols), half_cols)
        mine = jnp.where(y == 0, final[0], final[1])
        theirs = jnp.where(y == 0, final[1], final[0])
        out_v[:, rows, cols] = mine
        harm_out[p, :, pl.ds(sub * SUB, SUB)] = theirs.astype(jnp.bfloat16)

    def take_harm(p):
        harm_copy(p).wait_recv()
        rows = pl.ds(pl.multiple_of(p * CHUNK, CHUNK), CHUNK)
        cols = pl.ds(pl.multiple_of((1 - y) * half_cols, half_cols), half_cols)
        out_v[:, rows, cols] = harm_in[p].astype(jnp.float32)
        out_copy(p).start()

    @pl.when(is_mid)
    def _():
        own_copy(0).start()
        own_copy(1).start()
        end_copy(0).wait_recv()
        pass_copy(0).start()

        def step(p, carry):
            @pl.when(p + 1 < n_chunks)
            def _():
                end_copy(p + 1).wait_recv()
                pass_copy(p + 1).start()

            own_arrival(p).wait_recv()
            pass_arrival(p).wait_recv()

            @pl.when(p + 2 < n_chunks)
            def _():
                own_copy(p + 2).start()

            for sub in range(CHUNK // SUB):
                x = raw[p, :, pl.ds(sub * SUB, SUB)]
                x = x.reshape(x.shape[0] * SUB, half_cols)
                got = transform(wmid, x).reshape(4, n_harm, SUB, half_cols)
                comb_out[p, :, pl.ds(sub * SUB, SUB)] = (
                    got[2:].reshape(2 * n_harm, SUB, half_cols).astype(jnp.bfloat16)
                )
                store_final(p, sub, got[:2])
            comb_copy(p).start()
            harm_copy(p).start()

            @pl.when(p > 0)
            def _():
                take_harm(p - 1)

            return carry

        lax.fori_loop(0, n_chunks, step, 0)

    @pl.when(is_end)
    def _():
        for p in range(3):
            end_copy(p).start()

        def step(p, carry):
            @pl.when(p + 3 < n_chunks)
            def _():
                end_copy(p + 3).start()

            comb_copy(p).wait_recv()
            for sub in range(CHUNK // SUB):
                x = raw[p, pl.ds(z * per_layer, per_layer), pl.ds(sub * SUB, SUB)]
                x = x.reshape(per_layer * SUB, half_cols)
                got = transform(wend, x).reshape(2 * n_harm, SUB, half_cols)
                got = got + comb_in[p, :, pl.ds(sub * SUB, SUB)].astype(jnp.float32)
                store_final(p, sub, got.reshape(2, n_harm, SUB, half_cols))
            harm_copy(p).start()

            @pl.when(p > 0)
            def _():
                take_harm(p - 1)

            return carry

        lax.fori_loop(0, n_chunks, step, 0)

    take_harm(n_chunks - 1)

    for step in range(LAYERS - 1):

        @pl.when(jnp.logical_and(has_up, z >= step))
        def _(step=step):
            up_copy(step).wait_send()

        @pl.when(jnp.logical_and(has_dn, z + step < LAYERS))
        def _(step=step):
            dn_copy(step).wait_send()

    for zz in range(LAYERS):
        y_copy(zz).wait_send()
        for yy in range(PAIR):
            core_copy(zz, yy).wait_send()

    def drain_blade(b, carry):
        sum_copy(b).wait_send()
        swap_copy(b).wait_send()
        return carry

    lax.fori_loop(0, per_chip, drain_blade, 0)

    def drain_chunk(p, carry):
        @pl.when(is_mid)
        def _():
            own_copy(p).wait_send()
            pass_copy(p).wait_send()
            comb_copy(p).wait_send()

        @pl.when(is_end)
        def _():
            end_copy(p).wait_send()

        harm_copy(p).wait_send()
        out_copy(p).wait()
        return carry

    lax.fori_loop(0, n_chunks, drain_chunk, 0)


def line_body(panel, stiffness, block_rows, block_cols):
    per_chip, n_blocks, bs, _ = stiffness.shape
    modes = panel.shape[-1]
    shards = LAYERS * PAIR * 2
    per_shard = panel.shape[0] // bs
    n_all = shards * per_shard
    half = modes // 2
    n_chunks = half // CHUNK
    count = LAYERS * PAIR * per_chip
    n_harm = 2 * per_chip
    wmid, wend = dft_tables(per_chip)
    bf16, f32 = jnp.bfloat16, jnp.float32
    dma = pltpu.SemaphoreType.DMA
    vmem = pl.BlockSpec(memory_space=pltpu.VMEM)
    smem = pl.BlockSpec(memory_space=pltpu.SMEM)
    hbm = pl.BlockSpec(memory_space=pl.ANY)
    result = pl.pallas_call(
        kernel,
        out_shape=jax.ShapeDtypeStruct((n_harm, half, modes), f32),
        in_specs=[vmem, hbm, smem, smem, hbm, hbm],
        out_specs=hbm,
        scratch_shapes=[
            pltpu.VMEM((n_all, bs, modes), bf16),
            pltpu.VMEM((n_all, modes, bs), bf16),
            pltpu.VMEM(stiffness.shape, bf16),
            pltpu.VMEM((per_chip, modes, modes), f32),
            pltpu.VMEM((per_chip, half, modes), f32),
            pltpu.VMEM((n_chunks, count, CHUNK, half), bf16),
            pltpu.VMEM((per_chip, n_chunks, CHUNK, half), bf16),
            pltpu.VMEM(wmid.shape[1:], bf16),
            pltpu.VMEM(wend.shape[1:], bf16),
            pltpu.VMEM((n_chunks, 2 * n_harm, CHUNK, half), bf16),
            pltpu.VMEM((n_chunks, 2 * n_harm, CHUNK, half), bf16),
            pltpu.VMEM((n_chunks, n_harm, CHUNK, half), bf16),
            pltpu.VMEM((n_chunks, n_harm, CHUNK, half), bf16),
            pltpu.VMEM((n_harm, half, modes), f32),
            dma((3,)),
            dma((LAYERS - 1,)), dma((LAYERS - 1,)),
            dma((LAYERS - 1,)), dma((LAYERS - 1,)),
            dma((LAYERS,)), dma((LAYERS,)),
            dma((LAYERS * PAIR,)), dma((LAYERS * PAIR,)),
            dma((per_chip,)), dma((per_chip,)),
            dma((per_chip,)), dma((per_chip,)),
            dma((4, n_chunks)), dma((4, n_chunks)),
            dma((n_chunks,)), dma((n_chunks,)),
            dma((n_chunks,)),
        ],
        compiler_params=pltpu.CompilerParams(
            collective_id=0, has_side_effects=True, vmem_limit_bytes=60 * 1024 * 1024
        ),
    )(
        panel.reshape(per_shard, bs, modes),
        stiffness,
        block_rows,
        block_cols,
        jnp.asarray(wmid),
        jnp.asarray(wend),
    )
    return result.reshape(2, per_chip, half, modes)


def body(panel, stiffness, block_rows, block_cols):
    block_size = stiffness.shape[-1]
    modes = panel.shape[-1]
    whole = lax.all_gather(panel, ("blade", "dof"), axis=0, tiled=True)
    blocks = whole.reshape(-1, block_size, modes)

    def one_blade(items):
        mats, rows, cols = items
        chosen = jnp.take(blocks, cols, axis=0)
        image = jnp.einsum("nij,njm->nim", mats, chosen, preferred_element_type=jnp.float32)
        image = image.astype(jnp.bfloat16)
        left = jnp.take(blocks, rows, axis=0).reshape(-1, modes)
        return lax.dot_general(
            left,
            image.reshape(-1, modes),
            (((0,), (0,)), ((), ())),
            preferred_element_type=jnp.float32,
        )

    partial_proj = lax.map(one_blade, (stiffness, block_rows, block_cols))
    half = lax.psum_scatter(partial_proj, "dof", scatter_dimension=1, tiled=True)
    half = half.astype(jnp.bfloat16)
    blade_count = stiffness.shape[0] * lax.axis_size("blade")
    index = jnp.arange(blade_count, dtype=jnp.int32)
    angle = (index[:, None] * index[None, :] % blade_count).astype(jnp.float32) * (
        2.0 * math.pi / blade_count
    )
    table = jnp.stack([jnp.cos(angle), -jnp.sin(angle)])
    stacked = lax.all_to_all(half, "blade", split_axis=1, concat_axis=0, tiled=True)
    joined = jnp.einsum(
        "phb,brc->phrc", table, stacked.astype(jnp.float32), precision=lax.Precision.HIGHEST
    ).astype(jnp.bfloat16)
    full_spec = lax.all_to_all(joined, "blade", split_axis=1, concat_axis=2, tiled=True)
    return full_spec.astype(jnp.float32)


def solution(mesh):
    placed = (
        P(("grp", "blade", "dof"), None),
        P(("grp", "blade"), "dof", None, None),
        P(("grp", "blade"), "dof"),
        P(("grp", "blade"), "dof"),
    )
    chips = mesh.shape["blade"]
    return jax.shard_map(
        line_body if chips == LAYERS * PAIR else body,
        mesh=mesh,
        in_specs=placed,
        out_specs=P(None, ("grp", "blade"), "dof", None),
        check_vma=False,
    )
```

```python
import math

import jax
import jax.numpy as jnp
import numpy as np
from jax import lax
from jax.experimental import pallas as pl
from jax.experimental.pallas import tpu as pltpu
from jax.sharding import PartitionSpec as P

MESH = pl.DeviceIdType.MESH
LAYERS = 4
PAIR = 2
BLOCK_GROUP = 8
CHUNK = 32
SUB = 16
VMEM_BYTES = 60 * 1024 * 1024
PASSES = 2


def dft_tables(per_chip):
    per_layer = PAIR * per_chip
    count = LAYERS * per_layer
    index = np.arange(count)
    angle = (index[:, None] * index[None, :] % count) * (2.0 * math.pi / count)
    full = np.stack([np.cos(angle), -np.sin(angle)])

    def rows_for(layer):
        part = full[:, layer * per_layer : (layer + 1) * per_layer]
        part = part.reshape(2, PAIR, per_chip, count).transpose(1, 0, 2, 3)
        return part.reshape(2 * per_layer, count)

    def split(weights):
        wide = np.kron(weights, np.eye(SUB)).astype(np.float32)
        high = wide.astype(jnp.bfloat16)
        low = (wide - high.astype(np.float32)).astype(jnp.bfloat16)
        return np.stack([high, low])

    middle, ends = [], []
    for layer, near in ((1, 0), (2, 3)):
        partial = rows_for(near).copy()
        partial[:, near * per_layer : (near + 1) * per_layer] = 0.0
        middle.append(split(np.concatenate([rows_for(layer), partial])))
        own = rows_for(near)[:, near * per_layer : (near + 1) * per_layer]
        ends.append(split(own))
    return np.stack(middle), np.stack(ends)


def kernel(
    panel_ref, stiff_hbm, rows_ref, cols_ref, wmid_hbm, wend_hbm, out_hbm,
    pan, pan_t, stiff, acc, core_in, raw, y_out, wmid, wend,
    comb_out, comb_in, harm_out, harm_in, out_v,
    load_sem, up_send, up_recv, dn_send, dn_recv, ys_send, ys_recv, co_send, co_recv,
    sum_send, sum_recv, sw_send, sw_recv, z_send, z_recv, h_send, h_recv, out_sem,
):
    blade = lax.axis_index("blade")
    d = lax.axis_index("dof")
    z = blade // PAIR
    y = blade % PAIR
    other_y = z * PAIR + (1 - y)
    per_chip, n_blocks = stiff.shape[0], stiff.shape[1]
    per_layer = per_chip * PAIR
    rows_half = core_in.shape[2]
    n_chunks = raw.shape[0]
    per_pass = n_chunks // PASSES
    width = raw.shape[3]
    half_cols = width * PASSES
    per_shard = panel_ref.shape[0]

    def to(src, dst, send, recv, **device):
        return pltpu.make_async_remote_copy(
            src_ref=src, dst_ref=dst, send_sem=send, recv_sem=recv,
            device_id=device, device_id_type=MESH,
        )

    core = dict(dof=1 - d)
    across = dict(blade=other_y)
    up = dict(blade=jnp.minimum(blade + PAIR, LAYERS * PAIR - 1))
    down = dict(blade=jnp.maximum(blade - PAIR, 0))
    has_up = z < LAYERS - 1
    has_dn = z > 0
    is_mid = jnp.logical_and(has_up, has_dn)
    is_end = jnp.logical_not(is_mid)
    which = z // 2

    load = pltpu.make_async_copy(stiff_hbm, stiff, load_sem.at[0])
    load.start()
    load_mid = pltpu.make_async_copy(wmid_hbm.at[which], wmid, load_sem.at[1])
    load_mid.start()
    load_end = pltpu.make_async_copy(wend_hbm.at[which], wend, load_sem.at[2])
    load_end.start()

    barrier = pltpu.get_barrier_semaphore()
    pl.semaphore_signal(barrier, inc=1, device_id=core, device_id_type=MESH)
    pl.semaphore_signal(barrier, inc=1, device_id=across, device_id_type=MESH)

    @pl.when(has_up)
    def _():
        pl.semaphore_signal(barrier, inc=1, device_id=up, device_id_type=MESH)

    @pl.when(has_dn)
    def _():
        pl.semaphore_signal(barrier, inc=1, device_id=down, device_id_type=MESH)

    pl.semaphore_wait(barrier, 2 + has_up.astype(jnp.int32) + has_dn.astype(jnp.int32))

    def shard(zz, yy, dd):
        start = ((zz * PAIR + yy) * 2 + dd) * per_shard
        return pan.at[pl.ds(start, per_shard)]

    def flip(zz, yy, dd):
        start = ((zz * PAIR + yy) * 2 + dd) * per_shard
        for i in range(per_shard):
            pan_t[start + i] = pan[start + i].T

    def up_copy(step):
        s = shard(jnp.maximum(z - step, 0), y, d)
        return to(s, s, up_send.at[step], up_recv.at[step], **up)

    def dn_copy(step):
        s = shard(jnp.minimum(z + step, LAYERS - 1), y, d)
        return to(s, s, dn_send.at[step], dn_recv.at[step], **down)

    def up_arrival(step):
        s = shard(jnp.maximum(z - step, 0), y, d)
        return to(s, s, up_send.at[step - 1], up_recv.at[step - 1], **up)

    def dn_arrival(step):
        s = shard(jnp.minimum(z + step, LAYERS - 1), y, d)
        return to(s, s, dn_send.at[step - 1], dn_recv.at[step - 1], **down)

    def y_copy(zz):
        s = shard(zz, y, d)
        return to(s, s, ys_send.at[zz], ys_recv.at[zz], **across)

    def y_arrival(zz):
        s = shard(zz, 1 - y, d)
        return to(s, s, ys_send.at[zz], ys_recv.at[zz], **across)

    def core_copy(zz, yy):
        s = shard(zz, yy, d)
        return to(s, s, co_send.at[zz * PAIR + yy], co_recv.at[zz * PAIR + yy], **core)

    def core_arrival(zz, yy):
        s = shard(zz, yy, 1 - d)
        return to(s, s, co_send.at[zz * PAIR + yy], co_recv.at[zz * PAIR + yy], **core)

    mine = ((z * PAIR + y) * 2 + d) * per_shard
    pan[pl.ds(mine, per_shard)] = panel_ref[...]

    @pl.when(has_up)
    def _():
        up_copy(0).start()

    @pl.when(has_dn)
    def _():
        dn_copy(0).start()

    y_copy(z).start()
    core_copy(z, y).start()
    flip(z, y, d)

    def take_y(zz):
        y_arrival(zz).wait_recv()
        core_copy(zz, 1 - y).start()
        flip(zz, 1 - y, d)

    def take_core(zz, yy):
        core_arrival(zz, yy).wait_recv()
        flip(zz, yy, 1 - d)

    def at_distance(step, do):
        if step == 0:
            do(z)
            return

        @pl.when(z >= step)
        def _():
            do(z - step)

        @pl.when(z + step < LAYERS)
        def _():
            do(z + step)

    for step in range(1, LAYERS):

        @pl.when(z >= step)
        def _(step=step):
            up_arrival(step).wait_recv()
            if step < LAYERS - 1:

                @pl.when(has_up)
                def _():
                    up_copy(step).start()

            y_copy(z - step).start()
            core_copy(z - step, y).start()

        @pl.when(z + step < LAYERS)
        def _(step=step):
            dn_arrival(step).wait_recv()
            if step < LAYERS - 1:

                @pl.when(has_dn)
                def _():
                    dn_copy(step).start()

            y_copy(z + step).start()
            core_copy(z + step, y).start()

        at_distance(step, lambda zz: flip(zz, y, d))
        at_distance(step - 1, take_y)
        at_distance(step - 1, lambda zz: take_core(zz, y))
        if step > 1:
            at_distance(step - 2, lambda zz: take_core(zz, 1 - y))

    at_distance(LAYERS - 1, take_y)
    at_distance(LAYERS - 1, lambda zz: take_core(zz, y))
    at_distance(LAYERS - 2, lambda zz: take_core(zz, 1 - y))
    at_distance(LAYERS - 1, lambda zz: take_core(zz, 1 - y))
    load.wait()

    def sum_copy(h, b):
        src = acc.at[h, b, pl.ds(pl.multiple_of((1 - d) * rows_half, rows_half), rows_half)]
        return to(src, core_in.at[h, b], sum_send.at[h, b], sum_recv.at[h, b], **core)

    def slot(yy, b):
        return z * per_layer + yy * per_chip + b

    def swap_copy(h, b):
        dst = raw.at[pl.ds(h * per_pass, per_pass), slot(y, b)]
        return to(y_out.at[h, b], dst, sw_send.at[h, b], sw_recv.at[h, b], **across)

    def swap_arrival(h, b):
        dst = raw.at[pl.ds(h * per_pass, per_pass), slot(1 - y, b)]
        return to(y_out.at[h, b], dst, sw_send.at[h, b], sw_recv.at[h, b], **across)

    own_rows = pl.ds(pl.multiple_of(d * rows_half, rows_half), rows_half)

    def summed(h, b, yy):
        cols = pl.ds(pl.multiple_of(yy * width, width), width)
        total = acc[h, b, own_rows, cols] + core_in[h, b, :, cols]
        return total.astype(jnp.bfloat16).reshape(per_pass, CHUNK, width)

    def finish(h, b):
        sum_copy(h, b).wait_recv()
        y_out[h, b] = summed(h, b, 1 - y)
        swap_copy(h, b).start()
        raw[pl.ds(h * per_pass, per_pass), slot(y, b)] = summed(h, b, y)

    def one_blade(h, b):
        acc[h, b] = jnp.zeros(acc.shape[2:], jnp.float32)

        def group(q, carry):
            left, image = [], []
            for i in range(BLOCK_GROUP):
                n = q * BLOCK_GROUP + i
                c = cols_ref[b, n]
                right = jnp.concatenate(
                    [pan[c, :, pl.ds(yy * half_cols + h * width, width)] for yy in range(PAIR)],
                    axis=1,
                )
                product = jnp.dot(stiff[b, n], right, preferred_element_type=jnp.float32)
                image.append(product.astype(jnp.bfloat16))
                left.append(pan_t[rows_ref[b, n]])
            acc[h, b] += jnp.dot(
                jnp.concatenate(left, axis=1),
                jnp.concatenate(image, axis=0),
                preferred_element_type=jnp.float32,
            )
            return carry

        lax.fori_loop(0, n_blocks // BLOCK_GROUP, group, 0)
        sum_copy(h, b).start()

        @pl.when(b > 0)
        def _():
            finish(h, b - 1)

    def end_pass(h):
        finish(h, per_chip - 1)

        def take_swap(b, carry):
            swap_arrival(h, b).wait_recv()
            return carry

        lax.fori_loop(0, per_chip, take_swap, 0)

    def first_pass(b, carry):
        one_blade(0, b)
        return carry

    lax.fori_loop(0, per_chip, first_pass, 0)
    end_pass(0)

    n_harm = 2 * per_chip
    near = jnp.where(z < 2, 0, LAYERS - 1)
    far = LAYERS - 1 - z
    near_dev = dict(blade=near * PAIR + y)
    far_dev = dict(blade=far * PAIR + y)
    mid_dev = dict(blade=jnp.where(z < 2, 1, LAYERS - 2) * PAIR + y)

    def planes(p, zz):
        return raw.at[p, pl.ds(zz * per_layer, per_layer)]

    def end_copy(p):
        s = planes(p, near)
        return to(s, s, z_send.at[0, p], z_recv.at[0, p], **mid_dev)

    def own_copy(p):
        s = planes(p, z)
        return to(s, s, z_send.at[1, p], z_recv.at[1, p], **far_dev)

    def own_arrival(p):
        s = planes(p, far)
        return to(s, s, z_send.at[1, p], z_recv.at[1, p], **far_dev)

    def pass_copy(p):
        s = planes(p, near)
        return to(s, s, z_send.at[2, p], z_recv.at[2, p], **far_dev)

    def pass_arrival(p):
        s = planes(p, LAYERS - 1 - near)
        return to(s, s, z_send.at[2, p], z_recv.at[2, p], **far_dev)

    def comb_copy(p):
        return to(comb_out.at[p], comb_in.at[p], z_send.at[3, p], z_recv.at[3, p], **near_dev)

    def harm_copy(p):
        return to(harm_out.at[p], harm_in.at[p], h_send.at[p], h_recv.at[p], **across)

    def transform(weights, x):
        x = jnp.concatenate(
            [x[:, i : i + SUB].reshape(-1, width) for i in range(0, CHUNK, SUB)], axis=1
        )
        got = jnp.dot(weights[0], x, preferred_element_type=jnp.float32)
        got = got + jnp.dot(weights[1], x, preferred_element_type=jnp.float32)
        return [
            got[:, i * width : (i + 1) * width].reshape(-1, SUB, width)
            for i in range(CHUNK // SUB)
        ]

    def columns(p, yy):
        return pl.ds(pl.multiple_of(yy * half_cols + p // per_pass * width, width), width)

    def out_copy(r):
        rows = pl.ds(pl.multiple_of(r * CHUNK, CHUNK), CHUNK)
        return pltpu.make_async_copy(out_v.at[:, rows], out_hbm.at[:, rows], out_sem.at[r])

    def store_final(p, sub, final):
        row = lax.rem(p, per_pass) * CHUNK + sub * SUB
        first, second = final[:n_harm], final[n_harm:]
        out_v[:, pl.ds(pl.multiple_of(row, SUB), SUB), columns(p, y)] = jnp.where(
            y == 0, first, second
        )
        theirs = jnp.where(y == 0, second, first)
        harm_out[p, :, pl.ds(sub * SUB, SUB)] = theirs.astype(jnp.bfloat16)

    def take_harm(p):
        harm_copy(p).wait_recv()
        row = lax.rem(p, per_pass) * CHUNK
        out_v[:, pl.ds(pl.multiple_of(row, CHUNK), CHUNK), columns(p, 1 - y)] = harm_in[
            p
        ].astype(jnp.float32)

        @pl.when(p >= n_chunks - per_pass)
        def _():
            out_copy(p - (n_chunks - per_pass)).start()

    @pl.when(is_mid)
    def _():
        own_copy(0).start()
        own_copy(1).start()
        end_copy(0).wait_recv()
        pass_copy(0).start()

    @pl.when(is_end)
    def _():
        end_copy(0).start()
        end_copy(1).start()

    load_mid.wait()
    load_end.wait()

    def step(p, carry):
        @pl.when(p < per_chip)
        def _():
            one_blade(1, p)

        @pl.when(p == per_chip)
        def _():
            end_pass(1)

        @pl.when(is_mid)
        def _():
            @pl.when(p + 2 < n_chunks)
            def _():
                own_copy(p + 2).start()

            @pl.when(p + 1 < n_chunks)
            def _():
                end_copy(p + 1).wait_recv()
                pass_copy(p + 1).start()

            own_arrival(p).wait_recv()
            pass_arrival(p).wait_recv()
            for sub, got in enumerate(transform(wmid, raw[p])):
                comb_out[p, :, pl.ds(sub * SUB, SUB)] = got[2 * n_harm :].astype(jnp.bfloat16)
                store_final(p, sub, got[: 2 * n_harm])
            comb_copy(p).start()

        @pl.when(is_end)
        def _():
            @pl.when(p + 2 < n_chunks)
            def _():
                end_copy(p + 2).start()

            comb_copy(p).wait_recv()
            own = raw[p, pl.ds(z * per_layer, per_layer)]
            for sub, got in enumerate(transform(wend, own)):
                rows = pl.ds(sub * SUB, SUB)
                store_final(p, sub, got + comb_in[p, :, rows].astype(jnp.float32))

        harm_copy(p).start()

        @pl.when(p > 0)
        def _():
            take_harm(p - 1)

        return carry

    lax.fori_loop(0, n_chunks, step, 0)
    take_harm(n_chunks - 1)

    for step in range(LAYERS - 1):

        @pl.when(jnp.logical_and(has_up, z >= step))
        def _(step=step):
            up_copy(step).wait_send()

        @pl.when(jnp.logical_and(has_dn, z + step < LAYERS))
        def _(step=step):
            dn_copy(step).wait_send()

    for zz in range(LAYERS):
        y_copy(zz).wait_send()
        for yy in range(PAIR):
            core_copy(zz, yy).wait_send()

    def drain_blade(b, carry):
        for h in range(PASSES):
            sum_copy(h, b).wait_send()
            swap_copy(h, b).wait_send()
        return carry

    lax.fori_loop(0, per_chip, drain_blade, 0)

    def drain_chunk(p, carry):
        @pl.when(is_mid)
        def _():
            own_copy(p).wait_send()
            pass_copy(p).wait_send()
            comb_copy(p).wait_send()

        @pl.when(is_end)
        def _():
            end_copy(p).wait_send()

        harm_copy(p).wait_send()
        return carry

    lax.fori_loop(0, n_chunks, drain_chunk, 0)

    def drain_out(r, carry):
        out_copy(r).wait()
        return carry

    lax.fori_loop(0, per_pass, drain_out, 0)


def line_body(panel, stiffness, block_rows, block_cols):
    per_chip, n_blocks, bs, _ = stiffness.shape
    modes = panel.shape[-1]
    shards = LAYERS * PAIR * 2
    per_shard = panel.shape[0] // bs
    n_all = shards * per_shard
    half = modes // 2
    width = half // PASSES
    per_pass = half // CHUNK
    n_chunks = per_pass * PASSES
    count = LAYERS * PAIR * per_chip
    n_harm = 2 * per_chip
    wmid, wend = dft_tables(per_chip)
    bf16, f32 = jnp.bfloat16, jnp.float32
    dma = pltpu.SemaphoreType.DMA
    vmem = pl.BlockSpec(memory_space=pltpu.VMEM)
    smem = pl.BlockSpec(memory_space=pltpu.SMEM)
    hbm = pl.BlockSpec(memory_space=pl.ANY)
    result = pl.pallas_call(
        kernel,
        out_shape=jax.ShapeDtypeStruct((n_harm, half, modes), f32),
        in_specs=[vmem, hbm, smem, smem, hbm, hbm],
        out_specs=hbm,
        scratch_shapes=[
            pltpu.VMEM((n_all, bs, modes), bf16),
            pltpu.VMEM((n_all, modes, bs), bf16),
            pltpu.VMEM(stiffness.shape, bf16),
            pltpu.VMEM((PASSES, per_chip, modes, PAIR * width), f32),
            pltpu.VMEM((PASSES, per_chip, half, PAIR * width), f32),
            pltpu.VMEM((n_chunks, count, CHUNK, width), bf16),
            pltpu.VMEM((PASSES, per_chip, per_pass, CHUNK, width), bf16),
            pltpu.VMEM(wmid.shape[1:], bf16),
            pltpu.VMEM(wend.shape[1:], bf16),
            pltpu.VMEM((n_chunks, 2 * n_harm, CHUNK, width), bf16),
            pltpu.VMEM((n_chunks, 2 * n_harm, CHUNK, width), bf16),
            pltpu.VMEM((n_chunks, n_harm, CHUNK, width), bf16),
            pltpu.VMEM((n_chunks, n_harm, CHUNK, width), bf16),
            pltpu.VMEM((n_harm, half, modes), f32),
            dma((3,)),
            dma((LAYERS - 1,)), dma((LAYERS - 1,)),
            dma((LAYERS - 1,)), dma((LAYERS - 1,)),
            dma((LAYERS,)), dma((LAYERS,)),
            dma((LAYERS * PAIR,)), dma((LAYERS * PAIR,)),
            dma((PASSES, per_chip)), dma((PASSES, per_chip)),
            dma((PASSES, per_chip)), dma((PASSES, per_chip)),
            dma((4, n_chunks)), dma((4, n_chunks)),
            dma((n_chunks,)), dma((n_chunks,)),
            dma((per_pass,)),
        ],
        compiler_params=pltpu.CompilerParams(
            collective_id=0, has_side_effects=True, vmem_limit_bytes=VMEM_BYTES
        ),
    )(
        panel.reshape(per_shard, bs, modes),
        stiffness,
        block_rows,
        block_cols,
        jnp.asarray(wmid),
        jnp.asarray(wend),
    )
    return result.reshape(2, per_chip, half, modes)


def body(panel, stiffness, block_rows, block_cols):
    block_size = stiffness.shape[-1]
    modes = panel.shape[-1]
    whole = lax.all_gather(panel, ("blade", "dof"), axis=0, tiled=True)
    blocks = whole.reshape(-1, block_size, modes)

    def one_blade(items):
        mats, rows, cols = items
        chosen = jnp.take(blocks, cols, axis=0)
        image = jnp.einsum("nij,njm->nim", mats, chosen, preferred_element_type=jnp.float32)
        image = image.astype(jnp.bfloat16)
        left = jnp.take(blocks, rows, axis=0).reshape(-1, modes)
        return lax.dot_general(
            left,
            image.reshape(-1, modes),
            (((0,), (0,)), ((), ())),
            preferred_element_type=jnp.float32,
        )

    partial_proj = lax.map(one_blade, (stiffness, block_rows, block_cols))
    half = lax.psum_scatter(partial_proj, "dof", scatter_dimension=1, tiled=True)
    half = half.astype(jnp.bfloat16)
    blade_count = stiffness.shape[0] * lax.axis_size("blade")
    index = jnp.arange(blade_count, dtype=jnp.int32)
    angle = (index[:, None] * index[None, :] % blade_count).astype(jnp.float32) * (
        2.0 * math.pi / blade_count
    )
    table = jnp.stack([jnp.cos(angle), -jnp.sin(angle)])
    stacked = lax.all_to_all(half, "blade", split_axis=1, concat_axis=0, tiled=True)
    joined = jnp.einsum(
        "phb,brc->phrc", table, stacked.astype(jnp.float32), precision=lax.Precision.HIGHEST
    ).astype(jnp.bfloat16)
    full_spec = lax.all_to_all(joined, "blade", split_axis=1, concat_axis=2, tiled=True)
    return full_spec.astype(jnp.float32)


def solution(mesh):
    placed = (
        P(("grp", "blade", "dof"), None),
        P(("grp", "blade"), "dof", None, None),
        P(("grp", "blade"), "dof"),
        P(("grp", "blade"), "dof"),
    )
    chips = mesh.shape["blade"]
    return jax.shard_map(
        line_body if chips == LAYERS * PAIR else body,
        mesh=mesh,
        in_specs=placed,
        out_specs=P(None, ("grp", "blade"), "dof", None),
        check_vma=False,
    )
```

```python
import math

import jax
import jax.numpy as jnp
import numpy as np
from jax import lax
from jax.experimental import pallas as pl
from jax.experimental.pallas import tpu as pltpu
from jax.sharding import PartitionSpec as P

MESH = pl.DeviceIdType.MESH
LAYERS = 4
PAIR = 2
BLOCK_GROUP = 8
CHUNK = 16
SUB = 16
VMEM_BYTES = 60 * 1024 * 1024
PASSES = 1


def dft_tables(per_chip):
    per_layer = PAIR * per_chip
    count = LAYERS * per_layer
    index = np.arange(count)
    angle = (index[:, None] * index[None, :] % count) * (2.0 * math.pi / count)
    full = np.stack([np.cos(angle), -np.sin(angle)])

    def rows_for(layer):
        part = full[:, layer * per_layer : (layer + 1) * per_layer]
        part = part.reshape(2, PAIR, per_chip, count).transpose(1, 0, 2, 3)
        return part.reshape(2 * per_layer, count)

    def split(weights):
        wide = np.kron(weights, np.eye(SUB)).astype(np.float32)
        high = wide.astype(jnp.bfloat16)
        low = (wide - high.astype(np.float32)).astype(jnp.bfloat16)
        return np.stack([high, low])

    middle, ends = [], []
    for layer, near in ((1, 0), (2, 3)):
        partial = rows_for(near).copy()
        partial[:, near * per_layer : (near + 1) * per_layer] = 0.0
        middle.append(split(np.concatenate([rows_for(layer), partial])))
        own = rows_for(near)[:, near * per_layer : (near + 1) * per_layer]
        ends.append(split(own))
    return np.stack(middle), np.stack(ends)


def kernel(
    panel_ref, stiff_hbm, rows_ref, cols_ref, wmid_hbm, wend_hbm, out_hbm,
    pan, pan_t, stiff, acc, core_in, raw, y_out, wmid, wend,
    comb_out, comb_in, harm_out, harm_in, out_v,
    load_sem, up_send, up_recv, dn_send, dn_recv, ys_send, ys_recv, co_send, co_recv,
    sum_send, sum_recv, sw_send, sw_recv, z_send, z_recv, h_send, h_recv, out_sem,
):
    blade = lax.axis_index("blade")
    d = lax.axis_index("dof")
    z = blade // PAIR
    y = blade % PAIR
    other_y = z * PAIR + (1 - y)
    per_chip, n_blocks = stiff.shape[0], stiff.shape[1]
    per_layer = per_chip * PAIR
    rows_half = core_in.shape[2]
    n_chunks = raw.shape[0]
    per_pass = n_chunks // PASSES
    width = raw.shape[3]
    half_cols = width * PASSES
    per_shard = panel_ref.shape[0]

    def to(src, dst, send, recv, **device):
        return pltpu.make_async_remote_copy(
            src_ref=src, dst_ref=dst, send_sem=send, recv_sem=recv,
            device_id=device, device_id_type=MESH,
        )

    core = dict(dof=1 - d)
    across = dict(blade=other_y)
    up = dict(blade=jnp.minimum(blade + PAIR, LAYERS * PAIR - 1))
    down = dict(blade=jnp.maximum(blade - PAIR, 0))
    has_up = z < LAYERS - 1
    has_dn = z > 0
    is_mid = jnp.logical_and(has_up, has_dn)
    is_end = jnp.logical_not(is_mid)
    which = z // 2

    load = pltpu.make_async_copy(stiff_hbm, stiff, load_sem.at[0])
    load.start()
    load_mid = pltpu.make_async_copy(wmid_hbm.at[which], wmid, load_sem.at[1])
    load_mid.start()
    load_end = pltpu.make_async_copy(wend_hbm.at[which], wend, load_sem.at[2])
    load_end.start()

    barrier = pltpu.get_barrier_semaphore()
    pl.semaphore_signal(barrier, inc=1, device_id=core, device_id_type=MESH)
    pl.semaphore_signal(barrier, inc=1, device_id=across, device_id_type=MESH)

    @pl.when(has_up)
    def _():
        pl.semaphore_signal(barrier, inc=1, device_id=up, device_id_type=MESH)

    @pl.when(has_dn)
    def _():
        pl.semaphore_signal(barrier, inc=1, device_id=down, device_id_type=MESH)

    pl.semaphore_wait(barrier, 2 + has_up.astype(jnp.int32) + has_dn.astype(jnp.int32))

    def shard(zz, yy, dd):
        start = ((zz * PAIR + yy) * 2 + dd) * per_shard
        return pan.at[pl.ds(start, per_shard)]

    def flip(zz, yy, dd):
        start = ((zz * PAIR + yy) * 2 + dd) * per_shard
        for i in range(per_shard):
            pan_t[start + i] = pan[start + i].T

    def up_copy(step):
        s = shard(jnp.maximum(z - step, 0), y, d)
        return to(s, s, up_send.at[step], up_recv.at[step], **up)

    def dn_copy(step):
        s = shard(jnp.minimum(z + step, LAYERS - 1), y, d)
        return to(s, s, dn_send.at[step], dn_recv.at[step], **down)

    def up_arrival(step):
        s = shard(jnp.maximum(z - step, 0), y, d)
        return to(s, s, up_send.at[step - 1], up_recv.at[step - 1], **up)

    def dn_arrival(step):
        s = shard(jnp.minimum(z + step, LAYERS - 1), y, d)
        return to(s, s, dn_send.at[step - 1], dn_recv.at[step - 1], **down)

    def y_copy(zz):
        s = shard(zz, y, d)
        return to(s, s, ys_send.at[zz], ys_recv.at[zz], **across)

    def y_arrival(zz):
        s = shard(zz, 1 - y, d)
        return to(s, s, ys_send.at[zz], ys_recv.at[zz], **across)

    def core_copy(zz, yy):
        s = shard(zz, yy, d)
        return to(s, s, co_send.at[zz * PAIR + yy], co_recv.at[zz * PAIR + yy], **core)

    def core_arrival(zz, yy):
        s = shard(zz, yy, 1 - d)
        return to(s, s, co_send.at[zz * PAIR + yy], co_recv.at[zz * PAIR + yy], **core)

    mine = ((z * PAIR + y) * 2 + d) * per_shard
    pan[pl.ds(mine, per_shard)] = panel_ref[...]

    @pl.when(has_up)
    def _():
        up_copy(0).start()

    @pl.when(has_dn)
    def _():
        dn_copy(0).start()

    y_copy(z).start()
    core_copy(z, y).start()
    flip(z, y, d)

    def take_y(zz):
        y_arrival(zz).wait_recv()
        core_copy(zz, 1 - y).start()
        flip(zz, 1 - y, d)

    def take_core(zz, yy):
        core_arrival(zz, yy).wait_recv()
        flip(zz, yy, 1 - d)

    def at_distance(step, do):
        if step == 0:
            do(z)
            return

        @pl.when(z >= step)
        def _():
            do(z - step)

        @pl.when(z + step < LAYERS)
        def _():
            do(z + step)

    for step in range(1, LAYERS):

        @pl.when(z >= step)
        def _(step=step):
            up_arrival(step).wait_recv()
            if step < LAYERS - 1:

                @pl.when(has_up)
                def _():
                    up_copy(step).start()

            y_copy(z - step).start()
            core_copy(z - step, y).start()

        @pl.when(z + step < LAYERS)
        def _(step=step):
            dn_arrival(step).wait_recv()
            if step < LAYERS - 1:

                @pl.when(has_dn)
                def _():
                    dn_copy(step).start()

            y_copy(z + step).start()
            core_copy(z + step, y).start()

        at_distance(step, lambda zz: flip(zz, y, d))
        at_distance(step - 1, take_y)
        at_distance(step - 1, lambda zz: take_core(zz, y))
        if step > 1:
            at_distance(step - 2, lambda zz: take_core(zz, 1 - y))

    at_distance(LAYERS - 1, take_y)
    at_distance(LAYERS - 1, lambda zz: take_core(zz, y))
    at_distance(LAYERS - 2, lambda zz: take_core(zz, 1 - y))
    at_distance(LAYERS - 1, lambda zz: take_core(zz, 1 - y))
    load.wait()

    def sum_copy(h, b):
        src = acc.at[h, b, pl.ds(pl.multiple_of((1 - d) * rows_half, rows_half), rows_half)]
        return to(src, core_in.at[h, b], sum_send.at[h, b], sum_recv.at[h, b], **core)

    def slot(yy, b):
        return z * per_layer + yy * per_chip + b

    def swap_copy(h, b):
        dst = raw.at[pl.ds(h * per_pass, per_pass), slot(y, b)]
        return to(y_out.at[h, b], dst, sw_send.at[h, b], sw_recv.at[h, b], **across)

    def swap_arrival(h, b):
        dst = raw.at[pl.ds(h * per_pass, per_pass), slot(1 - y, b)]
        return to(y_out.at[h, b], dst, sw_send.at[h, b], sw_recv.at[h, b], **across)

    own_rows = pl.ds(pl.multiple_of(d * rows_half, rows_half), rows_half)

    def summed(h, b, yy):
        cols = pl.ds(pl.multiple_of(yy * width, width), width)
        total = acc[h, b, own_rows, cols] + core_in[h, b, :, cols]
        return total.astype(jnp.bfloat16).reshape(per_pass, CHUNK, width)

    def finish(h, b):
        sum_copy(h, b).wait_recv()
        y_out[h, b] = summed(h, b, 1 - y)
        swap_copy(h, b).start()
        raw[pl.ds(h * per_pass, per_pass), slot(y, b)] = summed(h, b, y)

    def one_blade(h, b):
        acc[h, b] = jnp.zeros(acc.shape[2:], jnp.float32)

        def group(q, carry):
            left, image = [], []
            for i in range(BLOCK_GROUP):
                n = q * BLOCK_GROUP + i
                c = cols_ref[b, n]
                if PASSES == 1:
                    right = pan[c]
                else:
                    right = jnp.concatenate(
                        [pan[c, :, pl.ds(yy * half_cols + h * width, width)] for yy in range(PAIR)],
                        axis=1,
                    )
                product = jnp.dot(stiff[b, n], right, preferred_element_type=jnp.float32)
                image.append(product.astype(jnp.bfloat16))
                left.append(pan_t[rows_ref[b, n]])
            acc[h, b] += jnp.dot(
                jnp.concatenate(left, axis=1),
                jnp.concatenate(image, axis=0),
                preferred_element_type=jnp.float32,
            )
            return carry

        lax.fori_loop(0, n_blocks // BLOCK_GROUP, group, 0)
        sum_copy(h, b).start()

        @pl.when(b > 0)
        def _():
            finish(h, b - 1)

    def end_pass(h):
        finish(h, per_chip - 1)

        def take_swap(b, carry):
            swap_arrival(h, b).wait_recv()
            return carry

        lax.fori_loop(0, per_chip, take_swap, 0)

    def first_pass(b, carry):
        one_blade(0, b)
        return carry

    lax.fori_loop(0, per_chip, first_pass, 0)
    end_pass(0)

    n_harm = 2 * per_chip
    near = jnp.where(z < 2, 0, LAYERS - 1)
    far = LAYERS - 1 - z
    near_dev = dict(blade=near * PAIR + y)
    far_dev = dict(blade=far * PAIR + y)
    mid_dev = dict(blade=jnp.where(z < 2, 1, LAYERS - 2) * PAIR + y)

    def planes(p, zz):
        return raw.at[p, pl.ds(zz * per_layer, per_layer)]

    def end_copy(p):
        s = planes(p, near)
        return to(s, s, z_send.at[0, p], z_recv.at[0, p], **mid_dev)

    def own_copy(p):
        s = planes(p, z)
        return to(s, s, z_send.at[1, p], z_recv.at[1, p], **far_dev)

    def own_arrival(p):
        s = planes(p, far)
        return to(s, s, z_send.at[1, p], z_recv.at[1, p], **far_dev)

    def pass_copy(p):
        s = planes(p, near)
        return to(s, s, z_send.at[2, p], z_recv.at[2, p], **far_dev)

    def pass_arrival(p):
        s = planes(p, LAYERS - 1 - near)
        return to(s, s, z_send.at[2, p], z_recv.at[2, p], **far_dev)

    def comb_copy(p):
        return to(comb_out.at[p], comb_in.at[p], z_send.at[3, p], z_recv.at[3, p], **near_dev)

    def harm_copy(p):
        return to(harm_out.at[p], harm_in.at[p], h_send.at[p], h_recv.at[p], **across)

    def transform(weights, x):
        x = jnp.concatenate(
            [x[:, i : i + SUB].reshape(-1, width) for i in range(0, CHUNK, SUB)], axis=1
        )
        got = jnp.dot(weights[0], x, preferred_element_type=jnp.float32)
        got = got + jnp.dot(weights[1], x, preferred_element_type=jnp.float32)
        return [
            got[:, i * width : (i + 1) * width].reshape(-1, SUB, width)
            for i in range(CHUNK // SUB)
        ]

    def columns(p, yy):
        return pl.ds(pl.multiple_of(yy * half_cols + p // per_pass * width, width), width)

    def out_copy(r):
        rows = pl.ds(pl.multiple_of(r * CHUNK, CHUNK), CHUNK)
        return pltpu.make_async_copy(out_v.at[:, rows], out_hbm.at[:, rows], out_sem.at[r])

    def store_final(p, sub, final):
        row = lax.rem(p, per_pass) * CHUNK + sub * SUB
        first, second = final[:n_harm], final[n_harm:]
        out_v[:, pl.ds(pl.multiple_of(row, SUB), SUB), columns(p, y)] = jnp.where(
            y == 0, first, second
        )
        theirs = jnp.where(y == 0, second, first)
        harm_out[p, :, pl.ds(sub * SUB, SUB)] = theirs.astype(jnp.bfloat16)

    def take_harm(p):
        harm_copy(p).wait_recv()
        row = lax.rem(p, per_pass) * CHUNK
        out_v[:, pl.ds(pl.multiple_of(row, CHUNK), CHUNK), columns(p, 1 - y)] = harm_in[
            p
        ].astype(jnp.float32)

        @pl.when(p >= n_chunks - per_pass)
        def _():
            out_copy(p - (n_chunks - per_pass)).start()

    @pl.when(is_mid)
    def _():
        own_copy(0).start()
        own_copy(1).start()
        end_copy(0).wait_recv()
        pass_copy(0).start()

    @pl.when(is_end)
    def _():
        end_copy(0).start()
        end_copy(1).start()

    load_mid.wait()
    load_end.wait()

    def step(p, carry):
        if PASSES > 1:

            @pl.when(p < per_chip)
            def _():
                one_blade(1, p)

            @pl.when(p == per_chip)
            def _():
                end_pass(1)

        @pl.when(is_mid)
        def _():
            @pl.when(p + 2 < n_chunks)
            def _():
                own_copy(p + 2).start()

            @pl.when(p + 1 < n_chunks)
            def _():
                end_copy(p + 1).wait_recv()
                pass_copy(p + 1).start()

            own_arrival(p).wait_recv()
            pass_arrival(p).wait_recv()
            for sub, got in enumerate(transform(wmid, raw[p])):
                comb_out[p, :, pl.ds(sub * SUB, SUB)] = got[2 * n_harm :].astype(jnp.bfloat16)
                store_final(p, sub, got[: 2 * n_harm])
            comb_copy(p).start()

        @pl.when(is_end)
        def _():
            @pl.when(p + 2 < n_chunks)
            def _():
                end_copy(p + 2).start()

            comb_copy(p).wait_recv()
            own = raw[p, pl.ds(z * per_layer, per_layer)]
            for sub, got in enumerate(transform(wend, own)):
                rows = pl.ds(sub * SUB, SUB)
                store_final(p, sub, got + comb_in[p, :, rows].astype(jnp.float32))

        harm_copy(p).start()

        @pl.when(p > 0)
        def _():
            take_harm(p - 1)

        return carry

    lax.fori_loop(0, n_chunks, step, 0)
    take_harm(n_chunks - 1)

    for step in range(LAYERS - 1):

        @pl.when(jnp.logical_and(has_up, z >= step))
        def _(step=step):
            up_copy(step).wait_send()

        @pl.when(jnp.logical_and(has_dn, z + step < LAYERS))
        def _(step=step):
            dn_copy(step).wait_send()

    for zz in range(LAYERS):
        y_copy(zz).wait_send()
        for yy in range(PAIR):
            core_copy(zz, yy).wait_send()

    def drain_blade(b, carry):
        for h in range(PASSES):
            sum_copy(h, b).wait_send()
            swap_copy(h, b).wait_send()
        return carry

    lax.fori_loop(0, per_chip, drain_blade, 0)

    def drain_chunk(p, carry):
        @pl.when(is_mid)
        def _():
            own_copy(p).wait_send()
            pass_copy(p).wait_send()
            comb_copy(p).wait_send()

        @pl.when(is_end)
        def _():
            end_copy(p).wait_send()

        harm_copy(p).wait_send()
        return carry

    lax.fori_loop(0, n_chunks, drain_chunk, 0)

    def drain_out(r, carry):
        out_copy(r).wait()
        return carry

    lax.fori_loop(0, per_pass, drain_out, 0)


def line_body(panel, stiffness, block_rows, block_cols):
    per_chip, n_blocks, bs, _ = stiffness.shape
    modes = panel.shape[-1]
    shards = LAYERS * PAIR * 2
    per_shard = panel.shape[0] // bs
    n_all = shards * per_shard
    half = modes // 2
    width = half // PASSES
    per_pass = half // CHUNK
    n_chunks = per_pass * PASSES
    count = LAYERS * PAIR * per_chip
    n_harm = 2 * per_chip
    wmid, wend = dft_tables(per_chip)
    bf16, f32 = jnp.bfloat16, jnp.float32
    dma = pltpu.SemaphoreType.DMA
    vmem = pl.BlockSpec(memory_space=pltpu.VMEM)
    smem = pl.BlockSpec(memory_space=pltpu.SMEM)
    hbm = pl.BlockSpec(memory_space=pl.ANY)
    result = pl.pallas_call(
        kernel,
        out_shape=jax.ShapeDtypeStruct((n_harm, half, modes), f32),
        in_specs=[vmem, hbm, smem, smem, hbm, hbm],
        out_specs=hbm,
        scratch_shapes=[
            pltpu.VMEM((n_all, bs, modes), bf16),
            pltpu.VMEM((n_all, modes, bs), bf16),
            pltpu.VMEM(stiffness.shape, bf16),
            pltpu.VMEM((PASSES, per_chip, modes, PAIR * width), f32),
            pltpu.VMEM((PASSES, per_chip, half, PAIR * width), f32),
            pltpu.VMEM((n_chunks, count, CHUNK, width), bf16),
            pltpu.VMEM((PASSES, per_chip, per_pass, CHUNK, width), bf16),
            pltpu.VMEM(wmid.shape[1:], bf16),
            pltpu.VMEM(wend.shape[1:], bf16),
            pltpu.VMEM((n_chunks, 2 * n_harm, CHUNK, width), bf16),
            pltpu.VMEM((n_chunks, 2 * n_harm, CHUNK, width), bf16),
            pltpu.VMEM((n_chunks, n_harm, CHUNK, width), bf16),
            pltpu.VMEM((n_chunks, n_harm, CHUNK, width), bf16),
            pltpu.VMEM((n_harm, half, modes), f32),
            dma((3,)),
            dma((LAYERS - 1,)), dma((LAYERS - 1,)),
            dma((LAYERS - 1,)), dma((LAYERS - 1,)),
            dma((LAYERS,)), dma((LAYERS,)),
            dma((LAYERS * PAIR,)), dma((LAYERS * PAIR,)),
            dma((PASSES, per_chip)), dma((PASSES, per_chip)),
            dma((PASSES, per_chip)), dma((PASSES, per_chip)),
            dma((4, n_chunks)), dma((4, n_chunks)),
            dma((n_chunks,)), dma((n_chunks,)),
            dma((per_pass,)),
        ],
        compiler_params=pltpu.CompilerParams(
            collective_id=0, has_side_effects=True, vmem_limit_bytes=VMEM_BYTES
        ),
    )(
        panel.reshape(per_shard, bs, modes),
        stiffness,
        block_rows,
        block_cols,
        jnp.asarray(wmid),
        jnp.asarray(wend),
    )
    return result.reshape(2, per_chip, half, modes)


def body(panel, stiffness, block_rows, block_cols):
    block_size = stiffness.shape[-1]
    modes = panel.shape[-1]
    whole = lax.all_gather(panel, ("blade", "dof"), axis=0, tiled=True)
    blocks = whole.reshape(-1, block_size, modes)

    def one_blade(items):
        mats, rows, cols = items
        chosen = jnp.take(blocks, cols, axis=0)
        image = jnp.einsum("nij,njm->nim", mats, chosen, preferred_element_type=jnp.float32)
        image = image.astype(jnp.bfloat16)
        left = jnp.take(blocks, rows, axis=0).reshape(-1, modes)
        return lax.dot_general(
            left,
            image.reshape(-1, modes),
            (((0,), (0,)), ((), ())),
            preferred_element_type=jnp.float32,
        )

    partial_proj = lax.map(one_blade, (stiffness, block_rows, block_cols))
    half = lax.psum_scatter(partial_proj, "dof", scatter_dimension=1, tiled=True)
    half = half.astype(jnp.bfloat16)
    blade_count = stiffness.shape[0] * lax.axis_size("blade")
    index = jnp.arange(blade_count, dtype=jnp.int32)
    angle = (index[:, None] * index[None, :] % blade_count).astype(jnp.float32) * (
        2.0 * math.pi / blade_count
    )
    table = jnp.stack([jnp.cos(angle), -jnp.sin(angle)])
    stacked = lax.all_to_all(half, "blade", split_axis=1, concat_axis=0, tiled=True)
    joined = jnp.einsum(
        "phb,brc->phrc", table, stacked.astype(jnp.float32), precision=lax.Precision.HIGHEST
    ).astype(jnp.bfloat16)
    full_spec = lax.all_to_all(joined, "blade", split_axis=1, concat_axis=2, tiled=True)
    return full_spec.astype(jnp.float32)


def solution(mesh):
    placed = (
        P(("grp", "blade", "dof"), None),
        P(("grp", "blade"), "dof", None, None),
        P(("grp", "blade"), "dof"),
        P(("grp", "blade"), "dof"),
    )
    chips = mesh.shape["blade"]
    return jax.shard_map(
        line_body if chips == LAYERS * PAIR else body,
        mesh=mesh,
        in_specs=placed,
        out_specs=P(None, ("grp", "blade"), "dof", None),
        check_vma=False,
    )
```

```python
import math

import jax
import jax.numpy as jnp
import numpy as np
from jax import lax
from jax.experimental import pallas as pl
from jax.experimental.pallas import tpu as pltpu
from jax.sharding import PartitionSpec as P

MESH = pl.DeviceIdType.MESH
LAYERS = 4
PAIR = 2
BLOCK_GROUP = 8
CHUNK = 16
AHEAD = 5
PASS_AHEAD = 3
SUB = 16
VMEM_BYTES = 60 * 1024 * 1024
PASSES = 1


def dft_tables(per_chip):
    per_layer = PAIR * per_chip
    count = LAYERS * per_layer
    index = np.arange(count)
    angle = (index[:, None] * index[None, :] % count) * (2.0 * math.pi / count)
    full = np.stack([np.cos(angle), -np.sin(angle)])

    def rows_for(layer):
        part = full[:, layer * per_layer : (layer + 1) * per_layer]
        part = part.reshape(2, PAIR, per_chip, count).transpose(1, 0, 2, 3)
        return part.reshape(2 * per_layer, count)

    def split(weights):
        wide = np.kron(weights, np.eye(SUB)).astype(np.float32)
        high = wide.astype(jnp.bfloat16)
        low = (wide - high.astype(np.float32)).astype(jnp.bfloat16)
        return np.stack([high, low])

    middle, ends = [], []
    for layer, near in ((1, 0), (2, 3)):
        partial = rows_for(near).copy()
        partial[:, near * per_layer : (near + 1) * per_layer] = 0.0
        middle.append(split(np.concatenate([rows_for(layer), partial])))
        own = rows_for(near)[:, near * per_layer : (near + 1) * per_layer]
        ends.append(split(own))
    return np.stack(middle), np.stack(ends)


def kernel(
    panel_ref, stiff_hbm, rows_ref, cols_ref, wmid_hbm, wend_hbm, out_hbm,
    pan, pan_t, stiff, acc, core_in, raw, y_out, wmid, wend,
    comb_out, comb_in, harm_out, harm_in, out_v,
    load_sem, up_send, up_recv, dn_send, dn_recv, ys_send, ys_recv, co_send, co_recv,
    sum_send, sum_recv, sw_send, sw_recv, z_send, z_recv, h_send, h_recv, out_sem,
):
    blade = lax.axis_index("blade")
    d = lax.axis_index("dof")
    z = blade // PAIR
    y = blade % PAIR
    other_y = z * PAIR + (1 - y)
    per_chip, n_blocks = stiff.shape[0], stiff.shape[1]
    per_layer = per_chip * PAIR
    rows_half = core_in.shape[2]
    n_chunks = raw.shape[0]
    per_pass = n_chunks // PASSES
    width = raw.shape[3]
    half_cols = width * PASSES
    per_shard = panel_ref.shape[0]

    def to(src, dst, send, recv, **device):
        return pltpu.make_async_remote_copy(
            src_ref=src, dst_ref=dst, send_sem=send, recv_sem=recv,
            device_id=device, device_id_type=MESH,
        )

    core = dict(dof=1 - d)
    across = dict(blade=other_y)
    up = dict(blade=jnp.minimum(blade + PAIR, LAYERS * PAIR - 1))
    down = dict(blade=jnp.maximum(blade - PAIR, 0))
    has_up = z < LAYERS - 1
    has_dn = z > 0
    is_mid = jnp.logical_and(has_up, has_dn)
    is_end = jnp.logical_not(is_mid)
    which = z // 2

    load = pltpu.make_async_copy(stiff_hbm, stiff, load_sem.at[0])
    load.start()
    load_mid = pltpu.make_async_copy(wmid_hbm.at[which], wmid, load_sem.at[1])
    load_mid.start()
    load_end = pltpu.make_async_copy(wend_hbm.at[which], wend, load_sem.at[2])
    load_end.start()

    barrier = pltpu.get_barrier_semaphore()
    pl.semaphore_signal(barrier, inc=1, device_id=core, device_id_type=MESH)
    pl.semaphore_signal(barrier, inc=1, device_id=across, device_id_type=MESH)

    @pl.when(has_up)
    def _():
        pl.semaphore_signal(barrier, inc=1, device_id=up, device_id_type=MESH)

    @pl.when(has_dn)
    def _():
        pl.semaphore_signal(barrier, inc=1, device_id=down, device_id_type=MESH)

    pl.semaphore_wait(barrier, 2 + has_up.astype(jnp.int32) + has_dn.astype(jnp.int32))

    def shard(zz, yy, dd):
        start = ((zz * PAIR + yy) * 2 + dd) * per_shard
        return pan.at[pl.ds(start, per_shard)]

    def flip(zz, yy, dd):
        start = ((zz * PAIR + yy) * 2 + dd) * per_shard
        for i in range(per_shard):
            pan_t[start + i] = pan[start + i].T

    def up_copy(step):
        s = shard(jnp.maximum(z - step, 0), y, d)
        return to(s, s, up_send.at[step], up_recv.at[step], **up)

    def dn_copy(step):
        s = shard(jnp.minimum(z + step, LAYERS - 1), y, d)
        return to(s, s, dn_send.at[step], dn_recv.at[step], **down)

    def up_arrival(step):
        s = shard(jnp.maximum(z - step, 0), y, d)
        return to(s, s, up_send.at[step - 1], up_recv.at[step - 1], **up)

    def dn_arrival(step):
        s = shard(jnp.minimum(z + step, LAYERS - 1), y, d)
        return to(s, s, dn_send.at[step - 1], dn_recv.at[step - 1], **down)

    def y_copy(zz):
        s = shard(zz, y, d)
        return to(s, s, ys_send.at[zz], ys_recv.at[zz], **across)

    def y_arrival(zz):
        s = shard(zz, 1 - y, d)
        return to(s, s, ys_send.at[zz], ys_recv.at[zz], **across)

    def core_copy(zz, yy):
        s = shard(zz, yy, d)
        return to(s, s, co_send.at[zz * PAIR + yy], co_recv.at[zz * PAIR + yy], **core)

    def core_arrival(zz, yy):
        s = shard(zz, yy, 1 - d)
        return to(s, s, co_send.at[zz * PAIR + yy], co_recv.at[zz * PAIR + yy], **core)

    mine = ((z * PAIR + y) * 2 + d) * per_shard
    pan[pl.ds(mine, per_shard)] = panel_ref[...]

    @pl.when(has_up)
    def _():
        up_copy(0).start()

    @pl.when(has_dn)
    def _():
        dn_copy(0).start()

    y_copy(z).start()
    core_copy(z, y).start()
    flip(z, y, d)

    def take_y(zz):
        y_arrival(zz).wait_recv()
        core_copy(zz, 1 - y).start()
        flip(zz, 1 - y, d)

    def take_core(zz, yy):
        core_arrival(zz, yy).wait_recv()
        flip(zz, yy, 1 - d)

    def at_distance(step, do):
        if step == 0:
            do(z)
            return

        @pl.when(z >= step)
        def _():
            do(z - step)

        @pl.when(z + step < LAYERS)
        def _():
            do(z + step)

    for step in range(1, LAYERS):

        @pl.when(z >= step)
        def _(step=step):
            up_arrival(step).wait_recv()
            if step < LAYERS - 1:

                @pl.when(has_up)
                def _():
                    up_copy(step).start()

            y_copy(z - step).start()
            core_copy(z - step, y).start()

        @pl.when(z + step < LAYERS)
        def _(step=step):
            dn_arrival(step).wait_recv()
            if step < LAYERS - 1:

                @pl.when(has_dn)
                def _():
                    dn_copy(step).start()

            y_copy(z + step).start()
            core_copy(z + step, y).start()

        at_distance(step, lambda zz: flip(zz, y, d))
        at_distance(step - 1, take_y)
        at_distance(step - 1, lambda zz: take_core(zz, y))
        if step > 1:
            at_distance(step - 2, lambda zz: take_core(zz, 1 - y))

    at_distance(LAYERS - 1, take_y)
    at_distance(LAYERS - 1, lambda zz: take_core(zz, y))
    at_distance(LAYERS - 2, lambda zz: take_core(zz, 1 - y))
    at_distance(LAYERS - 1, lambda zz: take_core(zz, 1 - y))
    load.wait()

    def sum_copy(h, b):
        src = acc.at[h, b, pl.ds(pl.multiple_of((1 - d) * rows_half, rows_half), rows_half)]
        return to(src, core_in.at[h, b], sum_send.at[h, b], sum_recv.at[h, b], **core)

    def slot(yy, b):
        return z * per_layer + yy * per_chip + b

    def swap_copy(h, b):
        dst = raw.at[pl.ds(h * per_pass, per_pass), slot(y, b)]
        return to(y_out.at[h, b], dst, sw_send.at[h, b], sw_recv.at[h, b], **across)

    def swap_arrival(h, b):
        dst = raw.at[pl.ds(h * per_pass, per_pass), slot(1 - y, b)]
        return to(y_out.at[h, b], dst, sw_send.at[h, b], sw_recv.at[h, b], **across)

    own_rows = pl.ds(pl.multiple_of(d * rows_half, rows_half), rows_half)

    def summed(h, b, yy):
        cols = pl.ds(pl.multiple_of(yy * width, width), width)
        total = acc[h, b, own_rows, cols] + core_in[h, b, :, cols]
        return total.astype(jnp.bfloat16).reshape(per_pass, CHUNK, width)

    def finish(h, b):
        sum_copy(h, b).wait_recv()
        y_out[h, b] = summed(h, b, 1 - y)
        swap_copy(h, b).start()
        raw[pl.ds(h * per_pass, per_pass), slot(y, b)] = summed(h, b, y)

    def one_blade(h, b):
        acc[h, b] = jnp.zeros(acc.shape[2:], jnp.float32)

        def group(q, carry):
            left, image = [], []
            for i in range(BLOCK_GROUP):
                n = q * BLOCK_GROUP + i
                c = cols_ref[b, n]
                if PASSES == 1:
                    right = pan[c]
                else:
                    right = jnp.concatenate(
                        [pan[c, :, pl.ds(yy * half_cols + h * width, width)] for yy in range(PAIR)],
                        axis=1,
                    )
                product = jnp.dot(stiff[b, n], right, preferred_element_type=jnp.float32)
                image.append(product.astype(jnp.bfloat16))
                left.append(pan_t[rows_ref[b, n]])
            acc[h, b] += jnp.dot(
                jnp.concatenate(left, axis=1),
                jnp.concatenate(image, axis=0),
                preferred_element_type=jnp.float32,
            )
            return carry

        lax.fori_loop(0, n_blocks // BLOCK_GROUP, group, 0)
        sum_copy(h, b).start()

        @pl.when(b > 0)
        def _():
            finish(h, b - 1)

    def end_pass(h):
        finish(h, per_chip - 1)

        def take_swap(b, carry):
            swap_arrival(h, b).wait_recv()
            return carry

        lax.fori_loop(0, per_chip, take_swap, 0)

    def first_pass(b, carry):
        one_blade(0, b)
        return carry

    lax.fori_loop(0, per_chip, first_pass, 0)
    end_pass(0)

    n_harm = 2 * per_chip
    near = jnp.where(z < 2, 0, LAYERS - 1)
    far = LAYERS - 1 - z
    near_dev = dict(blade=near * PAIR + y)
    far_dev = dict(blade=far * PAIR + y)
    mid_dev = dict(blade=jnp.where(z < 2, 1, LAYERS - 2) * PAIR + y)

    def planes(p, zz):
        return raw.at[p, pl.ds(zz * per_layer, per_layer)]

    def end_copy(p):
        s = planes(p, near)
        return to(s, s, z_send.at[0, p], z_recv.at[0, p], **mid_dev)

    def own_copy(p):
        s = planes(p, z)
        return to(s, s, z_send.at[1, p], z_recv.at[1, p], **far_dev)

    def own_arrival(p):
        s = planes(p, far)
        return to(s, s, z_send.at[1, p], z_recv.at[1, p], **far_dev)

    def pass_copy(p):
        s = planes(p, near)
        return to(s, s, z_send.at[2, p], z_recv.at[2, p], **far_dev)

    def pass_arrival(p):
        s = planes(p, LAYERS - 1 - near)
        return to(s, s, z_send.at[2, p], z_recv.at[2, p], **far_dev)

    def comb_copy(p):
        return to(comb_out.at[p], comb_in.at[p], z_send.at[3, p], z_recv.at[3, p], **near_dev)

    def harm_copy(p):
        return to(harm_out.at[p], harm_in.at[p], h_send.at[p], h_recv.at[p], **across)

    def transform(weights, x):
        x = jnp.concatenate(
            [x[:, i : i + SUB].reshape(-1, width) for i in range(0, CHUNK, SUB)], axis=1
        )
        got = jnp.dot(weights[0], x, preferred_element_type=jnp.float32)
        got = got + jnp.dot(weights[1], x, preferred_element_type=jnp.float32)
        return [
            got[:, i * width : (i + 1) * width].reshape(-1, SUB, width)
            for i in range(CHUNK // SUB)
        ]

    def columns(p, yy):
        return pl.ds(pl.multiple_of(yy * half_cols + p // per_pass * width, width), width)

    def out_copy(r):
        rows = pl.ds(pl.multiple_of(r * CHUNK, CHUNK), CHUNK)
        return pltpu.make_async_copy(out_v.at[:, rows], out_hbm.at[:, rows], out_sem.at[r])

    def store_final(p, sub, final):
        row = lax.rem(p, per_pass) * CHUNK + sub * SUB
        first, second = final[:n_harm], final[n_harm:]
        out_v[:, pl.ds(pl.multiple_of(row, SUB), SUB), columns(p, y)] = jnp.where(
            y == 0, first, second
        )
        theirs = jnp.where(y == 0, second, first)
        harm_out[p, :, pl.ds(sub * SUB, SUB)] = theirs.astype(jnp.bfloat16)

    def take_harm(p):
        harm_copy(p).wait_recv()
        row = lax.rem(p, per_pass) * CHUNK
        out_v[:, pl.ds(pl.multiple_of(row, CHUNK), CHUNK), columns(p, 1 - y)] = harm_in[
            p
        ].astype(jnp.float32)

        @pl.when(p >= n_chunks - per_pass)
        def _():
            out_copy(p - (n_chunks - per_pass)).start()

    @pl.when(is_mid)
    def _():
        own_copy(0).start()
        for p in range(1, AHEAD):
            own_copy(p).start()
            if p <= PASS_AHEAD:
                end_copy(p - 1).wait_recv()
                pass_copy(p - 1).start()

    @pl.when(is_end)
    def _():
        for p in range(AHEAD):
            end_copy(p).start()

    load_mid.wait()
    load_end.wait()

    def step(p, carry):
        if PASSES > 1:

            @pl.when(p < per_chip // 2)
            def _():
                def second_pass(b, carry):
                    one_blade(1, 2 * p + b)
                    return carry

                lax.fori_loop(0, 2, second_pass, 0)

            @pl.when(p == per_chip // 2)
            def _():
                end_pass(1)

        @pl.when(is_mid)
        def _():
            @pl.when(p + AHEAD < n_chunks)
            def _():
                own_copy(p + AHEAD).start()

            @pl.when(p + PASS_AHEAD < n_chunks)
            def _():
                end_copy(p + PASS_AHEAD).wait_recv()
                pass_copy(p + PASS_AHEAD).start()

            own_arrival(p).wait_recv()
            pass_arrival(p).wait_recv()
            for sub, got in enumerate(transform(wmid, raw[p])):
                comb_out[p, :, pl.ds(sub * SUB, SUB)] = got[2 * n_harm :].astype(jnp.bfloat16)
                store_final(p, sub, got[: 2 * n_harm])
            comb_copy(p).start()

        @pl.when(is_end)
        def _():
            @pl.when(p + AHEAD < n_chunks)
            def _():
                end_copy(p + AHEAD).start()

            comb_copy(p).wait_recv()
            own = raw[p, pl.ds(z * per_layer, per_layer)]
            for sub, got in enumerate(transform(wend, own)):
                rows = pl.ds(sub * SUB, SUB)
                store_final(p, sub, got + comb_in[p, :, rows].astype(jnp.float32))

        harm_copy(p).start()

        @pl.when(p > 0)
        def _():
            take_harm(p - 1)

        return carry

    lax.fori_loop(0, n_chunks, step, 0)
    take_harm(n_chunks - 1)

    for step in range(LAYERS - 1):

        @pl.when(jnp.logical_and(has_up, z >= step))
        def _(step=step):
            up_copy(step).wait_send()

        @pl.when(jnp.logical_and(has_dn, z + step < LAYERS))
        def _(step=step):
            dn_copy(step).wait_send()

    for zz in range(LAYERS):
        y_copy(zz).wait_send()
        for yy in range(PAIR):
            core_copy(zz, yy).wait_send()

    def drain_blade(b, carry):
        for h in range(PASSES):
            sum_copy(h, b).wait_send()
            swap_copy(h, b).wait_send()
        return carry

    lax.fori_loop(0, per_chip, drain_blade, 0)

    def drain_chunk(p, carry):
        @pl.when(is_mid)
        def _():
            own_copy(p).wait_send()
            pass_copy(p).wait_send()
            comb_copy(p).wait_send()

        @pl.when(is_end)
        def _():
            end_copy(p).wait_send()

        harm_copy(p).wait_send()
        return carry

    lax.fori_loop(0, n_chunks, drain_chunk, 0)

    def drain_out(r, carry):
        out_copy(r).wait()
        return carry

    lax.fori_loop(0, per_pass, drain_out, 0)


def line_body(panel, stiffness, block_rows, block_cols):
    per_chip, n_blocks, bs, _ = stiffness.shape
    modes = panel.shape[-1]
    shards = LAYERS * PAIR * 2
    per_shard = panel.shape[0] // bs
    n_all = shards * per_shard
    half = modes // 2
    width = half // PASSES
    per_pass = half // CHUNK
    n_chunks = per_pass * PASSES
    count = LAYERS * PAIR * per_chip
    n_harm = 2 * per_chip
    wmid, wend = dft_tables(per_chip)
    bf16, f32 = jnp.bfloat16, jnp.float32
    dma = pltpu.SemaphoreType.DMA
    vmem = pl.BlockSpec(memory_space=pltpu.VMEM)
    smem = pl.BlockSpec(memory_space=pltpu.SMEM)
    hbm = pl.BlockSpec(memory_space=pl.ANY)
    result = pl.pallas_call(
        kernel,
        out_shape=jax.ShapeDtypeStruct((n_harm, half, modes), f32),
        in_specs=[vmem, hbm, smem, smem, hbm, hbm],
        out_specs=hbm,
        scratch_shapes=[
            pltpu.VMEM((n_all, bs, modes), bf16),
            pltpu.VMEM((n_all, modes, bs), bf16),
            pltpu.VMEM(stiffness.shape, bf16),
            pltpu.VMEM((PASSES, per_chip, modes, PAIR * width), f32),
            pltpu.VMEM((PASSES, per_chip, half, PAIR * width), f32),
            pltpu.VMEM((n_chunks, count, CHUNK, width), bf16),
            pltpu.VMEM((PASSES, per_chip, per_pass, CHUNK, width), bf16),
            pltpu.VMEM(wmid.shape[1:], bf16),
            pltpu.VMEM(wend.shape[1:], bf16),
            pltpu.VMEM((n_chunks, 2 * n_harm, CHUNK, width), bf16),
            pltpu.VMEM((n_chunks, 2 * n_harm, CHUNK, width), bf16),
            pltpu.VMEM((n_chunks, n_harm, CHUNK, width), bf16),
            pltpu.VMEM((n_chunks, n_harm, CHUNK, width), bf16),
            pltpu.VMEM((n_harm, half, modes), f32),
            dma((3,)),
            dma((LAYERS - 1,)), dma((LAYERS - 1,)),
            dma((LAYERS - 1,)), dma((LAYERS - 1,)),
            dma((LAYERS,)), dma((LAYERS,)),
            dma((LAYERS * PAIR,)), dma((LAYERS * PAIR,)),
            dma((PASSES, per_chip)), dma((PASSES, per_chip)),
            dma((PASSES, per_chip)), dma((PASSES, per_chip)),
            dma((4, n_chunks)), dma((4, n_chunks)),
            dma((n_chunks,)), dma((n_chunks,)),
            dma((per_pass,)),
        ],
        compiler_params=pltpu.CompilerParams(
            collective_id=0, has_side_effects=True, vmem_limit_bytes=VMEM_BYTES
        ),
    )(
        panel.reshape(per_shard, bs, modes),
        stiffness,
        block_rows,
        block_cols,
        jnp.asarray(wmid),
        jnp.asarray(wend),
    )
    return result.reshape(2, per_chip, half, modes)


def body(panel, stiffness, block_rows, block_cols):
    block_size = stiffness.shape[-1]
    modes = panel.shape[-1]
    whole = lax.all_gather(panel, ("blade", "dof"), axis=0, tiled=True)
    blocks = whole.reshape(-1, block_size, modes)

    def one_blade(items):
        mats, rows, cols = items
        chosen = jnp.take(blocks, cols, axis=0)
        image = jnp.einsum("nij,njm->nim", mats, chosen, preferred_element_type=jnp.float32)
        image = image.astype(jnp.bfloat16)
        left = jnp.take(blocks, rows, axis=0).reshape(-1, modes)
        return lax.dot_general(
            left,
            image.reshape(-1, modes),
            (((0,), (0,)), ((), ())),
            preferred_element_type=jnp.float32,
        )

    partial_proj = lax.map(one_blade, (stiffness, block_rows, block_cols))
    half = lax.psum_scatter(partial_proj, "dof", scatter_dimension=1, tiled=True)
    half = half.astype(jnp.bfloat16)
    blade_count = stiffness.shape[0] * lax.axis_size("blade")
    index = jnp.arange(blade_count, dtype=jnp.int32)
    angle = (index[:, None] * index[None, :] % blade_count).astype(jnp.float32) * (
        2.0 * math.pi / blade_count
    )
    table = jnp.stack([jnp.cos(angle), -jnp.sin(angle)])
    stacked = lax.all_to_all(half, "blade", split_axis=1, concat_axis=0, tiled=True)
    joined = jnp.einsum(
        "phb,brc->phrc", table, stacked.astype(jnp.float32), precision=lax.Precision.HIGHEST
    ).astype(jnp.bfloat16)
    full_spec = lax.all_to_all(joined, "blade", split_axis=1, concat_axis=2, tiled=True)
    return full_spec.astype(jnp.float32)


def solution(mesh):
    placed = (
        P(("grp", "blade", "dof"), None),
        P(("grp", "blade"), "dof", None, None),
        P(("grp", "blade"), "dof"),
        P(("grp", "blade"), "dof"),
    )
    chips = mesh.shape["blade"]
    return jax.shard_map(
        line_body if chips == LAYERS * PAIR else body,
        mesh=mesh,
        in_specs=placed,
        out_specs=P(None, ("grp", "blade"), "dof", None),
        check_vma=False,
    )
```

```python
import math

import jax
import jax.numpy as jnp
import numpy as np
from jax import lax
from jax.experimental import pallas as pl
from jax.experimental.pallas import tpu as pltpu
from jax.sharding import PartitionSpec as P

MESH = pl.DeviceIdType.MESH
LAYERS = 4
PAIR = 2
BLOCK_GROUP = 8
CHUNK = 32
AHEAD = 5
PASS_AHEAD = 3
SUB = 16
VMEM_BYTES = 60 * 1024 * 1024
PASSES = 2


def dft_tables(per_chip):
    per_layer = PAIR * per_chip
    count = LAYERS * per_layer
    index = np.arange(count)
    angle = (index[:, None] * index[None, :] % count) * (2.0 * math.pi / count)
    full = np.stack([np.cos(angle), -np.sin(angle)])

    def rows_for(layer):
        part = full[:, layer * per_layer : (layer + 1) * per_layer]
        part = part.reshape(2, PAIR, per_chip, count).transpose(1, 0, 2, 3)
        return part.reshape(2 * per_layer, count)

    def split(weights):
        wide = np.kron(weights, np.eye(SUB)).astype(np.float32)
        high = wide.astype(jnp.bfloat16)
        low = (wide - high.astype(np.float32)).astype(jnp.bfloat16)
        return np.stack([high, low])

    middle, ends = [], []
    for layer, near in ((1, 0), (2, 3)):
        partial = rows_for(near).copy()
        partial[:, near * per_layer : (near + 1) * per_layer] = 0.0
        middle.append(split(np.concatenate([rows_for(layer), partial])))
        own = rows_for(near)[:, near * per_layer : (near + 1) * per_layer]
        ends.append(split(own))
    return np.stack(middle), np.stack(ends)


def kernel(
    panel_ref, stiff_hbm, rows_ref, cols_ref, wmid_hbm, wend_hbm, out_hbm,
    pan, pan_t, stiff, acc, core_in, raw, y_out, wmid, wend,
    comb_out, comb_in, harm_out, harm_in, out_v,
    load_sem, up_send, up_recv, dn_send, dn_recv, ys_send, ys_recv, co_send, co_recv,
    sum_send, sum_recv, sw_send, sw_recv, z_send, z_recv, h_send, h_recv, out_sem,
):
    blade = lax.axis_index("blade")
    d = lax.axis_index("dof")
    z = blade // PAIR
    y = blade % PAIR
    other_y = z * PAIR + (1 - y)
    per_chip, n_blocks = stiff.shape[0], stiff.shape[1]
    per_layer = per_chip * PAIR
    rows_half = core_in.shape[2]
    n_chunks = raw.shape[0]
    per_pass = n_chunks // PASSES
    width = raw.shape[3]
    half_cols = width * PASSES
    per_shard = panel_ref.shape[0]

    def to(src, dst, send, recv, **device):
        return pltpu.make_async_remote_copy(
            src_ref=src, dst_ref=dst, send_sem=send, recv_sem=recv,
            device_id=device, device_id_type=MESH,
        )

    core = dict(dof=1 - d)
    across = dict(blade=other_y)
    up = dict(blade=jnp.minimum(blade + PAIR, LAYERS * PAIR - 1))
    down = dict(blade=jnp.maximum(blade - PAIR, 0))
    has_up = z < LAYERS - 1
    has_dn = z > 0
    is_mid = jnp.logical_and(has_up, has_dn)
    is_end = jnp.logical_not(is_mid)
    which = z // 2

    load = pltpu.make_async_copy(stiff_hbm, stiff, load_sem.at[0])
    load.start()
    load_mid = pltpu.make_async_copy(wmid_hbm.at[which], wmid, load_sem.at[1])
    load_mid.start()
    load_end = pltpu.make_async_copy(wend_hbm.at[which], wend, load_sem.at[2])
    load_end.start()

    barrier = pltpu.get_barrier_semaphore()
    pl.semaphore_signal(barrier, inc=1, device_id=core, device_id_type=MESH)
    pl.semaphore_signal(barrier, inc=1, device_id=across, device_id_type=MESH)

    @pl.when(has_up)
    def _():
        pl.semaphore_signal(barrier, inc=1, device_id=up, device_id_type=MESH)

    @pl.when(has_dn)
    def _():
        pl.semaphore_signal(barrier, inc=1, device_id=down, device_id_type=MESH)

    pl.semaphore_wait(barrier, 2 + has_up.astype(jnp.int32) + has_dn.astype(jnp.int32))

    def shard(zz, yy, dd):
        start = ((zz * PAIR + yy) * 2 + dd) * per_shard
        return pan.at[pl.ds(start, per_shard)]

    def flip(zz, yy, dd):
        start = ((zz * PAIR + yy) * 2 + dd) * per_shard
        for i in range(per_shard):
            pan_t[start + i] = pan[start + i].T

    def up_copy(step):
        s = shard(jnp.maximum(z - step, 0), y, d)
        return to(s, s, up_send.at[step], up_recv.at[step], **up)

    def dn_copy(step):
        s = shard(jnp.minimum(z + step, LAYERS - 1), y, d)
        return to(s, s, dn_send.at[step], dn_recv.at[step], **down)

    def up_arrival(step):
        s = shard(jnp.maximum(z - step, 0), y, d)
        return to(s, s, up_send.at[step - 1], up_recv.at[step - 1], **up)

    def dn_arrival(step):
        s = shard(jnp.minimum(z + step, LAYERS - 1), y, d)
        return to(s, s, dn_send.at[step - 1], dn_recv.at[step - 1], **down)

    def y_copy(zz):
        s = shard(zz, y, d)
        return to(s, s, ys_send.at[zz], ys_recv.at[zz], **across)

    def y_arrival(zz):
        s = shard(zz, 1 - y, d)
        return to(s, s, ys_send.at[zz], ys_recv.at[zz], **across)

    def core_copy(zz, yy):
        s = shard(zz, yy, d)
        return to(s, s, co_send.at[zz * PAIR + yy], co_recv.at[zz * PAIR + yy], **core)

    def core_arrival(zz, yy):
        s = shard(zz, yy, 1 - d)
        return to(s, s, co_send.at[zz * PAIR + yy], co_recv.at[zz * PAIR + yy], **core)

    mine = ((z * PAIR + y) * 2 + d) * per_shard
    pan[pl.ds(mine, per_shard)] = panel_ref[...]

    @pl.when(has_up)
    def _():
        up_copy(0).start()

    @pl.when(has_dn)
    def _():
        dn_copy(0).start()

    y_copy(z).start()
    core_copy(z, y).start()
    flip(z, y, d)

    def take_y(zz):
        y_arrival(zz).wait_recv()
        core_copy(zz, 1 - y).start()
        flip(zz, 1 - y, d)

    def take_core(zz, yy):
        core_arrival(zz, yy).wait_recv()
        flip(zz, yy, 1 - d)

    def at_distance(step, do):
        if step == 0:
            do(z)
            return

        @pl.when(z >= step)
        def _():
            do(z - step)

        @pl.when(z + step < LAYERS)
        def _():
            do(z + step)

    for step in range(1, LAYERS):

        @pl.when(z >= step)
        def _(step=step):
            up_arrival(step).wait_recv()
            if step < LAYERS - 1:

                @pl.when(has_up)
                def _():
                    up_copy(step).start()

            y_copy(z - step).start()
            core_copy(z - step, y).start()

        @pl.when(z + step < LAYERS)
        def _(step=step):
            dn_arrival(step).wait_recv()
            if step < LAYERS - 1:

                @pl.when(has_dn)
                def _():
                    dn_copy(step).start()

            y_copy(z + step).start()
            core_copy(z + step, y).start()

        at_distance(step, lambda zz: flip(zz, y, d))
        at_distance(step - 1, take_y)
        at_distance(step - 1, lambda zz: take_core(zz, y))
        if step > 1:
            at_distance(step - 2, lambda zz: take_core(zz, 1 - y))

    at_distance(LAYERS - 1, take_y)
    at_distance(LAYERS - 1, lambda zz: take_core(zz, y))
    at_distance(LAYERS - 2, lambda zz: take_core(zz, 1 - y))
    at_distance(LAYERS - 1, lambda zz: take_core(zz, 1 - y))
    load.wait()

    def sum_copy(h, b):
        src = acc.at[h, b, pl.ds(pl.multiple_of((1 - d) * rows_half, rows_half), rows_half)]
        return to(src, core_in.at[h, b], sum_send.at[h, b], sum_recv.at[h, b], **core)

    def slot(yy, b):
        return z * per_layer + yy * per_chip + b

    def swap_copy(h, b):
        dst = raw.at[pl.ds(h * per_pass, per_pass), slot(y, b)]
        return to(y_out.at[h, b], dst, sw_send.at[h, b], sw_recv.at[h, b], **across)

    def swap_arrival(h, b):
        dst = raw.at[pl.ds(h * per_pass, per_pass), slot(1 - y, b)]
        return to(y_out.at[h, b], dst, sw_send.at[h, b], sw_recv.at[h, b], **across)

    own_rows = pl.ds(pl.multiple_of(d * rows_half, rows_half), rows_half)

    def summed(h, b, yy):
        cols = pl.ds(pl.multiple_of(yy * width, width), width)
        total = acc[h, b, own_rows, cols] + core_in[h, b, :, cols]
        return total.astype(jnp.bfloat16).reshape(per_pass, CHUNK, width)

    def finish(h, b):
        sum_copy(h, b).wait_recv()
        y_out[h, b] = summed(h, b, 1 - y)
        swap_copy(h, b).start()
        raw[pl.ds(h * per_pass, per_pass), slot(y, b)] = summed(h, b, y)

    def one_blade(h, b):
        acc[h, b] = jnp.zeros(acc.shape[2:], jnp.float32)

        def group(q, carry):
            left, image = [], []
            for i in range(BLOCK_GROUP):
                n = q * BLOCK_GROUP + i
                c = cols_ref[b, n]
                if PASSES == 1:
                    right = pan[c]
                else:
                    right = jnp.concatenate(
                        [pan[c, :, pl.ds(yy * half_cols + h * width, width)] for yy in range(PAIR)],
                        axis=1,
                    )
                product = jnp.dot(stiff[b, n], right, preferred_element_type=jnp.float32)
                image.append(product.astype(jnp.bfloat16))
                left.append(pan_t[rows_ref[b, n]])
            acc[h, b] += jnp.dot(
                jnp.concatenate(left, axis=1),
                jnp.concatenate(image, axis=0),
                preferred_element_type=jnp.float32,
            )
            return carry

        lax.fori_loop(0, n_blocks // BLOCK_GROUP, group, 0)
        sum_copy(h, b).start()

        @pl.when(b > 0)
        def _():
            finish(h, b - 1)

    def end_pass(h):
        finish(h, per_chip - 1)

        def take_swap(b, carry):
            swap_arrival(h, b).wait_recv()
            return carry

        lax.fori_loop(0, per_chip, take_swap, 0)

    def first_pass(b, carry):
        one_blade(0, b)
        return carry

    lax.fori_loop(0, per_chip, first_pass, 0)
    end_pass(0)

    n_harm = 2 * per_chip
    near = jnp.where(z < 2, 0, LAYERS - 1)
    far = LAYERS - 1 - z
    near_dev = dict(blade=near * PAIR + y)
    far_dev = dict(blade=far * PAIR + y)
    mid_dev = dict(blade=jnp.where(z < 2, 1, LAYERS - 2) * PAIR + y)

    def planes(p, zz):
        return raw.at[p, pl.ds(zz * per_layer, per_layer)]

    def end_copy(p):
        s = planes(p, near)
        return to(s, s, z_send.at[0, p], z_recv.at[0, p], **mid_dev)

    def own_copy(p):
        s = planes(p, z)
        return to(s, s, z_send.at[1, p], z_recv.at[1, p], **far_dev)

    def own_arrival(p):
        s = planes(p, far)
        return to(s, s, z_send.at[1, p], z_recv.at[1, p], **far_dev)

    def pass_copy(p):
        s = planes(p, near)
        return to(s, s, z_send.at[2, p], z_recv.at[2, p], **far_dev)

    def pass_arrival(p):
        s = planes(p, LAYERS - 1 - near)
        return to(s, s, z_send.at[2, p], z_recv.at[2, p], **far_dev)

    def comb_copy(p):
        return to(comb_out.at[p], comb_in.at[p], z_send.at[3, p], z_recv.at[3, p], **near_dev)

    def harm_copy(p):
        return to(harm_out.at[p], harm_in.at[p], h_send.at[p], h_recv.at[p], **across)

    def transform(weights, x):
        x = jnp.concatenate(
            [x[:, i : i + SUB].reshape(-1, width) for i in range(0, CHUNK, SUB)], axis=1
        )
        got = jnp.dot(weights[0], x, preferred_element_type=jnp.float32)
        got = got + jnp.dot(weights[1], x, preferred_element_type=jnp.float32)
        return [
            got[:, i * width : (i + 1) * width].reshape(-1, SUB, width)
            for i in range(CHUNK // SUB)
        ]

    def columns(p, yy):
        return pl.ds(pl.multiple_of(yy * half_cols + p // per_pass * width, width), width)

    def out_copy(r):
        rows = pl.ds(pl.multiple_of(r * CHUNK, CHUNK), CHUNK)
        return pltpu.make_async_copy(out_v.at[:, rows], out_hbm.at[:, rows], out_sem.at[r])

    def store_final(p, sub, final):
        row = lax.rem(p, per_pass) * CHUNK + sub * SUB
        first, second = final[:n_harm], final[n_harm:]
        out_v[:, pl.ds(pl.multiple_of(row, SUB), SUB), columns(p, y)] = jnp.where(
            y == 0, first, second
        )
        theirs = jnp.where(y == 0, second, first)
        harm_out[p, :, pl.ds(sub * SUB, SUB)] = theirs.astype(jnp.bfloat16)

    def take_harm(p):
        harm_copy(p).wait_recv()
        row = lax.rem(p, per_pass) * CHUNK
        out_v[:, pl.ds(pl.multiple_of(row, CHUNK), CHUNK), columns(p, 1 - y)] = harm_in[
            p
        ].astype(jnp.float32)

        @pl.when(p >= n_chunks - per_pass)
        def _():
            out_copy(p - (n_chunks - per_pass)).start()

    @pl.when(is_mid)
    def _():
        own_copy(0).start()
        for p in range(1, AHEAD):
            own_copy(p).start()
            if p <= PASS_AHEAD:
                end_copy(p - 1).wait_recv()
                pass_copy(p - 1).start()

    @pl.when(is_end)
    def _():
        for p in range(AHEAD):
            end_copy(p).start()

    load_mid.wait()
    load_end.wait()

    def step(p, carry):
        if PASSES > 1:

            @pl.when(p < per_chip // 2)
            def _():
                def second_pass(b, carry):
                    one_blade(1, 2 * p + b)
                    return carry

                lax.fori_loop(0, 2, second_pass, 0)

            @pl.when(p == per_chip // 2)
            def _():
                end_pass(1)

        @pl.when(is_mid)
        def _():
            @pl.when(p + AHEAD < n_chunks)
            def _():
                own_copy(p + AHEAD).start()

            @pl.when(p + PASS_AHEAD < n_chunks)
            def _():
                end_copy(p + PASS_AHEAD).wait_recv()
                pass_copy(p + PASS_AHEAD).start()

            own_arrival(p).wait_recv()
            pass_arrival(p).wait_recv()
            for sub, got in enumerate(transform(wmid, raw[p])):
                comb_out[p, :, pl.ds(sub * SUB, SUB)] = got[2 * n_harm :].astype(jnp.bfloat16)
                store_final(p, sub, got[: 2 * n_harm])
            comb_copy(p).start()

        @pl.when(is_end)
        def _():
            @pl.when(p + AHEAD < n_chunks)
            def _():
                end_copy(p + AHEAD).start()

            comb_copy(p).wait_recv()
            own = raw[p, pl.ds(z * per_layer, per_layer)]
            for sub, got in enumerate(transform(wend, own)):
                rows = pl.ds(sub * SUB, SUB)
                store_final(p, sub, got + comb_in[p, :, rows].astype(jnp.float32))

        harm_copy(p).start()

        @pl.when(p > 0)
        def _():
            take_harm(p - 1)

        return carry

    lax.fori_loop(0, n_chunks, step, 0)
    take_harm(n_chunks - 1)

    for step in range(LAYERS - 1):

        @pl.when(jnp.logical_and(has_up, z >= step))
        def _(step=step):
            up_copy(step).wait_send()

        @pl.when(jnp.logical_and(has_dn, z + step < LAYERS))
        def _(step=step):
            dn_copy(step).wait_send()

    for zz in range(LAYERS):
        y_copy(zz).wait_send()
        for yy in range(PAIR):
            core_copy(zz, yy).wait_send()

    def drain_blade(b, carry):
        for h in range(PASSES):
            sum_copy(h, b).wait_send()
            swap_copy(h, b).wait_send()
        return carry

    lax.fori_loop(0, per_chip, drain_blade, 0)

    def drain_chunk(p, carry):
        @pl.when(is_mid)
        def _():
            own_copy(p).wait_send()
            pass_copy(p).wait_send()
            comb_copy(p).wait_send()

        @pl.when(is_end)
        def _():
            end_copy(p).wait_send()

        harm_copy(p).wait_send()
        return carry

    lax.fori_loop(0, n_chunks, drain_chunk, 0)

    def drain_out(r, carry):
        out_copy(r).wait()
        return carry

    lax.fori_loop(0, per_pass, drain_out, 0)


def line_body(panel, stiffness, block_rows, block_cols):
    per_chip, n_blocks, bs, _ = stiffness.shape
    modes = panel.shape[-1]
    shards = LAYERS * PAIR * 2
    per_shard = panel.shape[0] // bs
    n_all = shards * per_shard
    half = modes // 2
    width = half // PASSES
    per_pass = half // CHUNK
    n_chunks = per_pass * PASSES
    count = LAYERS * PAIR * per_chip
    n_harm = 2 * per_chip
    wmid, wend = dft_tables(per_chip)
    bf16, f32 = jnp.bfloat16, jnp.float32
    dma = pltpu.SemaphoreType.DMA
    vmem = pl.BlockSpec(memory_space=pltpu.VMEM)
    smem = pl.BlockSpec(memory_space=pltpu.SMEM)
    hbm = pl.BlockSpec(memory_space=pl.ANY)
    result = pl.pallas_call(
        kernel,
        out_shape=jax.ShapeDtypeStruct((n_harm, half, modes), f32),
        in_specs=[vmem, hbm, smem, smem, hbm, hbm],
        out_specs=hbm,
        scratch_shapes=[
            pltpu.VMEM((n_all, bs, modes), bf16),
            pltpu.VMEM((n_all, modes, bs), bf16),
            pltpu.VMEM(stiffness.shape, bf16),
            pltpu.VMEM((PASSES, per_chip, modes, PAIR * width), f32),
            pltpu.VMEM((PASSES, per_chip, half, PAIR * width), f32),
            pltpu.VMEM((n_chunks, count, CHUNK, width), bf16),
            pltpu.VMEM((PASSES, per_chip, per_pass, CHUNK, width), bf16),
            pltpu.VMEM(wmid.shape[1:], bf16),
            pltpu.VMEM(wend.shape[1:], bf16),
            pltpu.VMEM((n_chunks, 2 * n_harm, CHUNK, width), bf16),
            pltpu.VMEM((n_chunks, 2 * n_harm, CHUNK, width), bf16),
            pltpu.VMEM((n_chunks, n_harm, CHUNK, width), bf16),
            pltpu.VMEM((n_chunks, n_harm, CHUNK, width), bf16),
            pltpu.VMEM((n_harm, half, modes), f32),
            dma((3,)),
            dma((LAYERS - 1,)), dma((LAYERS - 1,)),
            dma((LAYERS - 1,)), dma((LAYERS - 1,)),
            dma((LAYERS,)), dma((LAYERS,)),
            dma((LAYERS * PAIR,)), dma((LAYERS * PAIR,)),
            dma((PASSES, per_chip)), dma((PASSES, per_chip)),
            dma((PASSES, per_chip)), dma((PASSES, per_chip)),
            dma((4, n_chunks)), dma((4, n_chunks)),
            dma((n_chunks,)), dma((n_chunks,)),
            dma((per_pass,)),
        ],
        compiler_params=pltpu.CompilerParams(
            collective_id=0, has_side_effects=True, vmem_limit_bytes=VMEM_BYTES
        ),
    )(
        panel.reshape(per_shard, bs, modes),
        stiffness,
        block_rows,
        block_cols,
        jnp.asarray(wmid),
        jnp.asarray(wend),
    )
    return result.reshape(2, per_chip, half, modes)


def body(panel, stiffness, block_rows, block_cols):
    block_size = stiffness.shape[-1]
    modes = panel.shape[-1]
    whole = lax.all_gather(panel, ("blade", "dof"), axis=0, tiled=True)
    blocks = whole.reshape(-1, block_size, modes)

    def one_blade(items):
        mats, rows, cols = items
        chosen = jnp.take(blocks, cols, axis=0)
        image = jnp.einsum("nij,njm->nim", mats, chosen, preferred_element_type=jnp.float32)
        image = image.astype(jnp.bfloat16)
        left = jnp.take(blocks, rows, axis=0).reshape(-1, modes)
        return lax.dot_general(
            left,
            image.reshape(-1, modes),
            (((0,), (0,)), ((), ())),
            preferred_element_type=jnp.float32,
        )

    partial_proj = lax.map(one_blade, (stiffness, block_rows, block_cols))
    half = lax.psum_scatter(partial_proj, "dof", scatter_dimension=1, tiled=True)
    half = half.astype(jnp.bfloat16)
    blade_count = stiffness.shape[0] * lax.axis_size("blade")
    index = jnp.arange(blade_count, dtype=jnp.int32)
    angle = (index[:, None] * index[None, :] % blade_count).astype(jnp.float32) * (
        2.0 * math.pi / blade_count
    )
    table = jnp.stack([jnp.cos(angle), -jnp.sin(angle)])
    stacked = lax.all_to_all(half, "blade", split_axis=1, concat_axis=0, tiled=True)
    joined = jnp.einsum(
        "phb,brc->phrc", table, stacked.astype(jnp.float32), precision=lax.Precision.HIGHEST
    ).astype(jnp.bfloat16)
    full_spec = lax.all_to_all(joined, "blade", split_axis=1, concat_axis=2, tiled=True)
    return full_spec.astype(jnp.float32)


def solution(mesh):
    placed = (
        P(("grp", "blade", "dof"), None),
        P(("grp", "blade"), "dof", None, None),
        P(("grp", "blade"), "dof"),
        P(("grp", "blade"), "dof"),
    )
    chips = mesh.shape["blade"]
    return jax.shard_map(
        line_body if chips == LAYERS * PAIR else body,
        mesh=mesh,
        in_specs=placed,
        out_specs=P(None, ("grp", "blade"), "dof", None),
        check_vma=False,
    )
```

```python
import math

import jax
import jax.numpy as jnp
import numpy as np
from jax import lax
from jax.experimental import pallas as pl
from jax.experimental.pallas import tpu as pltpu
from jax.sharding import PartitionSpec as P

MESH = pl.DeviceIdType.MESH
LAYERS = 4
PAIR = 2
BLOCK_GROUP = 32
CHUNK = 32
AHEAD = 5
PASS_AHEAD = 3
SUB = 16
VMEM_BYTES = 60 * 1024 * 1024
PASSES = 2


def dft_tables(per_chip):
    per_layer = PAIR * per_chip
    count = LAYERS * per_layer
    index = np.arange(count)
    angle = (index[:, None] * index[None, :] % count) * (2.0 * math.pi / count)
    full = np.stack([np.cos(angle), -np.sin(angle)])

    def rows_for(layer):
        part = full[:, layer * per_layer : (layer + 1) * per_layer]
        part = part.reshape(2, PAIR, per_chip, count).transpose(1, 0, 2, 3)
        return part.reshape(2 * per_layer, count)

    def split(weights):
        wide = np.kron(weights, np.eye(SUB)).astype(np.float32)
        high = wide.astype(jnp.bfloat16)
        low = (wide - high.astype(np.float32)).astype(jnp.bfloat16)
        return np.stack([high, low])

    middle, ends = [], []
    for layer, near in ((1, 0), (2, 3)):
        partial = rows_for(near).copy()
        partial[:, near * per_layer : (near + 1) * per_layer] = 0.0
        middle.append(split(np.concatenate([rows_for(layer), partial])))
        own = rows_for(near)[:, near * per_layer : (near + 1) * per_layer]
        ends.append(split(own))
    return np.stack(middle), np.stack(ends)


def kernel(
    panel_ref, stiff_hbm, rows_ref, cols_ref, wmid_hbm, wend_hbm, out_hbm,
    pan, pan_t, stiff, acc, core_in, raw, y_out, wmid, wend,
    comb_out, comb_in, harm_out, harm_in, out_v,
    load_sem, up_send, up_recv, dn_send, dn_recv, ys_send, ys_recv, co_send, co_recv,
    sum_send, sum_recv, sw_send, sw_recv, z_send, z_recv, h_send, h_recv, out_sem,
):
    blade = lax.axis_index("blade")
    d = lax.axis_index("dof")
    z = blade // PAIR
    y = blade % PAIR
    other_y = z * PAIR + (1 - y)
    per_chip, n_blocks = stiff.shape[0], stiff.shape[1]
    per_layer = per_chip * PAIR
    rows_half = core_in.shape[2]
    n_chunks = raw.shape[0]
    per_pass = n_chunks // PASSES
    width = raw.shape[3]
    half_cols = width * PASSES
    per_shard = panel_ref.shape[0]

    def to(src, dst, send, recv, **device):
        return pltpu.make_async_remote_copy(
            src_ref=src, dst_ref=dst, send_sem=send, recv_sem=recv,
            device_id=device, device_id_type=MESH,
        )

    core = dict(dof=1 - d)
    across = dict(blade=other_y)
    up = dict(blade=jnp.minimum(blade + PAIR, LAYERS * PAIR - 1))
    down = dict(blade=jnp.maximum(blade - PAIR, 0))
    has_up = z < LAYERS - 1
    has_dn = z > 0
    is_mid = jnp.logical_and(has_up, has_dn)
    is_end = jnp.logical_not(is_mid)
    which = z // 2

    load = pltpu.make_async_copy(stiff_hbm, stiff, load_sem.at[0])
    load.start()
    load_mid = pltpu.make_async_copy(wmid_hbm.at[which], wmid, load_sem.at[1])
    load_mid.start()
    load_end = pltpu.make_async_copy(wend_hbm.at[which], wend, load_sem.at[2])
    load_end.start()

    barrier = pltpu.get_barrier_semaphore()
    pl.semaphore_signal(barrier, inc=1, device_id=core, device_id_type=MESH)
    pl.semaphore_signal(barrier, inc=1, device_id=across, device_id_type=MESH)

    @pl.when(has_up)
    def _():
        pl.semaphore_signal(barrier, inc=1, device_id=up, device_id_type=MESH)

    @pl.when(has_dn)
    def _():
        pl.semaphore_signal(barrier, inc=1, device_id=down, device_id_type=MESH)

    pl.semaphore_wait(barrier, 2 + has_up.astype(jnp.int32) + has_dn.astype(jnp.int32))

    def shard(zz, yy, dd):
        start = ((zz * PAIR + yy) * 2 + dd) * per_shard
        return pan.at[pl.ds(start, per_shard)]

    def flip(zz, yy, dd):
        start = ((zz * PAIR + yy) * 2 + dd) * per_shard
        for i in range(per_shard):
            pan_t[start + i] = pan[start + i].T

    def up_copy(step):
        s = shard(jnp.maximum(z - step, 0), y, d)
        return to(s, s, up_send.at[step], up_recv.at[step], **up)

    def dn_copy(step):
        s = shard(jnp.minimum(z + step, LAYERS - 1), y, d)
        return to(s, s, dn_send.at[step], dn_recv.at[step], **down)

    def up_arrival(step):
        s = shard(jnp.maximum(z - step, 0), y, d)
        return to(s, s, up_send.at[step - 1], up_recv.at[step - 1], **up)

    def dn_arrival(step):
        s = shard(jnp.minimum(z + step, LAYERS - 1), y, d)
        return to(s, s, dn_send.at[step - 1], dn_recv.at[step - 1], **down)

    def y_copy(zz):
        s = shard(zz, y, d)
        return to(s, s, ys_send.at[zz], ys_recv.at[zz], **across)

    def y_arrival(zz):
        s = shard(zz, 1 - y, d)
        return to(s, s, ys_send.at[zz], ys_recv.at[zz], **across)

    def core_copy(zz, yy):
        s = shard(zz, yy, d)
        return to(s, s, co_send.at[zz * PAIR + yy], co_recv.at[zz * PAIR + yy], **core)

    def core_arrival(zz, yy):
        s = shard(zz, yy, 1 - d)
        return to(s, s, co_send.at[zz * PAIR + yy], co_recv.at[zz * PAIR + yy], **core)

    mine = ((z * PAIR + y) * 2 + d) * per_shard
    pan[pl.ds(mine, per_shard)] = panel_ref[...]

    @pl.when(has_up)
    def _():
        up_copy(0).start()

    @pl.when(has_dn)
    def _():
        dn_copy(0).start()

    y_copy(z).start()
    core_copy(z, y).start()
    flip(z, y, d)

    def take_y(zz):
        y_arrival(zz).wait_recv()
        core_copy(zz, 1 - y).start()
        flip(zz, 1 - y, d)

    def take_core(zz, yy):
        core_arrival(zz, yy).wait_recv()
        flip(zz, yy, 1 - d)

    def at_distance(step, do):
        if step == 0:
            do(z)
            return

        @pl.when(z >= step)
        def _():
            do(z - step)

        @pl.when(z + step < LAYERS)
        def _():
            do(z + step)

    for step in range(1, LAYERS):

        @pl.when(z >= step)
        def _(step=step):
            up_arrival(step).wait_recv()
            if step < LAYERS - 1:

                @pl.when(has_up)
                def _():
                    up_copy(step).start()

            y_copy(z - step).start()
            core_copy(z - step, y).start()

        @pl.when(z + step < LAYERS)
        def _(step=step):
            dn_arrival(step).wait_recv()
            if step < LAYERS - 1:

                @pl.when(has_dn)
                def _():
                    dn_copy(step).start()

            y_copy(z + step).start()
            core_copy(z + step, y).start()

        at_distance(step, lambda zz: flip(zz, y, d))
        at_distance(step - 1, take_y)
        at_distance(step - 1, lambda zz: take_core(zz, y))
        if step > 1:
            at_distance(step - 2, lambda zz: take_core(zz, 1 - y))

    at_distance(LAYERS - 1, take_y)
    at_distance(LAYERS - 1, lambda zz: take_core(zz, y))
    at_distance(LAYERS - 2, lambda zz: take_core(zz, 1 - y))
    at_distance(LAYERS - 1, lambda zz: take_core(zz, 1 - y))
    load.wait()

    def sum_copy(h, b):
        src = acc.at[h, b, pl.ds(pl.multiple_of((1 - d) * rows_half, rows_half), rows_half)]
        return to(src, core_in.at[h, b], sum_send.at[h, b], sum_recv.at[h, b], **core)

    def slot(yy, b):
        return z * per_layer + yy * per_chip + b

    def swap_copy(h, b):
        dst = raw.at[pl.ds(h * per_pass, per_pass), slot(y, b)]
        return to(y_out.at[h, b], dst, sw_send.at[h, b], sw_recv.at[h, b], **across)

    def swap_arrival(h, b):
        dst = raw.at[pl.ds(h * per_pass, per_pass), slot(1 - y, b)]
        return to(y_out.at[h, b], dst, sw_send.at[h, b], sw_recv.at[h, b], **across)

    own_rows = pl.ds(pl.multiple_of(d * rows_half, rows_half), rows_half)

    def summed(h, b, yy):
        cols = pl.ds(pl.multiple_of(yy * width, width), width)
        total = acc[h, b, own_rows, cols] + core_in[h, b, :, cols]
        return total.astype(jnp.bfloat16).reshape(per_pass, CHUNK, width)

    def finish(h, b):
        sum_copy(h, b).wait_recv()
        y_out[h, b] = summed(h, b, 1 - y)
        swap_copy(h, b).start()
        raw[pl.ds(h * per_pass, per_pass), slot(y, b)] = summed(h, b, y)

    def one_blade(h, b):
        def group(q):
            left, image = [], []
            for i in range(BLOCK_GROUP):
                n = q * BLOCK_GROUP + i
                c = cols_ref[b, n]
                if PASSES == 1:
                    right = pan[c]
                else:
                    right = jnp.concatenate(
                        [pan[c, :, pl.ds(yy * half_cols + h * width, width)] for yy in range(PAIR)],
                        axis=1,
                    )
                product = jnp.dot(stiff[b, n], right, preferred_element_type=jnp.float32)
                image.append(product.astype(jnp.bfloat16))
                left.append(pan_t[rows_ref[b, n]])
            return jnp.dot(
                jnp.concatenate(left, axis=1),
                jnp.concatenate(image, axis=0),
                preferred_element_type=jnp.float32,
            )

        acc[h, b] = group(0)
        if n_blocks > BLOCK_GROUP:

            def more(q, carry):
                acc[h, b] += group(q)
                return carry

            lax.fori_loop(1, n_blocks // BLOCK_GROUP, more, 0)

        sum_copy(h, b).start()

        @pl.when(b > 0)
        def _():
            finish(h, b - 1)

    def end_pass(h):
        finish(h, per_chip - 1)

        def take_swap(b, carry):
            swap_arrival(h, b).wait_recv()
            return carry

        lax.fori_loop(0, per_chip, take_swap, 0)

    def first_pass(b, carry):
        one_blade(0, b)
        return carry

    lax.fori_loop(0, per_chip, first_pass, 0)
    end_pass(0)

    n_harm = 2 * per_chip
    near = jnp.where(z < 2, 0, LAYERS - 1)
    far = LAYERS - 1 - z
    near_dev = dict(blade=near * PAIR + y)
    far_dev = dict(blade=far * PAIR + y)
    mid_dev = dict(blade=jnp.where(z < 2, 1, LAYERS - 2) * PAIR + y)

    def planes(p, zz):
        return raw.at[p, pl.ds(zz * per_layer, per_layer)]

    def end_copy(p):
        s = planes(p, near)
        return to(s, s, z_send.at[0, p], z_recv.at[0, p], **mid_dev)

    def own_copy(p):
        s = planes(p, z)
        return to(s, s, z_send.at[1, p], z_recv.at[1, p], **far_dev)

    def own_arrival(p):
        s = planes(p, far)
        return to(s, s, z_send.at[1, p], z_recv.at[1, p], **far_dev)

    def pass_copy(p):
        s = planes(p, near)
        return to(s, s, z_send.at[2, p], z_recv.at[2, p], **far_dev)

    def pass_arrival(p):
        s = planes(p, LAYERS - 1 - near)
        return to(s, s, z_send.at[2, p], z_recv.at[2, p], **far_dev)

    def comb_copy(p):
        return to(comb_out.at[p], comb_in.at[p], z_send.at[3, p], z_recv.at[3, p], **near_dev)

    def harm_copy(p):
        return to(harm_out.at[p], harm_in.at[p], h_send.at[p], h_recv.at[p], **across)

    def transform(weights, x):
        x = jnp.concatenate(
            [x[:, i : i + SUB].reshape(-1, width) for i in range(0, CHUNK, SUB)], axis=1
        )
        got = jnp.dot(weights[0], x, preferred_element_type=jnp.float32)
        got = got + jnp.dot(weights[1], x, preferred_element_type=jnp.float32)
        return [
            got[:, i * width : (i + 1) * width].reshape(-1, SUB, width)
            for i in range(CHUNK // SUB)
        ]

    def columns(p, yy):
        return pl.ds(pl.multiple_of(yy * half_cols + p // per_pass * width, width), width)

    def out_copy(r):
        rows = pl.ds(pl.multiple_of(r * CHUNK, CHUNK), CHUNK)
        return pltpu.make_async_copy(out_v.at[:, rows], out_hbm.at[:, rows], out_sem.at[r])

    def store_final(p, sub, final):
        row = lax.rem(p, per_pass) * CHUNK + sub * SUB
        first, second = final[:n_harm], final[n_harm:]
        out_v[:, pl.ds(pl.multiple_of(row, SUB), SUB), columns(p, y)] = jnp.where(
            y == 0, first, second
        )
        theirs = jnp.where(y == 0, second, first)
        harm_out[p, :, pl.ds(sub * SUB, SUB)] = theirs.astype(jnp.bfloat16)

    def take_harm(p):
        harm_copy(p).wait_recv()
        row = lax.rem(p, per_pass) * CHUNK
        out_v[:, pl.ds(pl.multiple_of(row, CHUNK), CHUNK), columns(p, 1 - y)] = harm_in[
            p
        ].astype(jnp.float32)

        @pl.when(p >= n_chunks - per_pass)
        def _():
            out_copy(p - (n_chunks - per_pass)).start()

    @pl.when(is_mid)
    def _():
        own_copy(0).start()
        for p in range(1, AHEAD):
            own_copy(p).start()
            if p <= PASS_AHEAD:
                end_copy(p - 1).wait_recv()
                pass_copy(p - 1).start()

    @pl.when(is_end)
    def _():
        for p in range(AHEAD):
            end_copy(p).start()

    load_mid.wait()
    load_end.wait()

    def step(p, carry):
        if PASSES > 1:

            @pl.when(p < per_chip // 2)
            def _():
                def second_pass(b, carry):
                    one_blade(1, 2 * p + b)
                    return carry

                lax.fori_loop(0, 2, second_pass, 0)

            @pl.when(p == per_chip // 2)
            def _():
                end_pass(1)

        @pl.when(is_mid)
        def _():
            @pl.when(p + AHEAD < n_chunks)
            def _():
                own_copy(p + AHEAD).start()

            @pl.when(p + PASS_AHEAD < n_chunks)
            def _():
                end_copy(p + PASS_AHEAD).wait_recv()
                pass_copy(p + PASS_AHEAD).start()

            own_arrival(p).wait_recv()
            pass_arrival(p).wait_recv()
            for sub, got in enumerate(transform(wmid, raw[p])):
                comb_out[p, :, pl.ds(sub * SUB, SUB)] = got[2 * n_harm :].astype(jnp.bfloat16)
                store_final(p, sub, got[: 2 * n_harm])
            comb_copy(p).start()

        @pl.when(is_end)
        def _():
            @pl.when(p + AHEAD < n_chunks)
            def _():
                end_copy(p + AHEAD).start()

            comb_copy(p).wait_recv()
            own = raw[p, pl.ds(z * per_layer, per_layer)]
            for sub, got in enumerate(transform(wend, own)):
                rows = pl.ds(sub * SUB, SUB)
                store_final(p, sub, got + comb_in[p, :, rows].astype(jnp.float32))

        harm_copy(p).start()

        @pl.when(p > 0)
        def _():
            take_harm(p - 1)

        return carry

    lax.fori_loop(0, n_chunks, step, 0)
    take_harm(n_chunks - 1)

    for step in range(LAYERS - 1):

        @pl.when(jnp.logical_and(has_up, z >= step))
        def _(step=step):
            up_copy(step).wait_send()

        @pl.when(jnp.logical_and(has_dn, z + step < LAYERS))
        def _(step=step):
            dn_copy(step).wait_send()

    for zz in range(LAYERS):
        y_copy(zz).wait_send()
        for yy in range(PAIR):
            core_copy(zz, yy).wait_send()

    def drain_blade(b, carry):
        for h in range(PASSES):
            sum_copy(h, b).wait_send()
            swap_copy(h, b).wait_send()
        return carry

    lax.fori_loop(0, per_chip, drain_blade, 0)

    def drain_chunk(p, carry):
        @pl.when(is_mid)
        def _():
            own_copy(p).wait_send()
            pass_copy(p).wait_send()
            comb_copy(p).wait_send()

        @pl.when(is_end)
        def _():
            end_copy(p).wait_send()

        harm_copy(p).wait_send()
        return carry

    lax.fori_loop(0, n_chunks, drain_chunk, 0)

    def drain_out(r, carry):
        out_copy(r).wait()
        return carry

    lax.fori_loop(0, per_pass, drain_out, 0)


def line_body(panel, stiffness, block_rows, block_cols):
    per_chip, n_blocks, bs, _ = stiffness.shape
    modes = panel.shape[-1]
    shards = LAYERS * PAIR * 2
    per_shard = panel.shape[0] // bs
    n_all = shards * per_shard
    half = modes // 2
    width = half // PASSES
    per_pass = half // CHUNK
    n_chunks = per_pass * PASSES
    count = LAYERS * PAIR * per_chip
    n_harm = 2 * per_chip
    wmid, wend = dft_tables(per_chip)
    bf16, f32 = jnp.bfloat16, jnp.float32
    dma = pltpu.SemaphoreType.DMA
    vmem = pl.BlockSpec(memory_space=pltpu.VMEM)
    smem = pl.BlockSpec(memory_space=pltpu.SMEM)
    hbm = pl.BlockSpec(memory_space=pl.ANY)
    result = pl.pallas_call(
        kernel,
        out_shape=jax.ShapeDtypeStruct((n_harm, half, modes), f32),
        in_specs=[vmem, hbm, smem, smem, hbm, hbm],
        out_specs=hbm,
        scratch_shapes=[
            pltpu.VMEM((n_all, bs, modes), bf16),
            pltpu.VMEM((n_all, modes, bs), bf16),
            pltpu.VMEM(stiffness.shape, bf16),
            pltpu.VMEM((PASSES, per_chip, modes, PAIR * width), f32),
            pltpu.VMEM((PASSES, per_chip, half, PAIR * width), f32),
            pltpu.VMEM((n_chunks, count, CHUNK, width), bf16),
            pltpu.VMEM((PASSES, per_chip, per_pass, CHUNK, width), bf16),
            pltpu.VMEM(wmid.shape[1:], bf16),
            pltpu.VMEM(wend.shape[1:], bf16),
            pltpu.VMEM((n_chunks, 2 * n_harm, CHUNK, width), bf16),
            pltpu.VMEM((n_chunks, 2 * n_harm, CHUNK, width), bf16),
            pltpu.VMEM((n_chunks, n_harm, CHUNK, width), bf16),
            pltpu.VMEM((n_chunks, n_harm, CHUNK, width), bf16),
            pltpu.VMEM((n_harm, half, modes), f32),
            dma((3,)),
            dma((LAYERS - 1,)), dma((LAYERS - 1,)),
            dma((LAYERS - 1,)), dma((LAYERS - 1,)),
            dma((LAYERS,)), dma((LAYERS,)),
            dma((LAYERS * PAIR,)), dma((LAYERS * PAIR,)),
            dma((PASSES, per_chip)), dma((PASSES, per_chip)),
            dma((PASSES, per_chip)), dma((PASSES, per_chip)),
            dma((4, n_chunks)), dma((4, n_chunks)),
            dma((n_chunks,)), dma((n_chunks,)),
            dma((per_pass,)),
        ],
        compiler_params=pltpu.CompilerParams(
            collective_id=0, has_side_effects=True, vmem_limit_bytes=VMEM_BYTES
        ),
    )(
        panel.reshape(per_shard, bs, modes),
        stiffness,
        block_rows,
        block_cols,
        jnp.asarray(wmid),
        jnp.asarray(wend),
    )
    return result.reshape(2, per_chip, half, modes)


def body(panel, stiffness, block_rows, block_cols):
    block_size = stiffness.shape[-1]
    modes = panel.shape[-1]
    whole = lax.all_gather(panel, ("blade", "dof"), axis=0, tiled=True)
    blocks = whole.reshape(-1, block_size, modes)

    def one_blade(items):
        mats, rows, cols = items
        chosen = jnp.take(blocks, cols, axis=0)
        image = jnp.einsum("nij,njm->nim", mats, chosen, preferred_element_type=jnp.float32)
        image = image.astype(jnp.bfloat16)
        left = jnp.take(blocks, rows, axis=0).reshape(-1, modes)
        return lax.dot_general(
            left,
            image.reshape(-1, modes),
            (((0,), (0,)), ((), ())),
            preferred_element_type=jnp.float32,
        )

    partial_proj = lax.map(one_blade, (stiffness, block_rows, block_cols))
    half = lax.psum_scatter(partial_proj, "dof", scatter_dimension=1, tiled=True)
    half = half.astype(jnp.bfloat16)
    blade_count = stiffness.shape[0] * lax.axis_size("blade")
    index = jnp.arange(blade_count, dtype=jnp.int32)
    angle = (index[:, None] * index[None, :] % blade_count).astype(jnp.float32) * (
        2.0 * math.pi / blade_count
    )
    table = jnp.stack([jnp.cos(angle), -jnp.sin(angle)])
    stacked = lax.all_to_all(half, "blade", split_axis=1, concat_axis=0, tiled=True)
    joined = jnp.einsum(
        "phb,brc->phrc", table, stacked.astype(jnp.float32), precision=lax.Precision.HIGHEST
    ).astype(jnp.bfloat16)
    full_spec = lax.all_to_all(joined, "blade", split_axis=1, concat_axis=2, tiled=True)
    return full_spec.astype(jnp.float32)


def solution(mesh):
    placed = (
        P(("grp", "blade", "dof"), None),
        P(("grp", "blade"), "dof", None, None),
        P(("grp", "blade"), "dof"),
        P(("grp", "blade"), "dof"),
    )
    chips = mesh.shape["blade"]
    return jax.shard_map(
        line_body if chips == LAYERS * PAIR else body,
        mesh=mesh,
        in_specs=placed,
        out_specs=P(None, ("grp", "blade"), "dof", None),
        check_vma=False,
    )
```

```python
import math

import jax
import jax.numpy as jnp
import numpy as np
from jax import lax
from jax.experimental import pallas as pl
from jax.experimental.pallas import tpu as pltpu
from jax.sharding import PartitionSpec as P

MESH = pl.DeviceIdType.MESH
LAYERS = 4
PAIR = 2
BLOCK_GROUP = 32
CHUNK = 32
AHEAD = 5
PASS_AHEAD = 3
SUB = 16
VMEM_BYTES = 60 * 1024 * 1024
PASSES = 2


def dft_tables(per_chip):
    per_layer = PAIR * per_chip
    count = LAYERS * per_layer
    index = np.arange(count)
    angle = (index[:, None] * index[None, :] % count) * (2.0 * math.pi / count)
    full = np.stack([np.cos(angle), -np.sin(angle)])

    def rows_for(layer):
        part = full[:, layer * per_layer : (layer + 1) * per_layer]
        part = part.reshape(2, PAIR, per_chip, count).transpose(1, 0, 2, 3)
        return part.reshape(2 * per_layer, count)

    def split(weights):
        wide = np.kron(weights, np.eye(SUB)).astype(np.float32)
        high = wide.astype(jnp.bfloat16)
        low = (wide - high.astype(np.float32)).astype(jnp.bfloat16)
        return np.stack([high, low])

    middle, ends = [], []
    for layer, near in ((1, 0), (2, 3)):
        partial = rows_for(near).copy()
        partial[:, near * per_layer : (near + 1) * per_layer] = 0.0
        middle.append(split(np.concatenate([rows_for(layer), partial])))
        own = rows_for(near)[:, near * per_layer : (near + 1) * per_layer]
        ends.append(split(own))
    return np.stack(middle), np.stack(ends)


def kernel(
    panel_ref, stiff_hbm, rows_ref, cols_ref, wmid_hbm, wend_hbm, out_hbm,
    pan, pan_t, stiff, acc, core_in, raw, y_out, wmid, wend,
    comb_out, comb_in, harm_out, harm_in, out_v,
    load_sem, up_send, up_recv, dn_send, dn_recv, ys_send, ys_recv, co_send, co_recv,
    sum_send, sum_recv, sw_send, sw_recv, z_send, z_recv, h_send, h_recv, out_sem,
):
    blade = lax.axis_index("blade")
    d = lax.axis_index("dof")
    z = blade // PAIR
    y = blade % PAIR
    other_y = z * PAIR + (1 - y)
    per_chip, n_blocks = stiff.shape[0], stiff.shape[1]
    per_layer = per_chip * PAIR
    rows_half = core_in.shape[2]
    n_chunks = raw.shape[0]
    per_pass = n_chunks // PASSES
    width = raw.shape[3]
    half_cols = width * PASSES
    per_shard = panel_ref.shape[0]

    def to(src, dst, send, recv, **device):
        return pltpu.make_async_remote_copy(
            src_ref=src, dst_ref=dst, send_sem=send, recv_sem=recv,
            device_id=device, device_id_type=MESH,
        )

    core = dict(dof=1 - d)
    across = dict(blade=other_y)
    up = dict(blade=jnp.minimum(blade + PAIR, LAYERS * PAIR - 1))
    down = dict(blade=jnp.maximum(blade - PAIR, 0))
    has_up = z < LAYERS - 1
    has_dn = z > 0
    is_mid = jnp.logical_and(has_up, has_dn)
    is_end = jnp.logical_not(is_mid)
    which = z // 2

    load = pltpu.make_async_copy(stiff_hbm, stiff, load_sem.at[0])
    load.start()
    load_mid = pltpu.make_async_copy(wmid_hbm.at[which], wmid, load_sem.at[1])
    load_mid.start()
    load_end = pltpu.make_async_copy(wend_hbm.at[which], wend, load_sem.at[2])
    load_end.start()

    barrier = pltpu.get_barrier_semaphore()
    pl.semaphore_signal(barrier, inc=1, device_id=core, device_id_type=MESH)
    pl.semaphore_signal(barrier, inc=1, device_id=across, device_id_type=MESH)

    @pl.when(has_up)
    def _():
        pl.semaphore_signal(barrier, inc=1, device_id=up, device_id_type=MESH)

    @pl.when(has_dn)
    def _():
        pl.semaphore_signal(barrier, inc=1, device_id=down, device_id_type=MESH)

    pl.semaphore_wait(barrier, 2 + has_up.astype(jnp.int32) + has_dn.astype(jnp.int32))

    def place(zz, yy, dd, k):
        return ((zz * PAIR + yy) * 2 + dd) * per_shard + k

    def shard(zz, yy, dd, k):
        return pan.at[pl.ds(place(zz, yy, dd, k), 1)]

    def flip(zz, yy, dd, k):
        n = place(zz, yy, dd, k)
        pan_t[n] = pan[n].T

    def up_copy(step, k):
        s = shard(jnp.maximum(z - step, 0), y, d, k)
        return to(s, s, up_send.at[step, k], up_recv.at[step, k], **up)

    def dn_copy(step, k):
        s = shard(jnp.minimum(z + step, LAYERS - 1), y, d, k)
        return to(s, s, dn_send.at[step, k], dn_recv.at[step, k], **down)

    def up_arrival(step, k):
        s = shard(jnp.maximum(z - step, 0), y, d, k)
        return to(s, s, up_send.at[step - 1, k], up_recv.at[step - 1, k], **up)

    def dn_arrival(step, k):
        s = shard(jnp.minimum(z + step, LAYERS - 1), y, d, k)
        return to(s, s, dn_send.at[step - 1, k], dn_recv.at[step - 1, k], **down)

    def y_copy(zz, k):
        s = shard(zz, y, d, k)
        return to(s, s, ys_send.at[zz, k], ys_recv.at[zz, k], **across)

    def y_arrival(zz, k):
        s = shard(zz, 1 - y, d, k)
        return to(s, s, ys_send.at[zz, k], ys_recv.at[zz, k], **across)

    def core_copy(zz, yy, k):
        s = shard(zz, yy, d, k)
        i = zz * PAIR + yy
        return to(s, s, co_send.at[i, k], co_recv.at[i, k], **core)

    def core_arrival(zz, yy, k):
        s = shard(zz, yy, 1 - d, k)
        i = zz * PAIR + yy
        return to(s, s, co_send.at[i, k], co_recv.at[i, k], **core)

    for k in range(per_shard):
        pan[place(z, y, d, k)] = panel_ref[k]

        @pl.when(has_up)
        def _(k=k):
            up_copy(0, k).start()

        @pl.when(has_dn)
        def _(k=k):
            dn_copy(0, k).start()

        y_copy(z, k).start()
        core_copy(z, y, k).start()

    for k in range(per_shard):
        flip(z, y, d, k)

    def take_y(zz, k):
        y_arrival(zz, k).wait_recv()
        core_copy(zz, 1 - y, k).start()
        flip(zz, 1 - y, d, k)

    def take_core(zz, yy, k):
        core_arrival(zz, yy, k).wait_recv()
        flip(zz, yy, 1 - d, k)

    def at_distance(step, do):
        if step == 0:
            do(z)
            return

        @pl.when(z >= step)
        def _():
            do(z - step)

        @pl.when(z + step < LAYERS)
        def _():
            do(z + step)

    for step in range(1, LAYERS):
        for k in range(per_shard):

            @pl.when(z >= step)
            def _(step=step, k=k):
                up_arrival(step, k).wait_recv()
                if step < LAYERS - 1:

                    @pl.when(has_up)
                    def _():
                        up_copy(step, k).start()

                y_copy(z - step, k).start()
                core_copy(z - step, y, k).start()

            @pl.when(z + step < LAYERS)
            def _(step=step, k=k):
                dn_arrival(step, k).wait_recv()
                if step < LAYERS - 1:

                    @pl.when(has_dn)
                    def _():
                        dn_copy(step, k).start()

                y_copy(z + step, k).start()
                core_copy(z + step, y, k).start()

            at_distance(step, lambda zz: flip(zz, y, d, k))
            at_distance(step - 1, lambda zz: take_y(zz, k))
            at_distance(step - 1, lambda zz: take_core(zz, y, k))
            if step > 1:
                at_distance(step - 2, lambda zz: take_core(zz, 1 - y, k))

    for k in range(per_shard):
        at_distance(LAYERS - 2, lambda zz: take_core(zz, 1 - y, k))
        at_distance(LAYERS - 1, lambda zz: take_core(zz, y, k))
        at_distance(LAYERS - 1, lambda zz: take_y(zz, k))
    for k in range(per_shard):
        at_distance(LAYERS - 1, lambda zz: take_core(zz, 1 - y, k))
    load.wait()

    def sum_copy(h, b):
        src = acc.at[h, b, pl.ds(pl.multiple_of((1 - d) * rows_half, rows_half), rows_half)]
        return to(src, core_in.at[h, b], sum_send.at[h, b], sum_recv.at[h, b], **core)

    def slot(yy, b):
        return z * per_layer + yy * per_chip + b

    def swap_copy(h, b):
        dst = raw.at[pl.ds(h * per_pass, per_pass), slot(y, b)]
        return to(y_out.at[h, b], dst, sw_send.at[h, b], sw_recv.at[h, b], **across)

    def swap_arrival(h, b):
        dst = raw.at[pl.ds(h * per_pass, per_pass), slot(1 - y, b)]
        return to(y_out.at[h, b], dst, sw_send.at[h, b], sw_recv.at[h, b], **across)

    own_rows = pl.ds(pl.multiple_of(d * rows_half, rows_half), rows_half)

    def summed(h, b, yy):
        cols = pl.ds(pl.multiple_of(yy * width, width), width)
        total = acc[h, b, own_rows, cols] + core_in[h, b, :, cols]
        return total.astype(jnp.bfloat16).reshape(per_pass, CHUNK, width)

    def finish(h, b):
        sum_copy(h, b).wait_recv()
        y_out[h, b] = summed(h, b, 1 - y)
        swap_copy(h, b).start()
        raw[pl.ds(h * per_pass, per_pass), slot(y, b)] = summed(h, b, y)

    def one_blade(h, b):
        def group(q):
            left, image = [], []
            for i in range(BLOCK_GROUP):
                n = q * BLOCK_GROUP + i
                c = cols_ref[b, n]
                if PASSES == 1:
                    right = pan[c]
                else:
                    right = jnp.concatenate(
                        [pan[c, :, pl.ds(yy * half_cols + h * width, width)] for yy in range(PAIR)],
                        axis=1,
                    )
                product = jnp.dot(stiff[b, n], right, preferred_element_type=jnp.float32)
                image.append(product.astype(jnp.bfloat16))
                left.append(pan_t[rows_ref[b, n]])
            return jnp.dot(
                jnp.concatenate(left, axis=1),
                jnp.concatenate(image, axis=0),
                preferred_element_type=jnp.float32,
            )

        acc[h, b] = group(0)
        if n_blocks > BLOCK_GROUP:

            def more(q, carry):
                acc[h, b] += group(q)
                return carry

            lax.fori_loop(1, n_blocks // BLOCK_GROUP, more, 0)

        sum_copy(h, b).start()

        @pl.when(b > 0)
        def _():
            finish(h, b - 1)

    def end_pass(h):
        finish(h, per_chip - 1)

        def take_swap(b, carry):
            swap_arrival(h, b).wait_recv()
            return carry

        lax.fori_loop(0, per_chip, take_swap, 0)

    def first_pass(b, carry):
        one_blade(0, b)
        return carry

    lax.fori_loop(0, per_chip, first_pass, 0)
    end_pass(0)

    n_harm = 2 * per_chip
    near = jnp.where(z < 2, 0, LAYERS - 1)
    far = LAYERS - 1 - z
    near_dev = dict(blade=near * PAIR + y)
    far_dev = dict(blade=far * PAIR + y)
    mid_dev = dict(blade=jnp.where(z < 2, 1, LAYERS - 2) * PAIR + y)

    def planes(p, zz):
        return raw.at[p, pl.ds(zz * per_layer, per_layer)]

    def end_copy(p):
        s = planes(p, near)
        return to(s, s, z_send.at[0, p], z_recv.at[0, p], **mid_dev)

    def own_copy(p):
        s = planes(p, z)
        return to(s, s, z_send.at[1, p], z_recv.at[1, p], **far_dev)

    def own_arrival(p):
        s = planes(p, far)
        return to(s, s, z_send.at[1, p], z_recv.at[1, p], **far_dev)

    def pass_copy(p):
        s = planes(p, near)
        return to(s, s, z_send.at[2, p], z_recv.at[2, p], **far_dev)

    def pass_arrival(p):
        s = planes(p, LAYERS - 1 - near)
        return to(s, s, z_send.at[2, p], z_recv.at[2, p], **far_dev)

    def comb_copy(p):
        return to(comb_out.at[p], comb_in.at[p], z_send.at[3, p], z_recv.at[3, p], **near_dev)

    def harm_copy(p):
        return to(harm_out.at[p], harm_in.at[p], h_send.at[p], h_recv.at[p], **across)

    def transform(weights, x):
        x = jnp.concatenate(
            [x[:, i : i + SUB].reshape(-1, width) for i in range(0, CHUNK, SUB)], axis=1
        )
        got = jnp.dot(weights[0], x, preferred_element_type=jnp.float32)
        got = got + jnp.dot(weights[1], x, preferred_element_type=jnp.float32)
        return [
            got[:, i * width : (i + 1) * width].reshape(-1, SUB, width)
            for i in range(CHUNK // SUB)
        ]

    def columns(p, yy):
        return pl.ds(pl.multiple_of(yy * half_cols + p // per_pass * width, width), width)

    def out_copy(r):
        rows = pl.ds(pl.multiple_of(r * CHUNK, CHUNK), CHUNK)
        return pltpu.make_async_copy(out_v.at[:, rows], out_hbm.at[:, rows], out_sem.at[r])

    def store_final(p, sub, final):
        row = lax.rem(p, per_pass) * CHUNK + sub * SUB
        first, second = final[:n_harm], final[n_harm:]
        out_v[:, pl.ds(pl.multiple_of(row, SUB), SUB), columns(p, y)] = jnp.where(
            y == 0, first, second
        )
        theirs = jnp.where(y == 0, second, first)
        harm_out[p, :, pl.ds(sub * SUB, SUB)] = theirs.astype(jnp.bfloat16)

    def take_harm(p):
        harm_copy(p).wait_recv()
        row = lax.rem(p, per_pass) * CHUNK
        out_v[:, pl.ds(pl.multiple_of(row, CHUNK), CHUNK), columns(p, 1 - y)] = harm_in[
            p
        ].astype(jnp.float32)

        @pl.when(p >= n_chunks - per_pass)
        def _():
            out_copy(p - (n_chunks - per_pass)).start()

    @pl.when(is_mid)
    def _():
        own_copy(0).start()
        for p in range(1, AHEAD):
            own_copy(p).start()
            if p <= PASS_AHEAD:
                end_copy(p - 1).wait_recv()
                pass_copy(p - 1).start()

    @pl.when(is_end)
    def _():
        for p in range(AHEAD):
            end_copy(p).start()

    load_mid.wait()
    load_end.wait()

    def step(p, carry):
        if PASSES > 1:

            @pl.when(p < per_chip // 2)
            def _():
                def second_pass(b, carry):
                    one_blade(1, 2 * p + b)
                    return carry

                lax.fori_loop(0, 2, second_pass, 0)

            @pl.when(p == per_chip // 2)
            def _():
                end_pass(1)

        @pl.when(is_mid)
        def _():
            @pl.when(p + AHEAD < n_chunks)
            def _():
                own_copy(p + AHEAD).start()

            @pl.when(p + PASS_AHEAD < n_chunks)
            def _():
                end_copy(p + PASS_AHEAD).wait_recv()
                pass_copy(p + PASS_AHEAD).start()

            own_arrival(p).wait_recv()
            pass_arrival(p).wait_recv()
            for sub, got in enumerate(transform(wmid, raw[p])):
                comb_out[p, :, pl.ds(sub * SUB, SUB)] = got[2 * n_harm :].astype(jnp.bfloat16)
                store_final(p, sub, got[: 2 * n_harm])
            comb_copy(p).start()

        @pl.when(is_end)
        def _():
            @pl.when(p + AHEAD < n_chunks)
            def _():
                end_copy(p + AHEAD).start()

            comb_copy(p).wait_recv()
            own = raw[p, pl.ds(z * per_layer, per_layer)]
            for sub, got in enumerate(transform(wend, own)):
                rows = pl.ds(sub * SUB, SUB)
                store_final(p, sub, got + comb_in[p, :, rows].astype(jnp.float32))

        harm_copy(p).start()

        @pl.when(p > 0)
        def _():
            take_harm(p - 1)

        return carry

    lax.fori_loop(0, n_chunks, step, 0)
    take_harm(n_chunks - 1)

    for k in range(per_shard):
        for step in range(LAYERS - 1):

            @pl.when(jnp.logical_and(has_up, z >= step))
            def _(step=step, k=k):
                up_copy(step, k).wait_send()

            @pl.when(jnp.logical_and(has_dn, z + step < LAYERS))
            def _(step=step, k=k):
                dn_copy(step, k).wait_send()

        for zz in range(LAYERS):
            y_copy(zz, k).wait_send()
            for yy in range(PAIR):
                core_copy(zz, yy, k).wait_send()

    def drain_blade(b, carry):
        for h in range(PASSES):
            sum_copy(h, b).wait_send()
            swap_copy(h, b).wait_send()
        return carry

    lax.fori_loop(0, per_chip, drain_blade, 0)

    def drain_chunk(p, carry):
        @pl.when(is_mid)
        def _():
            own_copy(p).wait_send()
            pass_copy(p).wait_send()
            comb_copy(p).wait_send()

        @pl.when(is_end)
        def _():
            end_copy(p).wait_send()

        harm_copy(p).wait_send()
        return carry

    lax.fori_loop(0, n_chunks, drain_chunk, 0)

    def drain_out(r, carry):
        out_copy(r).wait()
        return carry

    lax.fori_loop(0, per_pass, drain_out, 0)


def line_body(panel, stiffness, block_rows, block_cols):
    per_chip, n_blocks, bs, _ = stiffness.shape
    modes = panel.shape[-1]
    shards = LAYERS * PAIR * 2
    per_shard = panel.shape[0] // bs
    n_all = shards * per_shard
    half = modes // 2
    width = half // PASSES
    per_pass = half // CHUNK
    n_chunks = per_pass * PASSES
    count = LAYERS * PAIR * per_chip
    n_harm = 2 * per_chip
    wmid, wend = dft_tables(per_chip)
    bf16, f32 = jnp.bfloat16, jnp.float32
    dma = pltpu.SemaphoreType.DMA
    vmem = pl.BlockSpec(memory_space=pltpu.VMEM)
    smem = pl.BlockSpec(memory_space=pltpu.SMEM)
    hbm = pl.BlockSpec(memory_space=pl.ANY)
    result = pl.pallas_call(
        kernel,
        out_shape=jax.ShapeDtypeStruct((n_harm, half, modes), f32),
        in_specs=[vmem, hbm, smem, smem, hbm, hbm],
        out_specs=hbm,
        scratch_shapes=[
            pltpu.VMEM((n_all, bs, modes), bf16),
            pltpu.VMEM((n_all, modes, bs), bf16),
            pltpu.VMEM(stiffness.shape, bf16),
            pltpu.VMEM((PASSES, per_chip, modes, PAIR * width), f32),
            pltpu.VMEM((PASSES, per_chip, half, PAIR * width), f32),
            pltpu.VMEM((n_chunks, count, CHUNK, width), bf16),
            pltpu.VMEM((PASSES, per_chip, per_pass, CHUNK, width), bf16),
            pltpu.VMEM(wmid.shape[1:], bf16),
            pltpu.VMEM(wend.shape[1:], bf16),
            pltpu.VMEM((n_chunks, 2 * n_harm, CHUNK, width), bf16),
            pltpu.VMEM((n_chunks, 2 * n_harm, CHUNK, width), bf16),
            pltpu.VMEM((n_chunks, n_harm, CHUNK, width), bf16),
            pltpu.VMEM((n_chunks, n_harm, CHUNK, width), bf16),
            pltpu.VMEM((n_harm, half, modes), f32),
            dma((3,)),
            dma((LAYERS - 1, per_shard)), dma((LAYERS - 1, per_shard)),
            dma((LAYERS - 1, per_shard)), dma((LAYERS - 1, per_shard)),
            dma((LAYERS, per_shard)), dma((LAYERS, per_shard)),
            dma((LAYERS * PAIR, per_shard)), dma((LAYERS * PAIR, per_shard)),
            dma((PASSES, per_chip)), dma((PASSES, per_chip)),
            dma((PASSES, per_chip)), dma((PASSES, per_chip)),
            dma((4, n_chunks)), dma((4, n_chunks)),
            dma((n_chunks,)), dma((n_chunks,)),
            dma((per_pass,)),
        ],
        compiler_params=pltpu.CompilerParams(
            collective_id=0, has_side_effects=True, vmem_limit_bytes=VMEM_BYTES
        ),
    )(
        panel.reshape(per_shard, bs, modes),
        stiffness,
        block_rows,
        block_cols,
        jnp.asarray(wmid),
        jnp.asarray(wend),
    )
    return result.reshape(2, per_chip, half, modes)


def body(panel, stiffness, block_rows, block_cols):
    block_size = stiffness.shape[-1]
    modes = panel.shape[-1]
    whole = lax.all_gather(panel, ("blade", "dof"), axis=0, tiled=True)
    blocks = whole.reshape(-1, block_size, modes)

    def one_blade(items):
        mats, rows, cols = items
        chosen = jnp.take(blocks, cols, axis=0)
        image = jnp.einsum("nij,njm->nim", mats, chosen, preferred_element_type=jnp.float32)
        image = image.astype(jnp.bfloat16)
        left = jnp.take(blocks, rows, axis=0).reshape(-1, modes)
        return lax.dot_general(
            left,
            image.reshape(-1, modes),
            (((0,), (0,)), ((), ())),
            preferred_element_type=jnp.float32,
        )

    partial_proj = lax.map(one_blade, (stiffness, block_rows, block_cols))
    half = lax.psum_scatter(partial_proj, "dof", scatter_dimension=1, tiled=True)
    half = half.astype(jnp.bfloat16)
    blade_count = stiffness.shape[0] * lax.axis_size("blade")
    index = jnp.arange(blade_count, dtype=jnp.int32)
    angle = (index[:, None] * index[None, :] % blade_count).astype(jnp.float32) * (
        2.0 * math.pi / blade_count
    )
    table = jnp.stack([jnp.cos(angle), -jnp.sin(angle)])
    stacked = lax.all_to_all(half, "blade", split_axis=1, concat_axis=0, tiled=True)
    joined = jnp.einsum(
        "phb,brc->phrc", table, stacked.astype(jnp.float32), precision=lax.Precision.HIGHEST
    ).astype(jnp.bfloat16)
    full_spec = lax.all_to_all(joined, "blade", split_axis=1, concat_axis=2, tiled=True)
    return full_spec.astype(jnp.float32)


def solution(mesh):
    placed = (
        P(("grp", "blade", "dof"), None),
        P(("grp", "blade"), "dof", None, None),
        P(("grp", "blade"), "dof"),
        P(("grp", "blade"), "dof"),
    )
    chips = mesh.shape["blade"]
    return jax.shard_map(
        line_body if chips == LAYERS * PAIR else body,
        mesh=mesh,
        in_specs=placed,
        out_specs=P(None, ("grp", "blade"), "dof", None),
        check_vma=False,
    )
```

```python
import math

import jax
import jax.numpy as jnp
import numpy as np
from jax import lax
from jax.experimental import pallas as pl
from jax.experimental.pallas import tpu as pltpu
from jax.sharding import PartitionSpec as P

MESH = pl.DeviceIdType.MESH
LAYERS = 4
PAIR = 2
BLOCK_GROUP = 32
CHUNK = 32
AHEAD = 5
EARLY = 3
PASS_AHEAD = 3
SUB = 16
VMEM_BYTES = 60 * 1024 * 1024
PASSES = 2


def dft_tables(per_chip):
    per_layer = PAIR * per_chip
    count = LAYERS * per_layer
    index = np.arange(count)
    angle = (index[:, None] * index[None, :] % count) * (2.0 * math.pi / count)
    full = np.stack([np.cos(angle), -np.sin(angle)])

    def rows_for(layer):
        part = full[:, layer * per_layer : (layer + 1) * per_layer]
        part = part.reshape(2, PAIR, per_chip, count).transpose(1, 0, 2, 3)
        return part.reshape(2 * per_layer, count)

    def split(weights):
        wide = np.kron(weights, np.eye(SUB)).astype(np.float32)
        high = wide.astype(jnp.bfloat16)
        low = (wide - high.astype(np.float32)).astype(jnp.bfloat16)
        return np.stack([high, low])

    middle, ends = [], []
    for layer, near in ((1, 0), (2, 3)):
        partial = rows_for(near).copy()
        partial[:, near * per_layer : (near + 1) * per_layer] = 0.0
        middle.append(split(np.concatenate([rows_for(layer), partial])))
        own = rows_for(near)[:, near * per_layer : (near + 1) * per_layer]
        ends.append(split(own))
    return np.stack(middle), np.stack(ends)


def kernel(
    panel_ref, stiff_hbm, rows_ref, cols_ref, wmid_hbm, wend_hbm, out_hbm,
    pan, pan_t, stiff, acc, core_in, raw, y_out, wmid, wend,
    comb_out, comb_in, harm_out, harm_in, out_v,
    load_sem, up_send, up_recv, dn_send, dn_recv, ys_send, ys_recv, co_send, co_recv,
    sum_send, sum_recv, sw_send, sw_recv, z_send, z_recv, h_send, h_recv, out_sem,
):
    blade = lax.axis_index("blade")
    d = lax.axis_index("dof")
    z = blade // PAIR
    y = blade % PAIR
    other_y = z * PAIR + (1 - y)
    per_chip, n_blocks = stiff.shape[0], stiff.shape[1]
    per_layer = per_chip * PAIR
    rows_half = core_in.shape[2]
    n_chunks = raw.shape[0]
    per_pass = n_chunks // PASSES
    width = raw.shape[3]
    half_cols = width * PASSES
    per_shard = panel_ref.shape[0]

    def to(src, dst, send, recv, **device):
        return pltpu.make_async_remote_copy(
            src_ref=src, dst_ref=dst, send_sem=send, recv_sem=recv,
            device_id=device, device_id_type=MESH,
        )

    core = dict(dof=1 - d)
    across = dict(blade=other_y)
    up = dict(blade=jnp.minimum(blade + PAIR, LAYERS * PAIR - 1))
    down = dict(blade=jnp.maximum(blade - PAIR, 0))
    has_up = z < LAYERS - 1
    has_dn = z > 0
    is_mid = jnp.logical_and(has_up, has_dn)
    is_end = jnp.logical_not(is_mid)
    which = z // 2

    load = pltpu.make_async_copy(stiff_hbm, stiff, load_sem.at[0])
    load.start()
    load_mid = pltpu.make_async_copy(wmid_hbm.at[which], wmid, load_sem.at[1])
    load_mid.start()
    load_end = pltpu.make_async_copy(wend_hbm.at[which], wend, load_sem.at[2])
    load_end.start()

    barrier = pltpu.get_barrier_semaphore()
    pl.semaphore_signal(barrier, inc=1, device_id=core, device_id_type=MESH)
    pl.semaphore_signal(barrier, inc=1, device_id=across, device_id_type=MESH)

    @pl.when(has_up)
    def _():
        pl.semaphore_signal(barrier, inc=1, device_id=up, device_id_type=MESH)

    @pl.when(has_dn)
    def _():
        pl.semaphore_signal(barrier, inc=1, device_id=down, device_id_type=MESH)

    pl.semaphore_wait(barrier, 2 + has_up.astype(jnp.int32) + has_dn.astype(jnp.int32))

    def place(zz, yy, dd, k):
        return ((zz * PAIR + yy) * 2 + dd) * per_shard + k

    def shard(zz, yy, dd, k):
        return pan.at[pl.ds(place(zz, yy, dd, k), 1)]

    def flip(zz, yy, dd, k):
        n = place(zz, yy, dd, k)
        pan_t[n] = pan[n].T

    def up_copy(step, k):
        s = shard(jnp.maximum(z - step, 0), y, d, k)
        return to(s, s, up_send.at[step, k], up_recv.at[step, k], **up)

    def dn_copy(step, k):
        s = shard(jnp.minimum(z + step, LAYERS - 1), y, d, k)
        return to(s, s, dn_send.at[step, k], dn_recv.at[step, k], **down)

    def up_arrival(step, k):
        s = shard(jnp.maximum(z - step, 0), y, d, k)
        return to(s, s, up_send.at[step - 1, k], up_recv.at[step - 1, k], **up)

    def dn_arrival(step, k):
        s = shard(jnp.minimum(z + step, LAYERS - 1), y, d, k)
        return to(s, s, dn_send.at[step - 1, k], dn_recv.at[step - 1, k], **down)

    def y_copy(zz, k):
        s = shard(zz, y, d, k)
        return to(s, s, ys_send.at[zz, k], ys_recv.at[zz, k], **across)

    def y_arrival(zz, k):
        s = shard(zz, 1 - y, d, k)
        return to(s, s, ys_send.at[zz, k], ys_recv.at[zz, k], **across)

    def core_copy(zz, yy, k):
        s = shard(zz, yy, d, k)
        i = zz * PAIR + yy
        return to(s, s, co_send.at[i, k], co_recv.at[i, k], **core)

    def core_arrival(zz, yy, k):
        s = shard(zz, yy, 1 - d, k)
        i = zz * PAIR + yy
        return to(s, s, co_send.at[i, k], co_recv.at[i, k], **core)

    for k in range(per_shard):
        pan[place(z, y, d, k)] = panel_ref[k]

        @pl.when(has_up)
        def _(k=k):
            up_copy(0, k).start()

        @pl.when(has_dn)
        def _(k=k):
            dn_copy(0, k).start()

        y_copy(z, k).start()
        core_copy(z, y, k).start()

    for k in range(per_shard):
        flip(z, y, d, k)

    def take_y(zz, k):
        y_arrival(zz, k).wait_recv()
        core_copy(zz, 1 - y, k).start()
        flip(zz, 1 - y, d, k)

    def take_core(zz, yy, k):
        core_arrival(zz, yy, k).wait_recv()
        flip(zz, yy, 1 - d, k)

    def at_distance(step, do):
        if step == 0:
            do(z)
            return

        @pl.when(z >= step)
        def _():
            do(z - step)

        @pl.when(z + step < LAYERS)
        def _():
            do(z + step)

    for step in range(1, LAYERS):
        for k in range(per_shard):

            @pl.when(z >= step)
            def _(step=step, k=k):
                up_arrival(step, k).wait_recv()
                if step < LAYERS - 1:

                    @pl.when(has_up)
                    def _():
                        up_copy(step, k).start()

                y_copy(z - step, k).start()
                core_copy(z - step, y, k).start()

            @pl.when(z + step < LAYERS)
            def _(step=step, k=k):
                dn_arrival(step, k).wait_recv()
                if step < LAYERS - 1:

                    @pl.when(has_dn)
                    def _():
                        dn_copy(step, k).start()

                y_copy(z + step, k).start()
                core_copy(z + step, y, k).start()

            at_distance(step, lambda zz: flip(zz, y, d, k))
            at_distance(step - 1, lambda zz: take_y(zz, k))
            at_distance(step - 1, lambda zz: take_core(zz, y, k))
            if step > 1:
                at_distance(step - 2, lambda zz: take_core(zz, 1 - y, k))

    for k in range(per_shard):
        at_distance(LAYERS - 2, lambda zz: take_core(zz, 1 - y, k))
        at_distance(LAYERS - 1, lambda zz: take_core(zz, y, k))
        at_distance(LAYERS - 1, lambda zz: take_y(zz, k))
    for k in range(per_shard):
        at_distance(LAYERS - 1, lambda zz: take_core(zz, 1 - y, k))
    load.wait()

    def sum_copy(h, b):
        src = acc.at[h, b, pl.ds(pl.multiple_of((1 - d) * rows_half, rows_half), rows_half)]
        return to(src, core_in.at[h, b], sum_send.at[h, b], sum_recv.at[h, b], **core)

    def slot(yy, b):
        return z * per_layer + yy * per_chip + b

    def swap_copy(h, b):
        dst = raw.at[pl.ds(h * per_pass, per_pass), slot(y, b)]
        return to(y_out.at[h, b], dst, sw_send.at[h, b], sw_recv.at[h, b], **across)

    def swap_arrival(h, b):
        dst = raw.at[pl.ds(h * per_pass, per_pass), slot(1 - y, b)]
        return to(y_out.at[h, b], dst, sw_send.at[h, b], sw_recv.at[h, b], **across)

    own_rows = pl.ds(pl.multiple_of(d * rows_half, rows_half), rows_half)

    def summed(h, b, yy):
        cols = pl.ds(pl.multiple_of(yy * width, width), width)
        total = acc[h, b, own_rows, cols] + core_in[h, b, :, cols]
        return total.astype(jnp.bfloat16).reshape(per_pass, CHUNK, width)

    def finish(h, b):
        sum_copy(h, b).wait_recv()
        y_out[h, b] = summed(h, b, 1 - y)
        swap_copy(h, b).start()
        raw[pl.ds(h * per_pass, per_pass), slot(y, b)] = summed(h, b, y)

    def one_blade(h, b):
        def group(q):
            left, image = [], []
            for i in range(BLOCK_GROUP):
                n = q * BLOCK_GROUP + i
                c = cols_ref[b, n]
                if PASSES == 1:
                    right = pan[c]
                else:
                    right = jnp.concatenate(
                        [pan[c, :, pl.ds(yy * half_cols + h * width, width)] for yy in range(PAIR)],
                        axis=1,
                    )
                product = jnp.dot(stiff[b, n], right, preferred_element_type=jnp.float32)
                image.append(product.astype(jnp.bfloat16))
                left.append(pan_t[rows_ref[b, n]])
            return jnp.dot(
                jnp.concatenate(left, axis=1),
                jnp.concatenate(image, axis=0),
                preferred_element_type=jnp.float32,
            )

        acc[h, b] = group(0)
        if n_blocks > BLOCK_GROUP:

            def more(q, carry):
                acc[h, b] += group(q)
                return carry

            lax.fori_loop(1, n_blocks // BLOCK_GROUP, more, 0)

        sum_copy(h, b).start()

        @pl.when(b > 0)
        def _():
            finish(h, b - 1)

    def end_pass(h):
        finish(h, per_chip - 1)

        def take_swap(b, carry):
            swap_arrival(h, b).wait_recv()
            return carry

        lax.fori_loop(0, per_chip, take_swap, 0)

    def first_pass(b, carry):
        one_blade(0, b)
        return carry

    lax.fori_loop(0, per_chip, first_pass, 0)
    end_pass(0)

    n_harm = 2 * per_chip
    near = jnp.where(z < 2, 0, LAYERS - 1)
    far = LAYERS - 1 - z
    near_dev = dict(blade=near * PAIR + y)
    far_dev = dict(blade=far * PAIR + y)
    mid_dev = dict(blade=jnp.where(z < 2, 1, LAYERS - 2) * PAIR + y)

    def planes(p, zz):
        return raw.at[p, pl.ds(zz * per_layer, per_layer)]

    def end_copy(p):
        s = planes(p, near)
        return to(s, s, z_send.at[0, p], z_recv.at[0, p], **mid_dev)

    def own_copy(p):
        s = planes(p, z)
        return to(s, s, z_send.at[1, p], z_recv.at[1, p], **far_dev)

    def own_arrival(p):
        s = planes(p, far)
        return to(s, s, z_send.at[1, p], z_recv.at[1, p], **far_dev)

    def pass_copy(p):
        s = planes(p, near)
        return to(s, s, z_send.at[2, p], z_recv.at[2, p], **far_dev)

    def pass_arrival(p):
        s = planes(p, LAYERS - 1 - near)
        return to(s, s, z_send.at[2, p], z_recv.at[2, p], **far_dev)

    def comb_copy(p):
        return to(comb_out.at[p], comb_in.at[p], z_send.at[3, p], z_recv.at[3, p], **near_dev)

    def harm_copy(p):
        return to(harm_out.at[p], harm_in.at[p], h_send.at[p], h_recv.at[p], **across)

    def transform(weights, x):
        x = jnp.concatenate(
            [x[:, i : i + SUB].reshape(-1, width) for i in range(0, CHUNK, SUB)], axis=1
        )
        got = jnp.dot(weights[0], x, preferred_element_type=jnp.float32)
        got = got + jnp.dot(weights[1], x, preferred_element_type=jnp.float32)
        return [
            got[:, i * width : (i + 1) * width].reshape(-1, SUB, width)
            for i in range(CHUNK // SUB)
        ]

    def columns(p, yy):
        return pl.ds(pl.multiple_of(yy * half_cols + p // per_pass * width, width), width)

    def out_copy(r):
        rows = pl.ds(pl.multiple_of(r * CHUNK, CHUNK), CHUNK)
        return pltpu.make_async_copy(out_v.at[:, rows], out_hbm.at[:, rows], out_sem.at[r])

    def store_final(p, sub, final):
        row = lax.rem(p, per_pass) * CHUNK + sub * SUB
        first, second = final[:n_harm], final[n_harm:]
        out_v[:, pl.ds(pl.multiple_of(row, SUB), SUB), columns(p, y)] = jnp.where(
            y == 0, first, second
        )
        theirs = jnp.where(y == 0, second, first)
        harm_out[p, :, pl.ds(sub * SUB, SUB)] = theirs.astype(jnp.bfloat16)

    def take_harm(p):
        harm_copy(p).wait_recv()
        row = lax.rem(p, per_pass) * CHUNK
        out_v[:, pl.ds(pl.multiple_of(row, CHUNK), CHUNK), columns(p, 1 - y)] = harm_in[
            p
        ].astype(jnp.float32)

        @pl.when(p >= n_chunks - per_pass)
        def _():
            out_copy(p - (n_chunks - per_pass)).start()

    @pl.when(is_mid)
    def _():
        own_copy(0).start()
        for p in range(1, AHEAD):
            own_copy(p).start()
            if p <= PASS_AHEAD:
                end_copy(p - 1).wait_recv()
                pass_copy(p - 1).start()

    @pl.when(is_end)
    def _():
        for p in range(AHEAD):
            end_copy(p).start()

    if PASSES > 1:

        def second_pass(b, carry):
            one_blade(1, b)
            return carry

        lax.fori_loop(0, EARLY, second_pass, 0)

    load_mid.wait()
    load_end.wait()

    def step(p, carry):
        if PASSES > 1:

            @pl.when(p < per_chip - EARLY)
            def _():
                one_blade(1, p + EARLY)

            @pl.when(p == per_chip - EARLY)
            def _():
                end_pass(1)

        @pl.when(is_mid)
        def _():
            @pl.when(p + AHEAD < n_chunks)
            def _():
                own_copy(p + AHEAD).start()

            @pl.when(p + PASS_AHEAD < n_chunks)
            def _():
                end_copy(p + PASS_AHEAD).wait_recv()
                pass_copy(p + PASS_AHEAD).start()

            own_arrival(p).wait_recv()
            pass_arrival(p).wait_recv()
            for sub, got in enumerate(transform(wmid, raw[p])):
                comb_out[p, :, pl.ds(sub * SUB, SUB)] = got[2 * n_harm :].astype(jnp.bfloat16)
                store_final(p, sub, got[: 2 * n_harm])
            comb_copy(p).start()

        @pl.when(is_end)
        def _():
            @pl.when(p + AHEAD < n_chunks)
            def _():
                end_copy(p + AHEAD).start()

            comb_copy(p).wait_recv()
            own = raw[p, pl.ds(z * per_layer, per_layer)]
            for sub, got in enumerate(transform(wend, own)):
                rows = pl.ds(sub * SUB, SUB)
                store_final(p, sub, got + comb_in[p, :, rows].astype(jnp.float32))

        harm_copy(p).start()

        @pl.when(p > 0)
        def _():
            take_harm(p - 1)

        return carry

    lax.fori_loop(0, n_chunks, step, 0)
    take_harm(n_chunks - 1)

    for k in range(per_shard):
        for step in range(LAYERS - 1):

            @pl.when(jnp.logical_and(has_up, z >= step))
            def _(step=step, k=k):
                up_copy(step, k).wait_send()

            @pl.when(jnp.logical_and(has_dn, z + step < LAYERS))
            def _(step=step, k=k):
                dn_copy(step, k).wait_send()

        for zz in range(LAYERS):
            y_copy(zz, k).wait_send()
            for yy in range(PAIR):
                core_copy(zz, yy, k).wait_send()

    def drain_blade(b, carry):
        for h in range(PASSES):
            sum_copy(h, b).wait_send()
            swap_copy(h, b).wait_send()
        return carry

    lax.fori_loop(0, per_chip, drain_blade, 0)

    def drain_chunk(p, carry):
        @pl.when(is_mid)
        def _():
            own_copy(p).wait_send()
            pass_copy(p).wait_send()
            comb_copy(p).wait_send()

        @pl.when(is_end)
        def _():
            end_copy(p).wait_send()

        harm_copy(p).wait_send()
        return carry

    lax.fori_loop(0, n_chunks, drain_chunk, 0)

    def drain_out(r, carry):
        out_copy(r).wait()
        return carry

    lax.fori_loop(0, per_pass, drain_out, 0)


def line_body(panel, stiffness, block_rows, block_cols):
    per_chip, n_blocks, bs, _ = stiffness.shape
    modes = panel.shape[-1]
    shards = LAYERS * PAIR * 2
    per_shard = panel.shape[0] // bs
    n_all = shards * per_shard
    half = modes // 2
    width = half // PASSES
    per_pass = half // CHUNK
    n_chunks = per_pass * PASSES
    count = LAYERS * PAIR * per_chip
    n_harm = 2 * per_chip
    wmid, wend = dft_tables(per_chip)
    bf16, f32 = jnp.bfloat16, jnp.float32
    dma = pltpu.SemaphoreType.DMA
    vmem = pl.BlockSpec(memory_space=pltpu.VMEM)
    smem = pl.BlockSpec(memory_space=pltpu.SMEM)
    hbm = pl.BlockSpec(memory_space=pl.ANY)
    result = pl.pallas_call(
        kernel,
        out_shape=jax.ShapeDtypeStruct((n_harm, half, modes), f32),
        in_specs=[vmem, hbm, smem, smem, hbm, hbm],
        out_specs=hbm,
        scratch_shapes=[
            pltpu.VMEM((n_all, bs, modes), bf16),
            pltpu.VMEM((n_all, modes, bs), bf16),
            pltpu.VMEM(stiffness.shape, bf16),
            pltpu.VMEM((PASSES, per_chip, modes, PAIR * width), f32),
            pltpu.VMEM((PASSES, per_chip, half, PAIR * width), f32),
            pltpu.VMEM((n_chunks, count, CHUNK, width), bf16),
            pltpu.VMEM((PASSES, per_chip, per_pass, CHUNK, width), bf16),
            pltpu.VMEM(wmid.shape[1:], bf16),
            pltpu.VMEM(wend.shape[1:], bf16),
            pltpu.VMEM((n_chunks, 2 * n_harm, CHUNK, width), bf16),
            pltpu.VMEM((n_chunks, 2 * n_harm, CHUNK, width), bf16),
            pltpu.VMEM((n_chunks, n_harm, CHUNK, width), bf16),
            pltpu.VMEM((n_chunks, n_harm, CHUNK, width), bf16),
            pltpu.VMEM((n_harm, half, modes), f32),
            dma((3,)),
            dma((LAYERS - 1, per_shard)), dma((LAYERS - 1, per_shard)),
            dma((LAYERS - 1, per_shard)), dma((LAYERS - 1, per_shard)),
            dma((LAYERS, per_shard)), dma((LAYERS, per_shard)),
            dma((LAYERS * PAIR, per_shard)), dma((LAYERS * PAIR, per_shard)),
            dma((PASSES, per_chip)), dma((PASSES, per_chip)),
            dma((PASSES, per_chip)), dma((PASSES, per_chip)),
            dma((4, n_chunks)), dma((4, n_chunks)),
            dma((n_chunks,)), dma((n_chunks,)),
            dma((per_pass,)),
        ],
        compiler_params=pltpu.CompilerParams(
            collective_id=0, has_side_effects=True, vmem_limit_bytes=VMEM_BYTES
        ),
    )(
        panel.reshape(per_shard, bs, modes),
        stiffness,
        block_rows,
        block_cols,
        jnp.asarray(wmid),
        jnp.asarray(wend),
    )
    return result.reshape(2, per_chip, half, modes)


def body(panel, stiffness, block_rows, block_cols):
    block_size = stiffness.shape[-1]
    modes = panel.shape[-1]
    whole = lax.all_gather(panel, ("blade", "dof"), axis=0, tiled=True)
    blocks = whole.reshape(-1, block_size, modes)

    def one_blade(items):
        mats, rows, cols = items
        chosen = jnp.take(blocks, cols, axis=0)
        image = jnp.einsum("nij,njm->nim", mats, chosen, preferred_element_type=jnp.float32)
        image = image.astype(jnp.bfloat16)
        left = jnp.take(blocks, rows, axis=0).reshape(-1, modes)
        return lax.dot_general(
            left,
            image.reshape(-1, modes),
            (((0,), (0,)), ((), ())),
            preferred_element_type=jnp.float32,
        )

    partial_proj = lax.map(one_blade, (stiffness, block_rows, block_cols))
    half = lax.psum_scatter(partial_proj, "dof", scatter_dimension=1, tiled=True)
    half = half.astype(jnp.bfloat16)
    blade_count = stiffness.shape[0] * lax.axis_size("blade")
    index = jnp.arange(blade_count, dtype=jnp.int32)
    angle = (index[:, None] * index[None, :] % blade_count).astype(jnp.float32) * (
        2.0 * math.pi / blade_count
    )
    table = jnp.stack([jnp.cos(angle), -jnp.sin(angle)])
    stacked = lax.all_to_all(half, "blade", split_axis=1, concat_axis=0, tiled=True)
    joined = jnp.einsum(
        "phb,brc->phrc", table, stacked.astype(jnp.float32), precision=lax.Precision.HIGHEST
    ).astype(jnp.bfloat16)
    full_spec = lax.all_to_all(joined, "blade", split_axis=1, concat_axis=2, tiled=True)
    return full_spec.astype(jnp.float32)


def solution(mesh):
    placed = (
        P(("grp", "blade", "dof"), None),
        P(("grp", "blade"), "dof", None, None),
        P(("grp", "blade"), "dof"),
        P(("grp", "blade"), "dof"),
    )
    chips = mesh.shape["blade"]
    return jax.shard_map(
        line_body if chips == LAYERS * PAIR else body,
        mesh=mesh,
        in_specs=placed,
        out_specs=P(None, ("grp", "blade"), "dof", None),
        check_vma=False,
    )
```

```python
import math

import jax
import jax.numpy as jnp
import numpy as np
from jax import lax
from jax.experimental import pallas as pl
from jax.experimental.pallas import tpu as pltpu
from jax.sharding import PartitionSpec as P

MESH = pl.DeviceIdType.MESH
LAYERS = 4
PAIR = 2
BLOCK_GROUP = 32
CHUNK = 32
AHEAD = 5
PASS_AHEAD = 3
SUB = 16
VMEM_BYTES = 60 * 1024 * 1024
PASSES = 2


def dft_tables(per_chip):
    per_layer = PAIR * per_chip
    count = LAYERS * per_layer
    index = np.arange(count)
    angle = (index[:, None] * index[None, :] % count) * (2.0 * math.pi / count)
    full = np.stack([np.cos(angle), -np.sin(angle)])

    def rows_for(layer):
        part = full[:, layer * per_layer : (layer + 1) * per_layer]
        part = part.reshape(2, PAIR, per_chip, count).transpose(1, 0, 2, 3)
        return part.reshape(2 * per_layer, count)

    def split(weights):
        wide = np.kron(weights, np.eye(SUB)).astype(np.float32)
        high = wide.astype(jnp.bfloat16)
        low = (wide - high.astype(np.float32)).astype(jnp.bfloat16)
        return np.stack([high, low])

    middle, ends = [], []
    for layer, near in ((1, 0), (2, 3)):
        partial = rows_for(near).copy()
        partial[:, near * per_layer : (near + 1) * per_layer] = 0.0
        middle.append(split(np.concatenate([rows_for(layer), partial])))
        own = rows_for(near)[:, near * per_layer : (near + 1) * per_layer]
        ends.append(split(own))
    return np.stack(middle), np.stack(ends)


def kernel(
    panel_ref, stiff_hbm, rows_ref, cols_ref, wmid_hbm, wend_hbm, out_hbm,
    pan, pan_t, stiff, acc, core_in, raw, y_out, wmid, wend,
    comb_out, comb_in, harm_out, harm_in, out_v,
    load_sem, up_send, up_recv, dn_send, dn_recv, ys_send, ys_recv, co_send, co_recv,
    sum_send, sum_recv, sw_send, sw_recv, z_send, z_recv, h_send, h_recv, out_sem,
):
    blade = lax.axis_index("blade")
    d = lax.axis_index("dof")
    z = blade // PAIR
    y = blade % PAIR
    other_y = z * PAIR + (1 - y)
    per_chip, n_blocks = stiff.shape[0], stiff.shape[1]
    per_layer = per_chip * PAIR
    rows_half = core_in.shape[2]
    n_chunks = raw.shape[0]
    per_pass = n_chunks // PASSES
    width = raw.shape[3]
    half_cols = width * PASSES
    per_shard = panel_ref.shape[0]

    def to(src, dst, send, recv, **device):
        return pltpu.make_async_remote_copy(
            src_ref=src, dst_ref=dst, send_sem=send, recv_sem=recv,
            device_id=device, device_id_type=MESH,
        )

    core = dict(dof=1 - d)
    across = dict(blade=other_y)
    up = dict(blade=jnp.minimum(blade + PAIR, LAYERS * PAIR - 1))
    down = dict(blade=jnp.maximum(blade - PAIR, 0))
    has_up = z < LAYERS - 1
    has_dn = z > 0
    is_mid = jnp.logical_and(has_up, has_dn)
    is_end = jnp.logical_not(is_mid)
    which = z // 2

    load = pltpu.make_async_copy(stiff_hbm, stiff, load_sem.at[0])
    load.start()
    load_mid = pltpu.make_async_copy(wmid_hbm.at[which], wmid, load_sem.at[1])
    load_mid.start()
    load_end = pltpu.make_async_copy(wend_hbm.at[which], wend, load_sem.at[2])
    load_end.start()

    barrier = pltpu.get_barrier_semaphore()
    pl.semaphore_signal(barrier, inc=1, device_id=core, device_id_type=MESH)
    pl.semaphore_signal(barrier, inc=1, device_id=across, device_id_type=MESH)

    @pl.when(has_up)
    def _():
        pl.semaphore_signal(barrier, inc=1, device_id=up, device_id_type=MESH)

    @pl.when(has_dn)
    def _():
        pl.semaphore_signal(barrier, inc=1, device_id=down, device_id_type=MESH)

    pl.semaphore_wait(barrier, 2 + has_up.astype(jnp.int32) + has_dn.astype(jnp.int32))

    def place(zz, yy, dd, k):
        return ((zz * PAIR + yy) * 2 + dd) * per_shard + k

    def shard(zz, yy, dd, k):
        return pan.at[pl.ds(place(zz, yy, dd, k), 1)]

    def flip(zz, yy, dd, k):
        n = place(zz, yy, dd, k)
        pan_t[n] = pan[n].T

    def up_copy(step, k):
        s = shard(jnp.maximum(z - step, 0), y, d, k)
        return to(s, s, up_send.at[step, k], up_recv.at[step, k], **up)

    def dn_copy(step, k):
        s = shard(jnp.minimum(z + step, LAYERS - 1), y, d, k)
        return to(s, s, dn_send.at[step, k], dn_recv.at[step, k], **down)

    def up_arrival(step, k):
        s = shard(jnp.maximum(z - step, 0), y, d, k)
        return to(s, s, up_send.at[step - 1, k], up_recv.at[step - 1, k], **up)

    def dn_arrival(step, k):
        s = shard(jnp.minimum(z + step, LAYERS - 1), y, d, k)
        return to(s, s, dn_send.at[step - 1, k], dn_recv.at[step - 1, k], **down)

    def y_copy(zz, k):
        s = shard(zz, y, d, k)
        return to(s, s, ys_send.at[zz, k], ys_recv.at[zz, k], **across)

    def y_arrival(zz, k):
        s = shard(zz, 1 - y, d, k)
        return to(s, s, ys_send.at[zz, k], ys_recv.at[zz, k], **across)

    def core_copy(zz, yy, k):
        s = shard(zz, yy, d, k)
        i = zz * PAIR + yy
        return to(s, s, co_send.at[i, k], co_recv.at[i, k], **core)

    def core_arrival(zz, yy, k):
        s = shard(zz, yy, 1 - d, k)
        i = zz * PAIR + yy
        return to(s, s, co_send.at[i, k], co_recv.at[i, k], **core)

    for k in range(per_shard):
        pan[place(z, y, d, k)] = panel_ref[k]

        @pl.when(has_up)
        def _(k=k):
            up_copy(0, k).start()

        @pl.when(has_dn)
        def _(k=k):
            dn_copy(0, k).start()

        y_copy(z, k).start()
        core_copy(z, y, k).start()

    for k in range(per_shard):
        flip(z, y, d, k)

    def take_y(zz, k):
        y_arrival(zz, k).wait_recv()
        core_copy(zz, 1 - y, k).start()
        flip(zz, 1 - y, d, k)

    def take_core(zz, yy, k):
        core_arrival(zz, yy, k).wait_recv()
        flip(zz, yy, 1 - d, k)

    def at_distance(step, do):
        if step == 0:
            do(z)
            return

        @pl.when(z >= step)
        def _():
            do(z - step)

        @pl.when(z + step < LAYERS)
        def _():
            do(z + step)

    for step in range(1, LAYERS):
        for k in range(per_shard):

            @pl.when(z >= step)
            def _(step=step, k=k):
                up_arrival(step, k).wait_recv()
                if step < LAYERS - 1:

                    @pl.when(has_up)
                    def _():
                        up_copy(step, k).start()

                y_copy(z - step, k).start()
                core_copy(z - step, y, k).start()

            @pl.when(z + step < LAYERS)
            def _(step=step, k=k):
                dn_arrival(step, k).wait_recv()
                if step < LAYERS - 1:

                    @pl.when(has_dn)
                    def _():
                        dn_copy(step, k).start()

                y_copy(z + step, k).start()
                core_copy(z + step, y, k).start()

            at_distance(step, lambda zz: flip(zz, y, d, k))
            at_distance(step - 1, lambda zz: take_y(zz, k))
            at_distance(step - 1, lambda zz: take_core(zz, y, k))
            if step > 1:
                at_distance(step - 2, lambda zz: take_core(zz, 1 - y, k))

    for k in range(per_shard):
        at_distance(LAYERS - 2, lambda zz: take_core(zz, 1 - y, k))
        at_distance(LAYERS - 1, lambda zz: take_core(zz, y, k))
        at_distance(LAYERS - 1, lambda zz: take_y(zz, k))
    for k in range(per_shard):
        at_distance(LAYERS - 1, lambda zz: take_core(zz, 1 - y, k))
    load.wait()

    def sum_copy(h, b):
        src = acc.at[h, b, pl.ds(pl.multiple_of((1 - d) * rows_half, rows_half), rows_half)]
        return to(src, core_in.at[h, b], sum_send.at[h, b], sum_recv.at[h, b], **core)

    def slot(yy, b):
        return z * per_layer + yy * per_chip + b

    def swap_copy(h, b):
        dst = raw.at[pl.ds(h * per_pass, per_pass), slot(y, b)]
        return to(y_out.at[h, b], dst, sw_send.at[h, b], sw_recv.at[h, b], **across)

    def swap_arrival(h, b):
        dst = raw.at[pl.ds(h * per_pass, per_pass), slot(1 - y, b)]
        return to(y_out.at[h, b], dst, sw_send.at[h, b], sw_recv.at[h, b], **across)

    own_rows = pl.ds(pl.multiple_of(d * rows_half, rows_half), rows_half)

    def summed(h, b, yy):
        cols = pl.ds(pl.multiple_of(yy * width, width), width)
        total = acc[h, b, own_rows, cols] + core_in[h, b, :, cols]
        return total.astype(jnp.bfloat16).reshape(per_pass, CHUNK, width)

    def finish(h, b):
        sum_copy(h, b).wait_recv()
        y_out[h, b] = summed(h, b, 1 - y)
        swap_copy(h, b).start()
        raw[pl.ds(h * per_pass, per_pass), slot(y, b)] = summed(h, b, y)

    def one_blade(h, b):
        def group(q):
            left, image = [], []
            for i in range(BLOCK_GROUP):
                n = q * BLOCK_GROUP + i
                c = cols_ref[b, n]
                if PASSES == 1:
                    right = pan[c]
                else:
                    right = jnp.concatenate(
                        [pan[c, :, pl.ds(yy * half_cols + h * width, width)] for yy in range(PAIR)],
                        axis=1,
                    )
                product = jnp.dot(stiff[b, n], right, preferred_element_type=jnp.float32)
                image.append(product.astype(jnp.bfloat16))
                left.append(pan_t[rows_ref[b, n]])
            return jnp.dot(
                jnp.concatenate(left, axis=1),
                jnp.concatenate(image, axis=0),
                preferred_element_type=jnp.float32,
            )

        acc[h, b] = group(0)
        if n_blocks > BLOCK_GROUP:

            def more(q, carry):
                acc[h, b] += group(q)
                return carry

            lax.fori_loop(1, n_blocks // BLOCK_GROUP, more, 0)

        sum_copy(h, b).start()

        @pl.when(b > 0)
        def _():
            finish(h, b - 1)

    def end_pass(h):
        finish(h, per_chip - 1)

        def take_swap(b, carry):
            swap_arrival(h, b).wait_recv()
            return carry

        lax.fori_loop(0, per_chip, take_swap, 0)

    def first_pass(b, carry):
        one_blade(0, b)
        return carry

    lax.fori_loop(0, per_chip, first_pass, 0)
    end_pass(0)

    n_harm = 2 * per_chip
    near = jnp.where(z < 2, 0, LAYERS - 1)
    far = LAYERS - 1 - z
    near_dev = dict(blade=near * PAIR + y)
    far_dev = dict(blade=far * PAIR + y)
    mid_dev = dict(blade=jnp.where(z < 2, 1, LAYERS - 2) * PAIR + y)

    def planes(p, zz):
        return raw.at[p, pl.ds(zz * per_layer, per_layer)]

    def end_copy(p):
        s = planes(p, near)
        return to(s, s, z_send.at[0, p], z_recv.at[0, p], **mid_dev)

    def own_copy(p):
        s = planes(p, z)
        return to(s, s, z_send.at[1, p], z_recv.at[1, p], **far_dev)

    def own_arrival(p):
        s = planes(p, far)
        return to(s, s, z_send.at[1, p], z_recv.at[1, p], **far_dev)

    def pass_copy(p):
        s = planes(p, near)
        return to(s, s, z_send.at[2, p], z_recv.at[2, p], **far_dev)

    def pass_arrival(p):
        s = planes(p, LAYERS - 1 - near)
        return to(s, s, z_send.at[2, p], z_recv.at[2, p], **far_dev)

    def comb_copy(p):
        return to(comb_out.at[p], comb_in.at[p], z_send.at[3, p], z_recv.at[3, p], **near_dev)

    def harm_copy(p):
        return to(harm_out.at[p], harm_in.at[p], h_send.at[p], h_recv.at[p], **across)

    def transform(weights, x):
        x = jnp.concatenate(
            [x[:, i : i + SUB].reshape(-1, width) for i in range(0, CHUNK, SUB)], axis=1
        )
        got = jnp.dot(weights[0], x, preferred_element_type=jnp.float32)
        got = got + jnp.dot(weights[1], x, preferred_element_type=jnp.float32)
        return [
            got[:, i * width : (i + 1) * width].reshape(-1, SUB, width)
            for i in range(CHUNK // SUB)
        ]

    def columns(p, yy):
        return pl.ds(pl.multiple_of(yy * half_cols + p // per_pass * width, width), width)

    def out_copy(r):
        rows = pl.ds(pl.multiple_of(r * CHUNK, CHUNK), CHUNK)
        return pltpu.make_async_copy(out_v.at[:, rows], out_hbm.at[:, rows], out_sem.at[r])

    def store_final(p, sub, final):
        row = lax.rem(p, per_pass) * CHUNK + sub * SUB
        first, second = final[:n_harm], final[n_harm:]
        out_v[:, pl.ds(pl.multiple_of(row, SUB), SUB), columns(p, y)] = jnp.where(
            y == 0, first, second
        )
        theirs = jnp.where(y == 0, second, first)
        harm_out[p, :, pl.ds(sub * SUB, SUB)] = theirs.astype(jnp.bfloat16)

    def take_harm(p):
        harm_copy(p).wait_recv()
        row = lax.rem(p, per_pass) * CHUNK
        out_v[:, pl.ds(pl.multiple_of(row, CHUNK), CHUNK), columns(p, 1 - y)] = harm_in[
            p
        ].astype(jnp.float32)

        @pl.when(p >= n_chunks - per_pass)
        def _():
            out_copy(p - (n_chunks - per_pass)).start()

    @pl.when(is_mid)
    def _():
        own_copy(0).start()
        for p in range(1, AHEAD):
            own_copy(p).start()
            if p <= PASS_AHEAD:
                end_copy(p - 1).wait_recv()
                pass_copy(p - 1).start()

    @pl.when(is_end)
    def _():
        for p in range(AHEAD):
            end_copy(p).start()

    load_mid.wait()
    load_end.wait()

    def step(p, carry):
        if PASSES > 1:

            @pl.when(p == per_chip // 2)
            def _():
                end_pass(1)

        @pl.when(is_mid)
        def _():
            @pl.when(p + AHEAD < n_chunks)
            def _():
                own_copy(p + AHEAD).start()

            @pl.when(p + PASS_AHEAD < n_chunks)
            def _():
                end_copy(p + PASS_AHEAD).wait_recv()
                pass_copy(p + PASS_AHEAD).start()

        @pl.when(is_end)
        def _():
            @pl.when(p + AHEAD < n_chunks)
            def _():
                end_copy(p + AHEAD).start()

        if PASSES > 1:

            @pl.when(p < per_chip // 2)
            def _():
                def second_pass(b, carry):
                    one_blade(1, 2 * p + b)
                    return carry

                lax.fori_loop(0, 2, second_pass, 0)

        @pl.when(is_mid)
        def _():
            own_arrival(p).wait_recv()
            pass_arrival(p).wait_recv()
            for sub, got in enumerate(transform(wmid, raw[p])):
                comb_out[p, :, pl.ds(sub * SUB, SUB)] = got[2 * n_harm :].astype(jnp.bfloat16)
                store_final(p, sub, got[: 2 * n_harm])
            comb_copy(p).start()

        @pl.when(is_end)
        def _():
            comb_copy(p).wait_recv()
            own = raw[p, pl.ds(z * per_layer, per_layer)]
            for sub, got in enumerate(transform(wend, own)):
                rows = pl.ds(sub * SUB, SUB)
                store_final(p, sub, got + comb_in[p, :, rows].astype(jnp.float32))

        harm_copy(p).start()

        @pl.when(p > 0)
        def _():
            take_harm(p - 1)

        return carry

    lax.fori_loop(0, n_chunks, step, 0)
    take_harm(n_chunks - 1)

    for k in range(per_shard):
        for step in range(LAYERS - 1):

            @pl.when(jnp.logical_and(has_up, z >= step))
            def _(step=step, k=k):
                up_copy(step, k).wait_send()

            @pl.when(jnp.logical_and(has_dn, z + step < LAYERS))
            def _(step=step, k=k):
                dn_copy(step, k).wait_send()

        for zz in range(LAYERS):
            y_copy(zz, k).wait_send()
            for yy in range(PAIR):
                core_copy(zz, yy, k).wait_send()

    def drain_blade(b, carry):
        for h in range(PASSES):
            sum_copy(h, b).wait_send()
            swap_copy(h, b).wait_send()
        return carry

    lax.fori_loop(0, per_chip, drain_blade, 0)

    def drain_chunk(p, carry):
        @pl.when(is_mid)
        def _():
            own_copy(p).wait_send()
            pass_copy(p).wait_send()
            comb_copy(p).wait_send()

        @pl.when(is_end)
        def _():
            end_copy(p).wait_send()

        harm_copy(p).wait_send()
        return carry

    lax.fori_loop(0, n_chunks, drain_chunk, 0)

    def drain_out(r, carry):
        out_copy(r).wait()
        return carry

    lax.fori_loop(0, per_pass, drain_out, 0)


def line_body(panel, stiffness, block_rows, block_cols):
    per_chip, n_blocks, bs, _ = stiffness.shape
    modes = panel.shape[-1]
    shards = LAYERS * PAIR * 2
    per_shard = panel.shape[0] // bs
    n_all = shards * per_shard
    half = modes // 2
    width = half // PASSES
    per_pass = half // CHUNK
    n_chunks = per_pass * PASSES
    count = LAYERS * PAIR * per_chip
    n_harm = 2 * per_chip
    wmid, wend = dft_tables(per_chip)
    bf16, f32 = jnp.bfloat16, jnp.float32
    dma = pltpu.SemaphoreType.DMA
    vmem = pl.BlockSpec(memory_space=pltpu.VMEM)
    smem = pl.BlockSpec(memory_space=pltpu.SMEM)
    hbm = pl.BlockSpec(memory_space=pl.ANY)
    result = pl.pallas_call(
        kernel,
        out_shape=jax.ShapeDtypeStruct((n_harm, half, modes), f32),
        in_specs=[vmem, hbm, smem, smem, hbm, hbm],
        out_specs=hbm,
        scratch_shapes=[
            pltpu.VMEM((n_all, bs, modes), bf16),
            pltpu.VMEM((n_all, modes, bs), bf16),
            pltpu.VMEM(stiffness.shape, bf16),
            pltpu.VMEM((PASSES, per_chip, modes, PAIR * width), f32),
            pltpu.VMEM((PASSES, per_chip, half, PAIR * width), f32),
            pltpu.VMEM((n_chunks, count, CHUNK, width), bf16),
            pltpu.VMEM((PASSES, per_chip, per_pass, CHUNK, width), bf16),
            pltpu.VMEM(wmid.shape[1:], bf16),
            pltpu.VMEM(wend.shape[1:], bf16),
            pltpu.VMEM((n_chunks, 2 * n_harm, CHUNK, width), bf16),
            pltpu.VMEM((n_chunks, 2 * n_harm, CHUNK, width), bf16),
            pltpu.VMEM((n_chunks, n_harm, CHUNK, width), bf16),
            pltpu.VMEM((n_chunks, n_harm, CHUNK, width), bf16),
            pltpu.VMEM((n_harm, half, modes), f32),
            dma((3,)),
            dma((LAYERS - 1, per_shard)), dma((LAYERS - 1, per_shard)),
            dma((LAYERS - 1, per_shard)), dma((LAYERS - 1, per_shard)),
            dma((LAYERS, per_shard)), dma((LAYERS, per_shard)),
            dma((LAYERS * PAIR, per_shard)), dma((LAYERS * PAIR, per_shard)),
            dma((PASSES, per_chip)), dma((PASSES, per_chip)),
            dma((PASSES, per_chip)), dma((PASSES, per_chip)),
            dma((4, n_chunks)), dma((4, n_chunks)),
            dma((n_chunks,)), dma((n_chunks,)),
            dma((per_pass,)),
        ],
        compiler_params=pltpu.CompilerParams(
            collective_id=0, has_side_effects=True, vmem_limit_bytes=VMEM_BYTES
        ),
    )(
        panel.reshape(per_shard, bs, modes),
        stiffness,
        block_rows,
        block_cols,
        jnp.asarray(wmid),
        jnp.asarray(wend),
    )
    return result.reshape(2, per_chip, half, modes)


def body(panel, stiffness, block_rows, block_cols):
    block_size = stiffness.shape[-1]
    modes = panel.shape[-1]
    whole = lax.all_gather(panel, ("blade", "dof"), axis=0, tiled=True)
    blocks = whole.reshape(-1, block_size, modes)

    def one_blade(items):
        mats, rows, cols = items
        chosen = jnp.take(blocks, cols, axis=0)
        image = jnp.einsum("nij,njm->nim", mats, chosen, preferred_element_type=jnp.float32)
        image = image.astype(jnp.bfloat16)
        left = jnp.take(blocks, rows, axis=0).reshape(-1, modes)
        return lax.dot_general(
            left,
            image.reshape(-1, modes),
            (((0,), (0,)), ((), ())),
            preferred_element_type=jnp.float32,
        )

    partial_proj = lax.map(one_blade, (stiffness, block_rows, block_cols))
    half = lax.psum_scatter(partial_proj, "dof", scatter_dimension=1, tiled=True)
    half = half.astype(jnp.bfloat16)
    blade_count = stiffness.shape[0] * lax.axis_size("blade")
    index = jnp.arange(blade_count, dtype=jnp.int32)
    angle = (index[:, None] * index[None, :] % blade_count).astype(jnp.float32) * (
        2.0 * math.pi / blade_count
    )
    table = jnp.stack([jnp.cos(angle), -jnp.sin(angle)])
    stacked = lax.all_to_all(half, "blade", split_axis=1, concat_axis=0, tiled=True)
    joined = jnp.einsum(
        "phb,brc->phrc", table, stacked.astype(jnp.float32), precision=lax.Precision.HIGHEST
    ).astype(jnp.bfloat16)
    full_spec = lax.all_to_all(joined, "blade", split_axis=1, concat_axis=2, tiled=True)
    return full_spec.astype(jnp.float32)


def solution(mesh):
    placed = (
        P(("grp", "blade", "dof"), None),
        P(("grp", "blade"), "dof", None, None),
        P(("grp", "blade"), "dof"),
        P(("grp", "blade"), "dof"),
    )
    chips = mesh.shape["blade"]
    return jax.shard_map(
        line_body if chips == LAYERS * PAIR else body,
        mesh=mesh,
        in_specs=placed,
        out_specs=P(None, ("grp", "blade"), "dof", None),
        check_vma=False,
    )
```
